32 devices in a mesh: section: 2 (over y), expert: 4 (over z), dp: 4 (over x, core).
Axes of the slice: x: 2, y: 2, z: 4, core: 2. Of those that a mesh axis runs over, the one named last changes fastest.
Arguments:
- inputs: bfloat16 [2, 128, 3072], P(None, ('expert', 'dp')), may hold values from -6 to 6
- cotangent: bfloat16 [2, 128, 3072], P(None, ('expert', 'dp')), may hold values from -6 to 6
- norm_gain: bfloat16 [2, 3072], P('section'), may hold values from 0.5 to 1.5
- router: bfloat16 [2, 3072, 4], P('section'), may hold values from -0.109375 to 0.109375
- w_gate: bfloat16 [2, 4, 3072, 8192], P('section', 'expert', None, 'dp'), may hold values from -0.109375 to 0.109375
- w_up: bfloat16 [2, 4, 3072, 8192], P('section', 'expert', None, 'dp'), may hold values from -0.109375 to 0.109375
- w_down: bfloat16 [2, 4, 8192, 3072], P('section', 'expert', 'dp'), may hold values from -0.0625 to 0.0625
- routes: int32 [2, 2, 128, 2], P('section', None, ('expert', 'dp')), may hold values from 0 to 3, as said below
Outputs:
- acts: bfloat16 [2, 2, 128, 3072], P('section', None, ('expert', 'dp'))
- grads: bfloat16 [2, 2, 128, 3072], P('section', None, ('expert', 'dp'))
- router_grad: float32 [2, 3072, 4], P('section')
The draws below stay inside these ranges and needn't reach their ends.
Inputs may be any that keep to these rules, and one draw needn't show every extreme that they name: `routes`: the two experts of a token differ. For each layer and micro-batch, the 8 tokens of one device name no expert more than 6 times, and one expert, the same on all devices for that layer and micro-batch, exactly 6 times.
All inputs are finite; a program needn't handle non-finite values.
Results may differ from the reference program's by a relative error of at most 0.017.
Values may be sent and summed in bfloat16 or wider, within the bound.
No kernel may reach another device: no remote copies, remote signals or barrier semaphores. Data moves between devices by JAX's collectives and lax.ppermute only.
A program may use at most 128 MiB of HBM per device.

```python
import jax
import jax.numpy as jnp
from jax import lax

D = 3072
FF = 8192
TOP = 2
MICRO = 2
TOK_DEV = 8
E = 4
LAYERS = 2
CAP = 6
TOKENS = 128
N_DP = 4


def routes_block(block_key, hot_expert):
    key_order, key_flip, key_shuffle = jax.random.split(block_key, 3)
    others = jnp.arange((E - 1) * CAP, dtype=jnp.int32) // CAP
    others = others + (others >= hot_expert).astype(jnp.int32)
    ordering = jax.random.permutation(key_order, (E - 1) * CAP)
    chosen_rest = others[ordering[:TOP * TOK_DEV - CAP]]
    merged = jnp.sort(jnp.concatenate([jnp.full((CAP,), hot_expert, jnp.int32), chosen_rest]))
    pair_table = jnp.stack([merged[:TOK_DEV], merged[TOK_DEV:]], axis=1)
    flipped = jax.random.randint(key_flip, (TOK_DEV,), 0, 2)
    pair_table = jnp.where(flipped[:, None] == 1, pair_table[:, ::-1], pair_table)
    shuffle = jax.random.permutation(key_shuffle, TOK_DEV)
    return pair_table[shuffle]


def draw_routes(key, part):
    slices = LAYERS * MICRO
    blocks = TOKENS // TOK_DEV
    hot_expert = jax.random.randint(jax.random.fold_in(key, 7), (slices,), 0, E)
    block_keys = jax.random.split(jax.random.fold_in(key, 11), slices * blocks)
    hot_each = jnp.repeat(hot_expert, blocks)
    result = jax.vmap(routes_block)(block_keys, hot_each)
    return result.reshape(LAYERS, MICRO, TOKENS, TOP).astype(jnp.int32)


def shard_levels(stream_key, dims, cuts, smallest, top_value):
    loudness, own = 1.0, jax.random.fold_in(stream_key, 6)
    for position, parts in cuts:
        draws = jnp.exp(jax.random.uniform(jax.random.fold_in(own, position), (parts,), jnp.float32, smallest / len(cuts), top_value / len(cuts)))
        loudness = loudness * jnp.repeat(draws, dims[position] // parts).reshape([-1 if axis == position else 1 for axis in range(len(dims))])
    return loudness


def gaussian(key, extent, width, most, pieces=(), kind=jnp.bfloat16):
    values = jax.random.normal(key, extent, jnp.float32) * width
    if len(pieces) > 0:
        values = shard_levels(key, extent, pieces, -0.22, 0.18) * values
    return jnp.clip(values, min=-most, max=most).astype(kind)


def setup_inputs(seed: int = 0) -> dict:
    key_of = jax.random.split(jax.random.key(seed), 9)
    inputs = gaussian(key_of[0], (MICRO, TOKENS, D), 1.0, 6.0, ((1, 16),))
    cotangent = gaussian(key_of[1], (MICRO, TOKENS, D), 1.0, 6.0, ((1, 16),))
    norm_gain = jnp.clip(1.0 + 0.1 * jax.random.normal(key_of[2], (LAYERS, D), jnp.float32), 0.5, 1.5).astype(jnp.bfloat16)
    router = gaussian(key_of[3], (LAYERS, D, E), D ** -0.5, 0.109375, ((0, 2),))
    w_gate = gaussian(key_of[4], (LAYERS, E, D, FF), D ** -0.5, 0.109375, ((0, 2), (1, 4), (3, 4)))
    w_up = gaussian(key_of[5], (LAYERS, E, D, FF), D ** -0.5, 0.109375, ((0, 2), (1, 4), (3, 4)))
    w_down = gaussian(key_of[6], (LAYERS, E, FF, D), FF ** -0.5, 0.0625, ((0, 2), (1, 4), (2, 4)))
    routes = draw_routes(jax.random.fold_in(key_of[8], 71), 0)
    return dict(inputs=inputs, cotangent=cotangent, norm_gain=norm_gain, router=router, w_gate=w_gate, w_up=w_up, w_down=w_down, routes=routes)


EPSILON = 1e-05

def norm_rows(layer_in, gain_row):
    values = layer_in.astype(jnp.float32)
    inv_rms = lax.rsqrt(lax.optimization_barrier(jnp.mean(values * values, axis=-1, keepdims=True)) + EPSILON)
    return (values, inv_rms, (values * inv_rms * gain_row).astype(jnp.bfloat16))

def gate_probs(hidden, router_w, picks):
    logits = jnp.dot(hidden, router_w, preferred_element_type=jnp.float32)
    chosen = jnp.take_along_axis(logits, picks, axis=1)
    logit_gap = chosen[:, 0] - chosen[:, 1]
    return jnp.stack([jax.nn.sigmoid(logit_gap), jax.nn.sigmoid(-logit_gap)], axis=1)

def slot_table(picks, experts, capacity):
    flat_pick = picks.reshape(-1).astype(jnp.int32)
    onehot = (flat_pick[:, None] == jnp.arange(experts, dtype=jnp.int32)[None, :]).astype(jnp.int32)
    earlier = jnp.cumsum(onehot, axis=0) - onehot
    slot_pos = lax.optimization_barrier(jnp.sum(earlier * onehot, axis=1))
    target = flat_pick * capacity + slot_pos
    return target[:, None] == jnp.arange(experts * capacity, dtype=jnp.int32)[None, :]

def route_tables(picks):
    blocks = picks.reshape(-1, TOK_DEV, TOP)
    return jax.vmap(lambda block_picks: slot_table(block_picks, E, CAP))(blocks)

def dispatch_rows(placing, row_values):
    grouped = jnp.einsum('bsr,bsd->brd', placing.astype(jnp.float32), row_values.astype(jnp.float32), precision=lax.Precision.HIGHEST)
    grouped = grouped.astype(jnp.bfloat16).reshape(-1, E, CAP, D)
    return grouped.transpose(1, 0, 2, 3).reshape(E, -1, D)

def return_rows(placing, per_expert):
    returned = per_expert.reshape(E, -1, CAP, D).transpose(1, 0, 2, 3).reshape(-1, E * CAP, D)
    picked = jnp.einsum('bsr,brd->bsd', placing.astype(jnp.float32), returned, precision=lax.Precision.HIGHEST)
    return picked.reshape(TOKENS, TOP, D)

def expert_out(operands):
    row_block, gate_w, up_w, down_w = operands
    shard_width = gate_w.shape[1] // N_DP
    summed = jnp.zeros((row_block.shape[0], down_w.shape[1]), jnp.float32)
    for shard_no in range(N_DP):
        offset = shard_no * shard_width
        gate_pre = jnp.dot(row_block, gate_w[:, offset:offset + shard_width], preferred_element_type=jnp.float32)
        up_pre = jnp.dot(row_block, up_w[:, offset:offset + shard_width], preferred_element_type=jnp.float32)
        active = (gate_pre * jax.nn.sigmoid(gate_pre) * up_pre).astype(jnp.bfloat16)
        partial_out = jnp.dot(active, down_w[offset:offset + shard_width], preferred_element_type=jnp.float32)
        partial_out = partial_out.astype(jnp.bfloat16)
        summed = summed + lax.optimization_barrier(partial_out).astype(jnp.float32)
    return summed

def expert_grad(operands):
    row_block, grad_block, gate_w, up_w, down_w = operands
    shard_width = gate_w.shape[1] // N_DP
    summed = jnp.zeros((row_block.shape[0], gate_w.shape[0]), jnp.float32)
    for shard_no in range(N_DP):
        offset = shard_no * shard_width
        gate_slab = gate_w[:, offset:offset + shard_width]
        up_slab = up_w[:, offset:offset + shard_width]
        gate_pre = jnp.dot(row_block, gate_slab, preferred_element_type=jnp.float32)
        up_pre = jnp.dot(row_block, up_slab, preferred_element_type=jnp.float32)
        d_active = jnp.dot(grad_block, down_w[offset:offset + shard_width].T, preferred_element_type=jnp.float32)
        gate_sig = jax.nn.sigmoid(gate_pre)
        d_gate = (d_active * up_pre * gate_sig * (1.0 + gate_pre * (1.0 - gate_sig))).astype(jnp.bfloat16)
        d_up = (d_active * gate_pre * gate_sig).astype(jnp.bfloat16)
        d_rows = jnp.dot(d_gate, gate_slab.T, preferred_element_type=jnp.float32)
        d_rows = d_rows + jnp.dot(d_up, up_slab.T, preferred_element_type=jnp.float32)
        summed = summed + lax.optimization_barrier(d_rows.astype(jnp.bfloat16)).astype(jnp.float32)
    return summed

def layer_forward(layer_in, picks, gain_row, router_w, gate_w, up_w, down_w):
    values, inv_rms, hidden = norm_rows(layer_in, gain_row)
    gate_prob = gate_probs(hidden, router_w, picks)
    placing = route_tables(picks)
    repeated = jnp.repeat(hidden, TOP, axis=0).reshape(-1, TOK_DEV * TOP, D)
    per_expert = lax.map(expert_out, (dispatch_rows(placing, repeated), gate_w, up_w, down_w))
    picked = return_rows(placing, per_expert)
    layer_out = (values + lax.optimization_barrier(jnp.sum(gate_prob[:, :, None] * picked, axis=1))).astype(jnp.bfloat16)
    return (layer_out, picked)

def layer_backward(layer_in, upstream, picks, gain_row, router_w, gate_w, up_w, down_w, picked):
    values, inv_rms, hidden = norm_rows(layer_in, gain_row)
    gate_prob = gate_probs(hidden, router_w, picks)
    placing = route_tables(picks)
    grad_out = upstream.astype(jnp.float32)
    d_prob = lax.optimization_barrier(jnp.sum(grad_out[:, None, :] * picked, axis=2))
    d_gap = gate_prob[:, 0] * gate_prob[:, 1] * (d_prob[:, 0] - d_prob[:, 1])
    d_chosen = jnp.stack([d_gap, -d_gap], axis=1)
    expert_hot = (picks[:, :, None] == jnp.arange(E, dtype=jnp.int32)[None, None, :]).astype(jnp.float32)
    d_logits = lax.optimization_barrier(jnp.sum(d_chosen[:, :, None] * expert_hot, axis=1))
    scaled = (gate_prob[:, :, None] * grad_out[:, None, :]).astype(jnp.bfloat16).reshape(-1, TOK_DEV * TOP, D)
    repeated = jnp.repeat(hidden, TOP, axis=0).reshape(-1, TOK_DEV * TOP, D)
    grads_expert = lax.map(expert_grad, (dispatch_rows(placing, repeated), dispatch_rows(placing, scaled), gate_w, up_w, down_w))
    returned = return_rows(placing, grads_expert)
    d_hidden = lax.optimization_barrier(jnp.sum(returned, axis=1)) + jnp.dot(d_logits, router_w.astype(jnp.float32).T, precision=lax.Precision.HIGHEST)
    router_term = jnp.dot(hidden.astype(jnp.float32).T, d_logits, precision=lax.Precision.HIGHEST)
    weighted = gain_row * d_hidden
    cubed = inv_rms * inv_rms * inv_rms
    d_in = grad_out + inv_rms * weighted - values * cubed * lax.optimization_barrier(jnp.mean(values * weighted, axis=-1, keepdims=True))
    return (d_in.astype(jnp.bfloat16), router_term)

def reference(inputs, cotangent, norm_gain, router, w_gate, w_up, w_down, routes):
    layer_inputs = [[None] * MICRO for _ in range(LAYERS)]
    layer_outputs = [[None] * MICRO for _ in range(LAYERS)]
    stashed = [[None] * MICRO for _ in range(LAYERS)]
    for micro_no in range(MICRO):
        current = inputs[micro_no]
        for layer_no in range(LAYERS):
            layer_inputs[layer_no][micro_no] = current
            current, picked = layer_forward(current, routes[layer_no, micro_no], norm_gain[layer_no].astype(jnp.float32), router[layer_no], w_gate[layer_no], w_up[layer_no], w_down[layer_no])
            layer_outputs[layer_no][micro_no] = current
            stashed[layer_no][micro_no] = picked
    layer_grads = [[None] * MICRO for _ in range(LAYERS)]
    router_sums = [jnp.zeros((D, E), jnp.float32) for _ in range(LAYERS)]
    for micro_no in range(MICRO):
        upstream = cotangent[micro_no]
        for layer_no in reversed(range(LAYERS)):
            upstream, router_term = layer_backward(layer_inputs[layer_no][micro_no], upstream, routes[layer_no, micro_no], norm_gain[layer_no].astype(jnp.float32), router[layer_no], w_gate[layer_no], w_up[layer_no], w_down[layer_no], stashed[layer_no][micro_no])
            layer_grads[layer_no][micro_no] = upstream
            router_sums[layer_no] = router_sums[layer_no] + router_term
    acts = jnp.stack([jnp.stack(per_layer) for per_layer in layer_outputs])
    grads = jnp.stack([jnp.stack(per_layer) for per_layer in layer_grads])
    router_grad = jnp.stack(router_sums)
    return (acts, grads, router_grad)
```

```python
import functools

import jax
import jax.numpy as jnp
from jax import lax
from jax.experimental import pallas as pl
from jax.experimental.pallas import tpu as pltpu
from jax.sharding import PartitionSpec as P

EPSILON = 1e-05
LANES = 128
GROUP = ("expert", "dp")
F32 = jnp.float32
BF16 = jnp.bfloat16


def dot_nn(a, b):
    return jnp.dot(a, b, preferred_element_type=F32)


def dot_nt(a, b):
    return lax.dot_general(a, b, (((1,), (1,)), ((), ())), preferred_element_type=F32)


def chunks(total):
    step = next(c for c in (512, 384, 256, 128) if total % c == 0)
    return [pl.ds(start, step) for start in range(0, total, step)]


def lanes_like(rows):
    return lax.broadcasted_iota(jnp.int32, (rows, LANES), 1)


def pick_lane(block, lane):
    return jnp.sum(jnp.where(lanes_like(block.shape[0]) == lane, block, 0.0), axis=1, keepdims=True)


def hi_lo(block):
    high = block.astype(BF16)
    return high, (block - high.astype(F32)).astype(BF16)


def place_rows(tail, me, place_ref, pick_ref):
    tokens, rows = place_ref.shape
    wide = -(-rows // LANES) * LANES
    first, second = pick_lane(tail, 0), pick_lane(tail, 1)
    mine = jnp.broadcast_to(((first == me) | (second == me)).astype(F32), (tokens, wide))
    row = lax.broadcasted_iota(jnp.int32, (tokens, tokens), 0)
    col = lax.broadcasted_iota(jnp.int32, (tokens, tokens), 1)
    earlier = dot_nn((col < row).astype(F32).astype(BF16), mine.astype(BF16))
    slot = lax.broadcasted_iota(jnp.int32, (tokens, wide), 1).astype(F32)
    place = jnp.where((earlier == slot) & (mine > 0.5), 1.0, 0.0)
    place_ref[...] = place[:, :rows].astype(BF16)
    pick_ref[...] = jnp.transpose(place)[:rows].astype(BF16)


def signs_of(tail, me):
    first, second = pick_lane(tail, 0), pick_lane(tail, 1)
    other = first + second - me
    lane = lanes_like(tail.shape[0]).astype(F32)
    both = (lane == me).astype(F32) - (lane == other).astype(F32)
    return jnp.where(first != second, both, 0.0)


def norm_and_gap(rows_ref, gain, router, signs, hidden_ref):
    values = rows_ref[...].astype(F32)
    inv_rms = lax.rsqrt(jnp.mean(values * values, axis=1, keepdims=True) + EPSILON)
    hidden = (values * inv_rms * gain).astype(BF16)
    hidden_ref[...] = hidden
    return jnp.sum(dot_nn(hidden, router) * signs, axis=1, keepdims=True)


def add_down(acc_ref, active, down_ref, first):
    for part in chunks(acc_ref.shape[1]):
        term = dot_nn(active, down_ref[:, part])
        acc_ref[:, part] = jnp.where(first, term, acc_ref[:, part] + term)


def add_back(acc_ref, d_gate, d_up, gate_ref, up_ref, first):
    for part in chunks(acc_ref.shape[1]):
        term = dot_nt(d_gate, gate_ref[part, :]) + dot_nt(d_up, up_ref[part, :])
        acc_ref[:, part] = jnp.where(first, term, acc_ref[:, part] + term)


def spread(place_ref, rows_ref, out_ref):
    for part in chunks(out_ref.shape[1]):
        out_ref[:, part] = dot_nn(place_ref[...], rows_ref[:, part]).astype(BF16)


def grads_of(gate_pre, up_pre, d_raw, prob, first, dprob_ref):
    gate_sig = jax.nn.sigmoid(gate_pre)
    act = gate_pre * gate_sig
    active = (act * up_pre).astype(BF16)
    gain = jnp.sum(active.astype(F32) * d_raw, axis=1, keepdims=True)
    gain = jnp.broadcast_to(gain, dprob_ref.shape)
    dprob_ref[...] = jnp.where(first, gain, dprob_ref[...] + gain)
    d_active = d_raw * prob
    d_gate = (d_active * up_pre * gate_sig * (1.0 + gate_pre * (1.0 - gate_sig))).astype(BF16)
    d_up = (d_active * act).astype(BF16)
    return active, d_gate, d_up


def finish_back(acc_ref, rows_ref, dprob_ref, gap, signs, hidden_ref, router, place_ref, back_ref, rg_ref):
    c = jax.nn.sigmoid(gap) * jax.nn.sigmoid(-gap) * dprob_ref[...] * signs
    c_high, c_low = hi_lo(c)
    for part in chunks(acc_ref.shape[1]):
        extra = dot_nt(c_high, router[part, :]) + dot_nt(c_low, router[part, :])
        rows_ref[:, part] = (acc_ref[:, part] + extra).astype(BF16)
    spread(place_ref, rows_ref, back_ref)
    kept = rg_ref.shape[0]
    t_high, t_low = hi_lo(jnp.transpose(c)[:kept])
    for part in chunks(acc_ref.shape[1]):
        hidden = hidden_ref[:, part]
        rg_ref[:, part] = dot_nn(t_high, hidden) + dot_nn(t_low, hidden)


def first_kernel(steps, x_ref, gain_ref, router_ref, gate_ref, up_ref, down_ref,
                 out_ref, place_ref, pick_ref, hidden_ref, info_ref, a_ref, b_ref,
                 rows_ref, acc_ref):
    step = pl.program_id(0)
    section = lax.axis_index("section")
    width = gain_ref.shape[1]

    @pl.when(step == 0)
    def _():
        me = lax.axis_index("expert").astype(F32)
        place_rows(x_ref[:, width:].astype(F32), me, place_ref, pick_ref)
        for part in chunks(width):
            rows_ref[:, part] = dot_nn(pick_ref[...], x_ref[:, part]).astype(BF16)
        info_ref[0] = signs_of(dot_nn(pick_ref[...], x_ref[:, width:]), me)

    @pl.when((step == 0) & (section == 0))
    def _():
        gap = norm_and_gap(rows_ref, gain_ref[...].astype(F32), router_ref[...], info_ref[0], hidden_ref)
        info_ref[1] = jnp.broadcast_to(gap, info_ref.shape[1:])

    @pl.when(section == 0)
    def _():
        gate_pre = dot_nn(hidden_ref[...], gate_ref[...])
        up_pre = dot_nn(hidden_ref[...], up_ref[...])
        a_ref[...] = gate_pre
        b_ref[...] = up_pre
        active = (gate_pre * jax.nn.sigmoid(gate_pre) * up_pre).astype(BF16)
        add_down(acc_ref, active, down_ref, step == 0)

    @pl.when(section != 0)
    def _():
        a_ref[...] = dot_nt(rows_ref[...], down_ref[...])

    @pl.when((step == steps - 1) & (section == 0))
    def _():
        prob = jax.nn.sigmoid(pick_lane(info_ref[1], 0))
        rows_ref[...] = (acc_ref[...] * prob).astype(BF16)
        spread(place_ref, rows_ref, out_ref)


def middle_kernel(steps, x_ref, gain_ref, router_ref, place_ref, pick_ref, info_ref, raw_ref,
                  gate_ref, up_ref, down_ref,
                  back_ref, prob_ref, rg_ref, active_ref,
                  rows_ref, hidden_ref, acc_ref, dprob_ref, gap_ref):
    step = pl.program_id(0)
    active_section = lax.axis_index("section") == 1

    @pl.when(active_section & (step == 0))
    def _():
        for part in chunks(x_ref.shape[1]):
            rows_ref[:, part] = dot_nn(pick_ref[...], x_ref[:, part]).astype(BF16)
        gap = norm_and_gap(rows_ref, gain_ref[...].astype(F32), router_ref[...], info_ref[0], hidden_ref)
        gap_ref[...] = jnp.broadcast_to(gap, gap_ref.shape)
        prob_ref[...] = jax.nn.sigmoid(gap_ref[...])

    @pl.when(active_section)
    def _():
        gate_pre = dot_nn(hidden_ref[...], gate_ref[...])
        up_pre = dot_nn(hidden_ref[...], up_ref[...])
        prob = pick_lane(prob_ref[...], 0)
        active, d_gate, d_up = grads_of(gate_pre, up_pre, raw_ref[...], prob, step == 0, dprob_ref)
        active_ref[...] = active
        add_back(acc_ref, d_gate, d_up, gate_ref, up_ref, step == 0)

    @pl.when(active_section & (step == steps - 1))
    def _():
        finish_back(acc_ref, rows_ref, dprob_ref, gap_ref[...], info_ref[0], hidden_ref,
                    router_ref[...], place_ref, back_ref, rg_ref)


def last_kernel(steps, u_ref, router_ref, place_ref, pick_ref, info_ref, hidden_ref, prob_ref,
                rg_in_ref, a_ref, b_ref, active_ref, gate_ref, up_ref, down_ref,
                out_ref, rg_ref,
                rows_ref, acc_ref, dprob_ref):
    step = pl.program_id(0)
    section = lax.axis_index("section")

    @pl.when((section == 0) & (step == 0))
    def _():
        for part in chunks(u_ref.shape[1]):
            rows_ref[:, part] = dot_nn(pick_ref[...], u_ref[:, part]).astype(BF16)

    @pl.when(section == 0)
    def _():
        prob = jax.nn.sigmoid(pick_lane(info_ref[1], 0))
        d_raw = dot_nt(rows_ref[...], down_ref[...])
        _, d_gate, d_up = grads_of(a_ref[...], b_ref[...], d_raw, prob, step == 0, dprob_ref)
        add_back(acc_ref, d_gate, d_up, gate_ref, up_ref, step == 0)

    @pl.when(section != 0)
    def _():
        add_down(acc_ref, active_ref[...], down_ref, step == 0)

    @pl.when((section == 0) & (step == steps - 1))
    def _():
        finish_back(acc_ref, rows_ref, dprob_ref, info_ref[1], info_ref[0], hidden_ref,
                    router_ref[...], place_ref, out_ref, rg_ref)

    @pl.when((section != 0) & (step == steps - 1))
    def _():
        rows_ref[...] = (acc_ref[...] * pick_lane(prob_ref[...], 0)).astype(BF16)
        spread(place_ref, rows_ref, out_ref)
        rg_ref[...] = rg_in_ref[...]


def whole(shape):
    return pl.BlockSpec(shape, lambda i: (0,) * len(shape))


def expert_call(body, steps, small, tiled, weights, outs, tiled_outs, scratch, flops):
    gate_w, up_w, down_w = weights
    width, hidden = gate_w.shape
    tile = hidden // steps
    rows = [whole(a.shape) for a in small]
    rows += [pl.BlockSpec((a.shape[0], tile), lambda i: (0, i)) for a in tiled]
    rows += [pl.BlockSpec((width, tile), lambda i: (0, i))] * 2
    rows += [pl.BlockSpec((tile, width), lambda i: (i, 0))]
    out_specs = [whole(o.shape) for o in outs]
    out_specs += [pl.BlockSpec((o.shape[0], tile), lambda i: (0, i)) for o in tiled_outs]
    size = lambda a: a.size * a.dtype.itemsize
    held = sum(2 * size(a) for a in list(small) + list(outs)) + 24 * 2**20
    return pl.pallas_call(
        functools.partial(body, steps),
        grid=(steps,),
        in_specs=rows,
        out_specs=out_specs,
        out_shape=list(outs) + list(tiled_outs),
        scratch_shapes=scratch,
        cost_estimate=pl.CostEstimate(
            flops=flops, bytes_accessed=sum(map(size, weights)), transcendentals=0
        ),
        compiler_params=pltpu.CompilerParams(vmem_limit_bytes=min(held, 60 * 2**20)),
    )(*small, *tiled, *weights)


def sent_on(block, distance):
    count = lax.axis_size("section")
    pairs = [(i, i + distance) for i in range(count) if 0 <= i + distance < count]
    return lax.ppermute(block, "section", pairs)


def gathered(block):
    return lax.all_gather(block, GROUP, axis=0, tiled=True)


def combined(block):
    return lax.psum_scatter(block, GROUP, scatter_dimension=0, tiled=True)


def input_grad(layer_in, upstream, d_hidden, gain_row):
    values = layer_in.astype(F32)
    inv_rms = lax.rsqrt(jnp.mean(values * values, axis=-1, keepdims=True) + EPSILON)
    weighted = gain_row * d_hidden.astype(F32)
    mean = jnp.mean(values * weighted, axis=-1, keepdims=True)
    cubed = inv_rms * inv_rms * inv_rms
    d_in = upstream.astype(F32) + inv_rms * weighted - values * cubed * mean
    return d_in.astype(BF16)


def per_device(inputs, cotangent, norm_gain, router, w_gate, w_up, w_down, routes):
    section = lax.axis_index("section")
    at_start = section == 0
    micro, toks, width = inputs.shape
    experts, top_k = router.shape[2], routes.shape[3]
    capacity = 3 * top_k * toks // (2 * experts)
    peers = lax.axis_size("expert") * lax.axis_size("dp")
    own = micro * toks
    tokens, rows = peers * own, peers * micro * capacity
    weights = (w_gate[0, 0], w_up[0, 0], w_down[0, 0])
    hidden_units = weights[0].shape[1]
    tile = 256 if hidden_units % 256 == 0 else hidden_units
    steps = hidden_units // tile
    gain_row = norm_gain[0].astype(F32)
    router_w = jnp.pad(router[0], ((0, 0), (0, LANES - experts)))
    kept = -(-experts // 8) * 8
    shape = jax.ShapeDtypeStruct
    dot_flops = 2 * rows * width * hidden_units

    mine = jnp.where(at_start, inputs, cotangent).reshape(own, width)
    tail = jnp.pad(routes[0].reshape(own, top_k).astype(BF16), ((0, 0), (0, LANES - top_k)))
    gathered_first = gathered(jnp.concatenate([mine, tail], axis=1))
    out, place, pick, hidden, info, stash_a, stash_b = expert_call(
        first_kernel, steps, [gathered_first, norm_gain, router_w], [], weights,
        [shape((tokens, width), BF16), shape((tokens, rows), BF16), shape((rows, tokens), BF16),
         shape((rows, width), BF16), shape((2, rows, LANES), F32)],
        [shape((rows, hidden_units), F32), shape((rows, hidden_units), F32)],
        [pltpu.VMEM((rows, width), BF16), pltpu.VMEM((rows, width), F32)],
        3 * dot_flops,
    )
    acts_start = (mine.astype(F32) + combined(out).astype(F32)).astype(BF16)

    arrived = sent_on(acts_start, 1)
    back, prob, rg, active = expert_call(
        middle_kernel, steps,
        [gathered(arrived), norm_gain, router_w, place, pick, info], [stash_a], weights,
        [shape((tokens, width), BF16), shape((rows, LANES), F32), shape((kept, width), F32)],
        [shape((rows, hidden_units), BF16)],
        [pltpu.VMEM((rows, width), BF16), pltpu.VMEM((rows, width), BF16),
         pltpu.VMEM((rows, width), F32), pltpu.VMEM((rows, LANES), F32), pltpu.VMEM((rows, LANES), F32)],
        4 * dot_flops,
    )
    grads_end = input_grad(arrived, mine, combined(back), gain_row)

    upstream = sent_on(grads_end, -1)
    out, rg = expert_call(
        last_kernel, steps,
        [gathered(upstream), router_w, place, pick, info, hidden, prob, rg],
        [stash_a, stash_b, active], weights,
        [shape((tokens, width), BF16), shape((kept, width), F32)], [],
        [pltpu.VMEM((rows, width), BF16), pltpu.VMEM((rows, width), F32), pltpu.VMEM((rows, LANES), F32)],
        3 * dot_flops,
    )
    total = combined(out)
    router_total = lax.psum(rg, GROUP)[:experts].T
    grads_start = input_grad(mine, upstream, total, gain_row)
    acts_end = (arrived.astype(F32) + total.astype(F32)).astype(BF16)
    acts = jnp.where(at_start, acts_start, acts_end).reshape(1, micro, toks, width)
    grads = jnp.where(at_start, grads_start, grads_end).reshape(1, micro, toks, width)
    return acts, grads, router_total[None]


def solution(mesh):
    placed = (
        P(None, GROUP, None),
        P(None, GROUP, None),
        P("section", None),
        P("section", None, None),
        P("section", "expert", None, "dp"),
        P("section", "expert", None, "dp"),
        P("section", "expert", "dp", None),
        P("section", None, GROUP, None),
    )
    return jax.shard_map(
        per_device,
        mesh=mesh,
        in_specs=placed,
        out_specs=(
            P("section", None, GROUP, None),
            P("section", None, GROUP, None),
            P("section", None, None),
        ),
        check_vma=False,
    )
```

```python
import functools

import jax
import jax.numpy as jnp
from jax import lax
from jax.experimental import pallas as pl
from jax.experimental.pallas import tpu as pltpu
from jax.sharding import PartitionSpec as P

EPSILON = 1e-05
LANES = 128
GROUP = ("expert", "dp")
F32 = jnp.float32
BF16 = jnp.bfloat16


def dot_nn(a, b):
    return jnp.dot(a, b, preferred_element_type=F32)


def dot_nt(a, b):
    return lax.dot_general(a, b, (((1,), (1,)), ((), ())), preferred_element_type=F32)


def chunks(total):
    step = next(c for c in (512, 384, 256, 128) if total % c == 0)
    return [pl.ds(start, step) for start in range(0, total, step)]


def lanes_like(rows):
    return lax.broadcasted_iota(jnp.int32, (rows, LANES), 1)


def pick_lane(block, lane):
    return jnp.sum(jnp.where(lanes_like(block.shape[0]) == lane, block, 0.0), axis=1, keepdims=True)


def hi_lo(block):
    high = block.astype(BF16)
    return high, (block - high.astype(F32)).astype(BF16)


def place_rows(tail, me, place_ref, pick_ref):
    tokens, rows = place_ref.shape
    wide = -(-rows // LANES) * LANES
    first, second = pick_lane(tail, 0), pick_lane(tail, 1)
    mine = jnp.broadcast_to(((first == me) | (second == me)).astype(F32), (tokens, wide))
    row = lax.broadcasted_iota(jnp.int32, (tokens, tokens), 0)
    col = lax.broadcasted_iota(jnp.int32, (tokens, tokens), 1)
    earlier = dot_nn((col < row).astype(F32).astype(BF16), mine.astype(BF16))
    slot = lax.broadcasted_iota(jnp.int32, (tokens, wide), 1).astype(F32)
    place = jnp.where((earlier == slot) & (mine > 0.5), 1.0, 0.0)
    place_ref[...] = place[:, :rows].astype(BF16)
    pick_ref[...] = jnp.transpose(place)[:rows].astype(BF16)


def signs_of(tail, me):
    first, second = pick_lane(tail, 0), pick_lane(tail, 1)
    other = first + second - me
    lane = lanes_like(tail.shape[0]).astype(F32)
    both = (lane == me).astype(F32) - (lane == other).astype(F32)
    return jnp.where(first != second, both, 0.0)


def norm_and_gap(rows_ref, gain, router, signs, hidden_ref):
    values = rows_ref[...].astype(F32)
    inv_rms = lax.rsqrt(jnp.mean(values * values, axis=1, keepdims=True) + EPSILON)
    hidden = (values * inv_rms * gain).astype(BF16)
    hidden_ref[...] = hidden
    return jnp.sum(dot_nn(hidden, router) * signs, axis=1, keepdims=True)


def add_down(acc_ref, active, down_ref, first):
    for part in chunks(acc_ref.shape[1]):
        term = dot_nn(active, down_ref[:, part])
        acc_ref[:, part] = jnp.where(first, term, acc_ref[:, part] + term)


def add_back(acc_ref, d_gate, d_up, gate_ref, up_ref, first):
    for part in chunks(acc_ref.shape[1]):
        term = dot_nt(d_gate, gate_ref[part, :]) + dot_nt(d_up, up_ref[part, :])
        acc_ref[:, part] = jnp.where(first, term, acc_ref[:, part] + term)


def joined(refs, part):
    return jnp.concatenate([ref[:, part] for ref in refs], axis=0)


def select(pick_ref, x_refs, rows_ref):
    for part in chunks(rows_ref.shape[1]):
        rows_ref[:, part] = dot_nn(pick_ref[...], joined(x_refs, part)).astype(BF16)


def spread(place_ref, rows_ref, out_refs):
    piece = out_refs[0].shape[0]
    for part in chunks(rows_ref.shape[1]):
        block = dot_nn(place_ref[...], rows_ref[:, part]).astype(BF16)
        for i, out_ref in enumerate(out_refs):
            out_ref[:, part] = block[i * piece:(i + 1) * piece]


def grads_of(gate_pre, up_pre, d_raw, prob, first, dprob_ref):
    gate_sig = jax.nn.sigmoid(gate_pre)
    act = gate_pre * gate_sig
    active = (act * up_pre).astype(BF16)
    gain = jnp.sum(active.astype(F32) * d_raw, axis=1, keepdims=True)
    gain = jnp.broadcast_to(gain, dprob_ref.shape)
    dprob_ref[...] = jnp.where(first, gain, dprob_ref[...] + gain)
    d_active = d_raw * prob
    d_gate = (d_active * up_pre * gate_sig * (1.0 + gate_pre * (1.0 - gate_sig))).astype(BF16)
    d_up = (d_active * act).astype(BF16)
    return active, d_gate, d_up


def finish_back(acc_ref, rows_ref, dprob_ref, gap, signs, hidden_ref, router, place_ref, back_refs, rg_ref):
    c = jax.nn.sigmoid(gap) * jax.nn.sigmoid(-gap) * dprob_ref[...] * signs
    c_high, c_low = hi_lo(c)
    for part in chunks(acc_ref.shape[1]):
        extra = dot_nt(c_high, router[part, :]) + dot_nt(c_low, router[part, :])
        rows_ref[:, part] = (acc_ref[:, part] + extra).astype(BF16)
    spread(place_ref, rows_ref, back_refs)
    kept = rg_ref.shape[0]
    t_high, t_low = hi_lo(jnp.transpose(c)[:kept])
    for part in chunks(acc_ref.shape[1]):
        hidden = hidden_ref[:, part]
        rg_ref[:, part] = dot_nn(t_high, hidden) + dot_nn(t_low, hidden)


def first_kernel(steps, x_refs, out_refs, gain_ref, router_ref, gate_ref, up_ref, down_ref,
                 place_ref, pick_ref, hidden_ref, info_ref, a_ref, b_ref,
                 rows_ref, acc_ref):
    step = pl.program_id(0)
    section = lax.axis_index("section")
    width = gain_ref.shape[1]

    @pl.when(step == 0)
    def _():
        me = lax.axis_index("expert").astype(F32)
        tail = joined(x_refs, pl.ds(width, LANES))
        place_rows(tail.astype(F32), me, place_ref, pick_ref)
        select(pick_ref, x_refs, rows_ref)
        info_ref[0] = signs_of(dot_nn(pick_ref[...], tail), me)

    @pl.when((step == 0) & (section == 0))
    def _():
        gap = norm_and_gap(rows_ref, gain_ref[...].astype(F32), router_ref[...], info_ref[0], hidden_ref)
        info_ref[1] = jnp.broadcast_to(gap, info_ref.shape[1:])

    @pl.when(section == 0)
    def _():
        gate_pre = dot_nn(hidden_ref[...], gate_ref[...])
        up_pre = dot_nn(hidden_ref[...], up_ref[...])
        a_ref[...] = gate_pre
        b_ref[...] = up_pre
        active = (gate_pre * jax.nn.sigmoid(gate_pre) * up_pre).astype(BF16)
        add_down(acc_ref, active, down_ref, step == 0)

    @pl.when(section != 0)
    def _():
        a_ref[...] = dot_nt(rows_ref[...], down_ref[...])

    @pl.when((step == steps - 1) & (section == 0))
    def _():
        prob = jax.nn.sigmoid(pick_lane(info_ref[1], 0))
        rows_ref[...] = (acc_ref[...] * prob).astype(BF16)
        spread(place_ref, rows_ref, out_refs)


def middle_kernel(steps, x_refs, back_refs, gain_ref, router_ref, place_ref, pick_ref, info_ref, raw_ref,
                  gate_ref, up_ref, down_ref,
                  prob_ref, rg_ref, active_ref,
                  rows_ref, hidden_ref, acc_ref, dprob_ref, gap_ref):
    step = pl.program_id(0)
    active_section = lax.axis_index("section") == 1

    @pl.when(active_section & (step == 0))
    def _():
        select(pick_ref, x_refs, rows_ref)
        gap = norm_and_gap(rows_ref, gain_ref[...].astype(F32), router_ref[...], info_ref[0], hidden_ref)
        gap_ref[...] = jnp.broadcast_to(gap, gap_ref.shape)
        prob_ref[...] = jax.nn.sigmoid(gap_ref[...])

    @pl.when(active_section)
    def _():
        gate_pre = dot_nn(hidden_ref[...], gate_ref[...])
        up_pre = dot_nn(hidden_ref[...], up_ref[...])
        prob = pick_lane(prob_ref[...], 0)
        active, d_gate, d_up = grads_of(gate_pre, up_pre, raw_ref[...], prob, step == 0, dprob_ref)
        active_ref[...] = active
        add_back(acc_ref, d_gate, d_up, gate_ref, up_ref, step == 0)

    @pl.when(active_section & (step == steps - 1))
    def _():
        finish_back(acc_ref, rows_ref, dprob_ref, gap_ref[...], info_ref[0], hidden_ref,
                    router_ref[...], place_ref, back_refs, rg_ref)


def last_kernel(steps, u_refs, out_refs, router_ref, place_ref, pick_ref, info_ref, hidden_ref, prob_ref,
                rg_in_ref, a_ref, b_ref, active_ref, gate_ref, up_ref, down_ref,
                rg_ref,
                rows_ref, acc_ref, dprob_ref):
    step = pl.program_id(0)
    section = lax.axis_index("section")

    @pl.when((section == 0) & (step == 0))
    def _():
        select(pick_ref, u_refs, rows_ref)

    @pl.when(section == 0)
    def _():
        prob = jax.nn.sigmoid(pick_lane(info_ref[1], 0))
        d_raw = dot_nt(rows_ref[...], down_ref[...])
        _, d_gate, d_up = grads_of(a_ref[...], b_ref[...], d_raw, prob, step == 0, dprob_ref)
        add_back(acc_ref, d_gate, d_up, gate_ref, up_ref, step == 0)

    @pl.when(section != 0)
    def _():
        add_down(acc_ref, active_ref[...], down_ref, step == 0)

    @pl.when((section == 0) & (step == steps - 1))
    def _():
        finish_back(acc_ref, rows_ref, dprob_ref, info_ref[1], info_ref[0], hidden_ref,
                    router_ref[...], place_ref, out_refs, rg_ref)

    @pl.when((section != 0) & (step == steps - 1))
    def _():
        rows_ref[...] = (acc_ref[...] * pick_lane(prob_ref[...], 0)).astype(BF16)
        spread(place_ref, rows_ref, out_refs)
        rg_ref[...] = rg_in_ref[...]


def whole(shape):
    return pl.BlockSpec(shape, lambda i: (0,) * len(shape))


def with_pieces(body, steps, count, inputs, *refs):
    ins, rest = refs[:inputs], refs[inputs:]
    body(steps, ins[:count], rest[:count], *ins[count:], *rest[count:])


def expert_call(body, steps, pieces, small, tiled, weights, outs, tiled_outs, scratch, flops):
    gate_w, up_w, down_w = weights
    width, hidden = gate_w.shape
    tile = hidden // steps
    small = list(pieces) + small
    outs = [jax.ShapeDtypeStruct((p.shape[0], width), BF16) for p in pieces] + outs
    rows = [whole(a.shape) for a in small]
    rows += [pl.BlockSpec((a.shape[0], tile), lambda i: (0, i)) for a in tiled]
    rows += [pl.BlockSpec((width, tile), lambda i: (0, i))] * 2
    rows += [pl.BlockSpec((tile, width), lambda i: (i, 0))]
    out_specs = [whole(o.shape) for o in outs]
    out_specs += [pl.BlockSpec((o.shape[0], tile), lambda i: (0, i)) for o in tiled_outs]
    size = lambda a: a.size * a.dtype.itemsize
    held = sum(2 * size(a) for a in small + outs) + 24 * 2**20
    results = pl.pallas_call(
        functools.partial(with_pieces, body, steps, len(pieces), len(rows)),
        grid=(steps,),
        in_specs=rows,
        out_specs=out_specs,
        out_shape=outs + tiled_outs,
        scratch_shapes=scratch,
        cost_estimate=pl.CostEstimate(
            flops=flops, bytes_accessed=sum(map(size, weights)), transcendentals=0
        ),
        compiler_params=pltpu.CompilerParams(vmem_limit_bytes=min(held, 60 * 2**20)),
    )(*small, *tiled, *weights)
    return results[:len(pieces)], *results[len(pieces):]


def moved(block, axes, target):
    sizes = [lax.axis_size(a) for a in axes]
    spots = [()]
    for n in sizes:
        spots = [spot + (i,) for spot in spots for i in range(n)]
    number = {spot: i for i, spot in enumerate(spots)}
    pairs = [(number[spot], number[target(*spot)]) for spot in spots if target(*spot) in number]
    return lax.ppermute(block, axes, pairs)


def flips():
    bits = lax.axis_size("dp").bit_length() - 1
    return [1 << b for b in reversed(range(bits))]


def flipped(block, bit):
    return moved(block, ("dp",), lambda d: (d ^ bit,))


def gathered(block, distance):
    count = lax.axis_size("expert")
    if distance == 0:
        parts = [block] + [
            moved(block, ("expert",), lambda e, k=k: ((e + k) % count,)) for k in range(1, count)
        ]
    else:
        parts = [
            moved(block, ("section", "expert"), lambda s, e, k=k: (s + distance, (e + k) % count))
            for k in range(count)
        ]
    pieces = [jnp.concatenate(parts, axis=0)]
    for bit in flips():
        pieces = pieces + [flipped(piece, bit) for piece in pieces]
    return pieces


def combined(pieces):
    count = lax.axis_size("expert")
    for bit in reversed(flips()):
        half = len(pieces) // 2
        arrived = [flipped(piece, bit) for piece in pieces[half:]]
        pieces = [
            (kept.astype(F32) + came.astype(F32)).astype(BF16)
            for kept, came in zip(pieces[:half], arrived)
        ]
    own = pieces[0].shape[0] // count
    parts = [pieces[0][k * own:(k + 1) * own] for k in range(count)]
    total = parts[0].astype(F32)
    for k in range(1, count):
        total = total + moved(parts[k], ("expert",), lambda e, k=k: ((e - k) % count,)).astype(F32)
    return total


def summed(block):
    for bit in flips():
        block = block + flipped(block, bit)
    count = lax.axis_size("expert")
    for bit in [1 << b for b in range(count.bit_length() - 1)]:
        block = block + moved(block, ("expert",), lambda e, bit=bit: (e ^ bit,))
    return block


def sent_on(block, distance):
    return moved(block, ("section",), lambda s: (s + distance,))


def input_grad(layer_in, upstream, d_hidden, gain_row):
    values = layer_in.astype(F32)
    inv_rms = lax.rsqrt(jnp.mean(values * values, axis=-1, keepdims=True) + EPSILON)
    weighted = gain_row * d_hidden
    mean = jnp.mean(values * weighted, axis=-1, keepdims=True)
    cubed = inv_rms * inv_rms * inv_rms
    d_in = upstream.astype(F32) + inv_rms * weighted - values * cubed * mean
    return d_in.astype(BF16)


def per_device(inputs, cotangent, norm_gain, router, w_gate, w_up, w_down, routes):
    section = lax.axis_index("section")
    at_start = section == 0
    micro, toks, width = inputs.shape
    experts, top_k = router.shape[2], routes.shape[3]
    capacity = 3 * top_k * toks // (2 * experts)
    peers = lax.axis_size("expert") * lax.axis_size("dp")
    own = micro * toks
    tokens, rows = peers * own, peers * micro * capacity
    weights = (w_gate[0, 0], w_up[0, 0], w_down[0, 0])
    hidden_units = weights[0].shape[1]
    tile = 256 if hidden_units % 256 == 0 else hidden_units
    steps = hidden_units // tile
    gain_row = norm_gain[0].astype(F32)
    router_w = jnp.pad(router[0], ((0, 0), (0, LANES - experts)))
    kept = -(-experts // 8) * 8
    shape = jax.ShapeDtypeStruct
    dot_flops = 2 * rows * width * hidden_units

    mine = jnp.where(at_start, inputs, cotangent).reshape(own, width)
    tail = jnp.pad(routes[0].reshape(own, top_k).astype(BF16), ((0, 0), (0, LANES - top_k)))
    payload = jnp.concatenate([mine, tail], axis=1)
    out, place, pick, hidden, info, stash_a, stash_b = expert_call(
        first_kernel, steps, gathered(payload, 0), [norm_gain, router_w], [], weights,
        [shape((tokens, rows), BF16), shape((rows, tokens), BF16),
         shape((rows, width), BF16), shape((2, rows, LANES), F32)],
        [shape((rows, hidden_units), F32), shape((rows, hidden_units), F32)],
        [pltpu.VMEM((rows, width), BF16), pltpu.VMEM((rows, width), F32)],
        3 * dot_flops,
    )
    acts_start = (mine.astype(F32) + combined(out)).astype(BF16)

    back, prob, rg, active = expert_call(
        middle_kernel, steps, gathered(acts_start, 1),
        [norm_gain, router_w, place, pick, info], [stash_a], weights,
        [shape((rows, LANES), F32), shape((kept, width), F32)],
        [shape((rows, hidden_units), BF16)],
        [pltpu.VMEM((rows, width), BF16), pltpu.VMEM((rows, width), BF16),
         pltpu.VMEM((rows, width), F32), pltpu.VMEM((rows, LANES), F32), pltpu.VMEM((rows, LANES), F32)],
        4 * dot_flops,
    )
    arrived = sent_on(acts_start, 1)
    grads_end = input_grad(arrived, mine, combined(back), gain_row)

    out, rg = expert_call(
        last_kernel, steps, gathered(grads_end, -1),
        [router_w, place, pick, info, hidden, prob, rg],
        [stash_a, stash_b, active], weights,
        [shape((kept, width), F32)], [],
        [pltpu.VMEM((rows, width), BF16), pltpu.VMEM((rows, width), F32), pltpu.VMEM((rows, LANES), F32)],
        3 * dot_flops,
    )
    total = combined(out)
    upstream = sent_on(grads_end, -1)
    router_total = summed(rg)[:experts].T
    grads_start = input_grad(mine, upstream, total, gain_row)
    acts_end = (arrived.astype(F32) + total).astype(BF16)
    acts = jnp.where(at_start, acts_start, acts_end).reshape(1, micro, toks, width)
    grads = jnp.where(at_start, grads_start, grads_end).reshape(1, micro, toks, width)
    return acts, grads, router_total[None]


def solution(mesh):
    placed = (
        P(None, GROUP, None),
        P(None, GROUP, None),
        P("section", None),
        P("section", None, None),
        P("section", "expert", None, "dp"),
        P("section", "expert", None, "dp"),
        P("section", "expert", "dp", None),
        P("section", None, GROUP, None),
    )
    return jax.shard_map(
        per_device,
        mesh=mesh,
        in_specs=placed,
        out_specs=(
            P("section", None, GROUP, None),
            P("section", None, GROUP, None),
            P("section", None, None),
        ),
        check_vma=False,
    )
```

```python
import functools

import jax
import jax.numpy as jnp
from jax import lax
from jax.experimental import pallas as pl
from jax.experimental.pallas import tpu as pltpu
from jax.sharding import PartitionSpec as P

EPSILON = 1e-05
LANES = 128
GROUP = ("expert", "dp")
F32 = jnp.float32
BF16 = jnp.bfloat16


def dot_nn(a, b):
    return jnp.dot(a, b, preferred_element_type=F32)


def dot_nt(a, b):
    return lax.dot_general(a, b, (((1,), (1,)), ((), ())), preferred_element_type=F32)


def chunks(total):
    step = next(c for c in (512, 384, 256, 128) if total % c == 0)
    return [pl.ds(start, step) for start in range(0, total, step)]


def lanes_like(rows):
    return lax.broadcasted_iota(jnp.int32, (rows, LANES), 1)


def pick_lane(block, lane):
    return jnp.sum(jnp.where(lanes_like(block.shape[0]) == lane, block, 0.0), axis=1, keepdims=True)


def hi_lo(block):
    high = block.astype(BF16)
    return high, (block - high.astype(F32)).astype(BF16)


def place_rows(tail, me, place_ref, pick_ref):
    tokens, rows = place_ref.shape
    wide = -(-rows // LANES) * LANES
    first, second = pick_lane(tail, 0), pick_lane(tail, 1)
    mine = jnp.broadcast_to(((first == me) | (second == me)).astype(F32), (tokens, wide))
    row = lax.broadcasted_iota(jnp.int32, (tokens, tokens), 0)
    col = lax.broadcasted_iota(jnp.int32, (tokens, tokens), 1)
    earlier = dot_nn((col < row).astype(F32).astype(BF16), mine.astype(BF16))
    slot = lax.broadcasted_iota(jnp.int32, (tokens, wide), 1).astype(F32)
    place = jnp.where((earlier == slot) & (mine > 0.5), 1.0, 0.0)
    place_ref[...] = place[:, :rows].astype(BF16)
    pick_ref[...] = jnp.transpose(place)[:rows].astype(BF16)


def signs_of(tail, me):
    first, second = pick_lane(tail, 0), pick_lane(tail, 1)
    other = first + second - me
    lane = lanes_like(tail.shape[0]).astype(F32)
    both = (lane == me).astype(F32) - (lane == other).astype(F32)
    return jnp.where(first != second, both, 0.0)


def norm_and_gap(rows_ref, gain, router, signs, hidden_ref):
    values = rows_ref[...].astype(F32)
    inv_rms = lax.rsqrt(jnp.mean(values * values, axis=1, keepdims=True) + EPSILON)
    hidden = (values * inv_rms * gain).astype(BF16)
    hidden_ref[...] = hidden
    return jnp.sum(dot_nn(hidden, router) * signs, axis=1, keepdims=True)


def add_down(acc_ref, active, down_ref, first):
    for part in chunks(acc_ref.shape[1]):
        term = dot_nn(active, down_ref[:, part])
        acc_ref[:, part] = jnp.where(first, term, acc_ref[:, part] + term)


def add_back(acc_ref, d_gate, d_up, gate_ref, up_ref, first):
    for part in chunks(acc_ref.shape[1]):
        term = dot_nt(d_gate, gate_ref[part, :]) + dot_nt(d_up, up_ref[part, :])
        acc_ref[:, part] = jnp.where(first, term, acc_ref[:, part] + term)


def joined(refs, part):
    return jnp.concatenate([ref[:, part] for ref in refs], axis=0)


def select(pick_ref, x_refs, rows_ref):
    for part in chunks(rows_ref.shape[1]):
        rows_ref[:, part] = dot_nn(pick_ref[...], joined(x_refs, part)).astype(BF16)


def spread(place_ref, rows_ref, out_refs):
    piece = out_refs[0].shape[0]
    for part in chunks(rows_ref.shape[1]):
        block = dot_nn(place_ref[...], rows_ref[:, part]).astype(BF16)
        for i, out_ref in enumerate(out_refs):
            out_ref[:, part] = block[i * piece:(i + 1) * piece]


def grads_of(gate_pre, up_pre, d_raw, prob, first, dprob_ref):
    gate_sig = jax.nn.sigmoid(gate_pre)
    act = gate_pre * gate_sig
    active = (act * up_pre).astype(BF16)
    gain = jnp.sum(active.astype(F32) * d_raw, axis=1, keepdims=True)
    gain = jnp.broadcast_to(gain, dprob_ref.shape)
    dprob_ref[...] = jnp.where(first, gain, dprob_ref[...] + gain)
    d_active = d_raw * prob
    d_gate = (d_active * up_pre * gate_sig * (1.0 + gate_pre * (1.0 - gate_sig))).astype(BF16)
    d_up = (d_active * act).astype(BF16)
    return active, d_gate, d_up


def finish_back(acc_ref, rows_ref, dprob_ref, gap, signs, hidden_ref, router, place_ref, back_refs, rg_ref):
    c = jax.nn.sigmoid(gap) * jax.nn.sigmoid(-gap) * dprob_ref[...] * signs
    c_high, c_low = hi_lo(c)
    for part in chunks(acc_ref.shape[1]):
        extra = dot_nt(c_high, router[part, :]) + dot_nt(c_low, router[part, :])
        rows_ref[:, part] = (acc_ref[:, part] + extra).astype(BF16)
    spread(place_ref, rows_ref, back_refs)
    kept = rg_ref.shape[0]
    t_high, t_low = hi_lo(jnp.transpose(c)[:kept])
    for part in chunks(acc_ref.shape[1]):
        hidden = hidden_ref[:, part]
        rg_ref[:, part] = dot_nn(t_high, hidden) + dot_nn(t_low, hidden)


def first_kernel(steps, x_refs, out_refs, gain_ref, router_ref, gate_ref, up_ref, down_ref,
                 place_ref, pick_ref, hidden_ref, info_ref, a_ref, b_ref,
                 rows_ref, acc_ref):
    step = pl.program_id(0)
    section = lax.axis_index("section")
    width = gain_ref.shape[1]

    @pl.when(step == 0)
    def _():
        me = lax.axis_index("expert").astype(F32)
        tail = joined(x_refs, pl.ds(width, LANES))
        place_rows(tail.astype(F32), me, place_ref, pick_ref)
        select(pick_ref, x_refs, rows_ref)
        info_ref[0] = signs_of(dot_nn(pick_ref[...], tail), me)

    @pl.when((step == 0) & (section == 0))
    def _():
        gap = norm_and_gap(rows_ref, gain_ref[...].astype(F32), router_ref[...], info_ref[0], hidden_ref)
        info_ref[1] = jnp.broadcast_to(gap, info_ref.shape[1:])

    @pl.when(section == 0)
    def _():
        gate_pre = dot_nn(hidden_ref[...], gate_ref[...])
        up_pre = dot_nn(hidden_ref[...], up_ref[...])
        a_ref[...] = gate_pre
        b_ref[...] = up_pre
        active = (gate_pre * jax.nn.sigmoid(gate_pre) * up_pre).astype(BF16)
        add_down(acc_ref, active, down_ref, step == 0)

    @pl.when(section != 0)
    def _():
        a_ref[...] = dot_nt(rows_ref[...], down_ref[...])

    @pl.when((step == steps - 1) & (section == 0))
    def _():
        prob = jax.nn.sigmoid(pick_lane(info_ref[1], 0))
        rows_ref[...] = (acc_ref[...] * prob).astype(BF16)
        spread(place_ref, rows_ref, out_refs)


def middle_kernel(steps, x_refs, back_refs, gain_ref, router_ref, place_ref, pick_ref, info_ref, raw_ref,
                  gate_ref, up_ref, down_ref,
                  prob_ref, rg_ref, active_ref,
                  rows_ref, hidden_ref, acc_ref, dprob_ref, gap_ref):
    step = pl.program_id(0)
    active_section = lax.axis_index("section") == 1

    @pl.when(active_section & (step == 0))
    def _():
        select(pick_ref, x_refs, rows_ref)
        gap = norm_and_gap(rows_ref, gain_ref[...].astype(F32), router_ref[...], info_ref[0], hidden_ref)
        gap_ref[...] = jnp.broadcast_to(gap, gap_ref.shape)
        prob_ref[...] = jax.nn.sigmoid(gap_ref[...])

    @pl.when(active_section)
    def _():
        gate_pre = dot_nn(hidden_ref[...], gate_ref[...])
        up_pre = dot_nn(hidden_ref[...], up_ref[...])
        prob = pick_lane(prob_ref[...], 0)
        active, d_gate, d_up = grads_of(gate_pre, up_pre, raw_ref[...], prob, step == 0, dprob_ref)
        active_ref[...] = active
        add_back(acc_ref, d_gate, d_up, gate_ref, up_ref, step == 0)

    @pl.when(active_section & (step == steps - 1))
    def _():
        finish_back(acc_ref, rows_ref, dprob_ref, gap_ref[...], info_ref[0], hidden_ref,
                    router_ref[...], place_ref, back_refs, rg_ref)


def last_kernel(steps, u_refs, out_refs, router_ref, place_ref, pick_ref, info_ref, hidden_ref, prob_ref,
                rg_in_ref, a_ref, b_ref, active_ref, gate_ref, up_ref, down_ref,
                rg_ref,
                rows_ref, acc_ref, dprob_ref):
    step = pl.program_id(0)
    section = lax.axis_index("section")

    @pl.when((section == 0) & (step == 0))
    def _():
        select(pick_ref, u_refs, rows_ref)

    @pl.when(section == 0)
    def _():
        prob = jax.nn.sigmoid(pick_lane(info_ref[1], 0))
        d_raw = dot_nt(rows_ref[...], down_ref[...])
        _, d_gate, d_up = grads_of(a_ref[...], b_ref[...], d_raw, prob, step == 0, dprob_ref)
        add_back(acc_ref, d_gate, d_up, gate_ref, up_ref, step == 0)

    @pl.when(section != 0)
    def _():
        add_down(acc_ref, active_ref[...], down_ref, step == 0)

    @pl.when((section == 0) & (step == steps - 1))
    def _():
        finish_back(acc_ref, rows_ref, dprob_ref, info_ref[1], info_ref[0], hidden_ref,
                    router_ref[...], place_ref, out_refs, rg_ref)

    @pl.when((section != 0) & (step == steps - 1))
    def _():
        rows_ref[...] = (acc_ref[...] * pick_lane(prob_ref[...], 0)).astype(BF16)
        spread(place_ref, rows_ref, out_refs)
        rg_ref[...] = rg_in_ref[...]


def whole(shape):
    return pl.BlockSpec(shape, lambda i: (0,) * len(shape))


def with_pieces(body, steps, count, inputs, groups, *refs):
    ins, rest = refs[:inputs], refs[inputs:]
    body(steps, ins[:count], rest[:groups], *ins[count:], *rest[groups:])


def expert_call(body, steps, pieces, small, tiled, weights, outs, tiled_outs, scratch, flops):
    gate_w, up_w, down_w = weights
    width, hidden = gate_w.shape
    tile = hidden // steps
    small = list(pieces) + small
    groups = lax.axis_size("dp")
    group_rows = sum(p.shape[0] for p in pieces) // groups
    outs = [jax.ShapeDtypeStruct((group_rows, width), BF16)] * groups + outs
    rows = [whole(a.shape) for a in small]
    rows += [pl.BlockSpec((a.shape[0], tile), lambda i: (0, i)) for a in tiled]
    rows += [pl.BlockSpec((width, tile), lambda i: (0, i))] * 2
    rows += [pl.BlockSpec((tile, width), lambda i: (i, 0))]
    out_specs = [whole(o.shape) for o in outs]
    out_specs += [pl.BlockSpec((o.shape[0], tile), lambda i: (0, i)) for o in tiled_outs]
    size = lambda a: a.size * a.dtype.itemsize
    held = sum(2 * size(a) for a in small + outs) + 24 * 2**20
    results = pl.pallas_call(
        functools.partial(with_pieces, body, steps, len(pieces), len(rows), groups),
        grid=(steps,),
        in_specs=rows,
        out_specs=out_specs,
        out_shape=outs + tiled_outs,
        scratch_shapes=scratch,
        cost_estimate=pl.CostEstimate(
            flops=flops, bytes_accessed=sum(map(size, weights)), transcendentals=0
        ),
        compiler_params=pltpu.CompilerParams(vmem_limit_bytes=min(held, 60 * 2**20)),
    )(*small, *tiled, *weights)
    return results[:groups], *results[groups:]


def moved(block, axes, target):
    sizes = [lax.axis_size(a) for a in axes]
    spots = [()]
    for n in sizes:
        spots = [spot + (i,) for spot in spots for i in range(n)]
    number = {spot: i for i, spot in enumerate(spots)}
    pairs = [(number[spot], number[target(*spot)]) for spot in spots if target(*spot) in number]
    return lax.ppermute(block, axes, pairs)


def flips():
    bits = lax.axis_size("dp").bit_length() - 1
    return [1 << b for b in reversed(range(bits))]


def flipped(block, bit):
    return moved(block, ("dp",), lambda d: (d ^ bit,))


def gathered(block, distance):
    count = lax.axis_size("expert")
    if distance == 0:
        parts = [block] + [
            moved(block, ("expert",), lambda e, k=k: ((e + k) % count,)) for k in range(1, count)
        ]
    else:
        parts = [
            moved(block, ("section", "expert"), lambda s, e, k=k: (s + distance, (e + k) % count))
            for k in range(count)
        ]
    groups = [parts]
    for bit in flips():
        groups = groups + [[flipped(part, bit) for part in group] for group in groups]
    return [part for group in groups for part in group]


def combined(pieces):
    count = lax.axis_size("expert")
    own = pieces[0].shape[0] // count
    add = lambda kept, came: (kept.astype(F32) + came.astype(F32)).astype(BF16)
    cut = lambda group: [group[k * own:(k + 1) * own] for k in range(count)]
    order = list(reversed(flips()))
    half = len(pieces) // 2
    came = [flipped(group, order[0]) for group in pieces[half:]]
    groups = [
        [add(*pair) for pair in zip(cut(kept), cut(got))] for kept, got in zip(pieces[:half], came)
    ]
    for bit in order[1:]:
        groups = lax.optimization_barrier(groups)
        half = len(groups) // 2
        groups = [
            [add(kept, flipped(sent, bit)) for kept, sent in zip(*pair)]
            for pair in zip(groups[:half], groups[half:])
        ]
    parts = groups[0]
    total = parts[0].astype(F32)
    for k in range(1, count):
        total = total + moved(parts[k], ("expert",), lambda e, k=k: ((e - k) % count,)).astype(F32)
    return total


def summed(block):
    for bit in flips():
        block = block + flipped(block, bit)
    count = lax.axis_size("expert")
    for bit in [1 << b for b in range(count.bit_length() - 1)]:
        block = block + moved(block, ("expert",), lambda e, bit=bit: (e ^ bit,))
    return block


def sent_on(block, distance):
    return moved(block, ("section",), lambda s: (s + distance,))


def input_grad(layer_in, upstream, d_hidden, gain_row):
    values = layer_in.astype(F32)
    inv_rms = lax.rsqrt(jnp.mean(values * values, axis=-1, keepdims=True) + EPSILON)
    weighted = gain_row * d_hidden
    mean = jnp.mean(values * weighted, axis=-1, keepdims=True)
    cubed = inv_rms * inv_rms * inv_rms
    d_in = upstream.astype(F32) + inv_rms * weighted - values * cubed * mean
    return d_in.astype(BF16)


def per_device(inputs, cotangent, norm_gain, router, w_gate, w_up, w_down, routes):
    section = lax.axis_index("section")
    at_start = section == 0
    micro, toks, width = inputs.shape
    experts, top_k = router.shape[2], routes.shape[3]
    capacity = 3 * top_k * toks // (2 * experts)
    peers = lax.axis_size("expert") * lax.axis_size("dp")
    own = micro * toks
    tokens, rows = peers * own, peers * micro * capacity
    weights = (w_gate[0, 0], w_up[0, 0], w_down[0, 0])
    hidden_units = weights[0].shape[1]
    tile = 256 if hidden_units % 256 == 0 else hidden_units
    steps = hidden_units // tile
    gain_row = norm_gain[0].astype(F32)
    router_w = jnp.pad(router[0], ((0, 0), (0, LANES - experts)))
    kept = -(-experts // 8) * 8
    shape = jax.ShapeDtypeStruct
    dot_flops = 2 * rows * width * hidden_units

    mine = jnp.where(at_start, inputs, cotangent).reshape(own, width)
    tail = jnp.pad(routes[0].reshape(own, top_k).astype(BF16), ((0, 0), (0, LANES - top_k)))
    payload = jnp.concatenate([mine, tail], axis=1)
    out, place, pick, hidden, info, stash_a, stash_b = expert_call(
        first_kernel, steps, gathered(payload, 0), [norm_gain, router_w], [], weights,
        [shape((tokens, rows), BF16), shape((rows, tokens), BF16),
         shape((rows, width), BF16), shape((2, rows, LANES), F32)],
        [shape((rows, hidden_units), F32), shape((rows, hidden_units), F32)],
        [pltpu.VMEM((rows, width), BF16), pltpu.VMEM((rows, width), F32)],
        3 * dot_flops,
    )
    acts_start = (mine.astype(F32) + combined(out)).astype(BF16)

    back, prob, rg, active = expert_call(
        middle_kernel, steps, gathered(acts_start, 1),
        [norm_gain, router_w, place, pick, info], [stash_a], weights,
        [shape((rows, LANES), F32), shape((kept, width), F32)],
        [shape((rows, hidden_units), BF16)],
        [pltpu.VMEM((rows, width), BF16), pltpu.VMEM((rows, width), BF16),
         pltpu.VMEM((rows, width), F32), pltpu.VMEM((rows, LANES), F32), pltpu.VMEM((rows, LANES), F32)],
        4 * dot_flops,
    )
    arrived = sent_on(acts_start, 1)
    grads_end = input_grad(arrived, mine, combined(back), gain_row)

    out, rg = expert_call(
        last_kernel, steps, gathered(grads_end, -1),
        [router_w, place, pick, info, hidden, prob, rg],
        [stash_a, stash_b, active], weights,
        [shape((kept, width), F32)], [],
        [pltpu.VMEM((rows, width), BF16), pltpu.VMEM((rows, width), F32), pltpu.VMEM((rows, LANES), F32)],
        3 * dot_flops,
    )
    total = combined(out)
    upstream = sent_on(grads_end, -1)
    router_total = summed(rg)[:experts].T
    grads_start = input_grad(mine, upstream, total, gain_row)
    acts_end = (arrived.astype(F32) + total).astype(BF16)
    acts = jnp.where(at_start, acts_start, acts_end).reshape(1, micro, toks, width)
    grads = jnp.where(at_start, grads_start, grads_end).reshape(1, micro, toks, width)
    return acts, grads, router_total[None]


def solution(mesh):
    placed = (
        P(None, GROUP, None),
        P(None, GROUP, None),
        P("section", None),
        P("section", None, None),
        P("section", "expert", None, "dp"),
        P("section", "expert", None, "dp"),
        P("section", "expert", "dp", None),
        P("section", None, GROUP, None),
    )
    return jax.shard_map(
        per_device,
        mesh=mesh,
        in_specs=placed,
        out_specs=(
            P("section", None, GROUP, None),
            P("section", None, GROUP, None),
            P("section", None, None),
        ),
        check_vma=False,
    )
```

```python
import functools

import jax
import jax.numpy as jnp
from jax import lax
from jax.experimental import pallas as pl
from jax.experimental.pallas import tpu as pltpu
from jax.sharding import PartitionSpec as P

EPSILON = 1e-05
LANES = 128
GROUP = ("expert", "dp")
F32 = jnp.float32
BF16 = jnp.bfloat16


def dot_nn(a, b):
    return jnp.dot(a, b, preferred_element_type=F32)


def dot_nt(a, b):
    return lax.dot_general(a, b, (((1,), (1,)), ((), ())), preferred_element_type=F32)


def chunks(total):
    step = next(c for c in (512, 384, 256, 128) if total % c == 0)
    return [pl.ds(start, step) for start in range(0, total, step)]


def lanes_like(rows):
    return lax.broadcasted_iota(jnp.int32, (rows, LANES), 1)


def pick_lane(block, lane):
    return jnp.sum(jnp.where(lanes_like(block.shape[0]) == lane, block, 0.0), axis=1, keepdims=True)


def hi_lo(block):
    high = block.astype(BF16)
    return high, (block - high.astype(F32)).astype(BF16)


def place_rows(tail, me, place_ref, pick_ref):
    tokens, rows = place_ref.shape
    wide = -(-rows // LANES) * LANES
    first, second = pick_lane(tail, 0), pick_lane(tail, 1)
    mine = jnp.broadcast_to(((first == me) | (second == me)).astype(F32), (tokens, wide))
    row = lax.broadcasted_iota(jnp.int32, (tokens, tokens), 0)
    col = lax.broadcasted_iota(jnp.int32, (tokens, tokens), 1)
    earlier = dot_nn((col < row).astype(F32).astype(BF16), mine.astype(BF16))
    slot = lax.broadcasted_iota(jnp.int32, (tokens, wide), 1).astype(F32)
    place = jnp.where((earlier == slot) & (mine > 0.5), 1.0, 0.0)
    place_ref[...] = place[:, :rows].astype(BF16)
    pick_ref[...] = jnp.transpose(place)[:rows].astype(BF16)


def signs_of(tail, me):
    first, second = pick_lane(tail, 0), pick_lane(tail, 1)
    other = first + second - me
    lane = lanes_like(tail.shape[0]).astype(F32)
    both = (lane == me).astype(F32) - (lane == other).astype(F32)
    return jnp.where(first != second, both, 0.0)


def norm_and_gap(rows_ref, gain_ref, router_ref, signs, hidden_ref):
    parts = chunks(rows_ref.shape[1])
    squares = 0.0
    for part in parts:
        values = rows_ref[:, part].astype(F32)
        squares = squares + jnp.sum(values * values, axis=1, keepdims=True)
    inv_rms = lax.rsqrt(squares / rows_ref.shape[1] + EPSILON)
    logits = 0.0
    for part in parts:
        hidden = (rows_ref[:, part].astype(F32) * inv_rms * gain_ref[:, part].astype(F32)).astype(BF16)
        hidden_ref[:, part] = hidden
        logits = logits + dot_nn(hidden, router_ref[part, :])
    return jnp.sum(logits * signs, axis=1, keepdims=True)


class Loads:
    def __init__(self, source, target, sems, axis):
        self.count, total = sems.shape[0], target.shape[axis]
        step = total // self.count
        self.parts = [pl.ds(i * step, step) for i in range(self.count)]
        spot = lambda part: (slice(None), part) if axis else (part,)
        self.copies = [
            pltpu.make_async_copy(source.at[spot(part)], target.at[spot(part)], sems.at[i])
            for i, part in enumerate(self.parts)
        ]

    def start(self, i):
        self.copies[i].start()

    def start_all(self):
        for copy in self.copies:
            copy.start()

    def wait(self, i):
        self.copies[i].wait()


def start_pair(gate_loads, up_loads):
    for i in range(gate_loads.count):
        gate_loads.start(i)
        up_loads.start(i)


def select(pick_ref, x_ref, rows_ref):
    for part in chunks(rows_ref.shape[1]):
        rows_ref[:, part] = dot_nn(pick_ref[...], x_ref[:, part]).astype(BF16)


def piece_copies(x_refs, x_ref, sems):
    start, copies = 0, []
    for i, ref in enumerate(x_refs):
        copies.append(pltpu.make_async_copy(ref, x_ref.at[pl.ds(start, ref.shape[0])], sems.at[i]))
        start += ref.shape[0]
    return copies


def fetch(x_refs, x_ref, sems):
    copies = piece_copies(x_refs, x_ref, sems)
    for copy in copies:
        copy.start()
    for copy in copies:
        copy.wait()


def spread(place_ref, rows, out_refs, part):
    piece = out_refs[0].shape[0]
    block = dot_nn(place_ref[...], rows).astype(BF16)
    for i, out_ref in enumerate(out_refs):
        out_ref[:, part] = block[i * piece:(i + 1) * piece]


def turn(rows_ref, turned_ref):
    for part in chunks(rows_ref.shape[1]):
        turned_ref[part, :] = jnp.transpose(rows_ref[:, part].astype(F32)).astype(BF16)


def send_down(active_ref, down_ref, down_loads, prob, place_ref, out_refs):
    for i, part in enumerate(down_loads.parts):
        down_loads.wait(i)
        rows = dot_nn(active_ref[...], down_ref[:, part]) * prob
        spread(place_ref, rows.astype(BF16), out_refs, part)


def grads_of(gate_pre, up_pre, d_raw, prob, part, dprob_ref, active_ref, d_gate_ref, d_up_ref):
    gate_sig = jax.nn.sigmoid(gate_pre)
    act = gate_pre * gate_sig
    active = (act * up_pre).astype(BF16)
    if active_ref is not None:
        active_ref[:, part] = active
    gain = jnp.sum(active.astype(F32) * d_raw, axis=1, keepdims=True)
    dprob_ref[...] += jnp.broadcast_to(gain, dprob_ref.shape)
    d_active = d_raw * prob
    d_gate = d_active * up_pre * gate_sig * (1.0 + gate_pre * (1.0 - gate_sig))
    d_gate_ref[part, :] = jnp.transpose(d_gate).astype(BF16)
    d_up_ref[part, :] = jnp.transpose(d_active * act).astype(BF16)


def send_back(gate_ref, up_ref, gate_loads, up_loads, d_gate_ref, d_up_ref, dprob_ref, gap, signs,
              hidden_ref, router_ref, place_ref, out_refs, rg_ref):
    c = jax.nn.sigmoid(gap) * jax.nn.sigmoid(-gap) * dprob_ref[...] * signs
    c_high, c_low = hi_lo(c)
    t_high, t_low = hi_lo(jnp.transpose(c)[:rg_ref.shape[0]])
    width = gate_ref.shape[0]
    step = width // gate_loads.count if gate_loads is not None else 256
    for i in range(width // step):
        part = pl.ds(i * step, step)
        if gate_loads is not None:
            gate_loads.wait(i)
            up_loads.wait(i)
        turned = dot_nn(gate_ref[part, :], d_gate_ref[...]) + dot_nn(up_ref[part, :], d_up_ref[...])
        extra = dot_nt(c_high, router_ref[part, :]) + dot_nt(c_low, router_ref[part, :])
        spread(place_ref, (jnp.transpose(turned) + extra).astype(BF16), out_refs, part)
        hidden = hidden_ref[:, part]
        rg_ref[:, part] = dot_nn(t_high, hidden) + dot_nn(t_low, hidden)


def first_kernel(x_refs, out_refs, gain_ref, router_ref, gate_in, up_in, down_in,
                 place_ref, pick_ref, hidden_ref, info_ref, a_ref, b_ref,
                 x_ref, x_sems, gate_ref, up_ref, down_ref, hidden_sems, hidden_sems_b, width_sems, width_sems_b,
                 rows_ref, turned_ref, active_ref):
    section = lax.axis_index("section")
    width = gain_ref.shape[1]
    gate_loads = Loads(gate_in, gate_ref, hidden_sems, 1)
    up_loads = Loads(up_in, up_ref, hidden_sems_b, 1)
    down_cols = Loads(down_in, down_ref, width_sems, 1)
    down_rows = Loads(down_in, down_ref, hidden_sems, 0)
    fetches = piece_copies(x_refs, x_ref, x_sems)
    for copy in fetches:
        copy.start()

    @pl.when(section == 0)
    def _():
        start_pair(gate_loads, up_loads)
        down_cols.start_all()

    @pl.when(section != 0)
    def _():
        down_rows.start_all()

    for copy in fetches:
        copy.wait()
    me = lax.axis_index("expert").astype(F32)
    tail = x_ref[:, width:]
    place_rows(tail.astype(F32), me, place_ref, pick_ref)
    select(pick_ref, x_ref, rows_ref)
    info_ref[0] = signs_of(dot_nn(pick_ref[...], tail), me)

    @pl.when(section == 0)
    def _():
        gap = norm_and_gap(rows_ref, gain_ref, router_ref, info_ref[0], hidden_ref)
        info_ref[1] = jnp.broadcast_to(gap, info_ref.shape[1:])
        for i, part in enumerate(gate_loads.parts):
            gate_loads.wait(i)
            up_loads.wait(i)
            gate_pre = dot_nn(hidden_ref[...], gate_ref[:, part])
            up_pre = dot_nn(hidden_ref[...], up_ref[:, part])
            a_ref[:, part] = gate_pre.astype(BF16)
            b_ref[:, part] = up_pre.astype(BF16)
            active_ref[:, part] = (gate_pre * jax.nn.sigmoid(gate_pre) * up_pre).astype(BF16)
        send_down(active_ref, down_ref, down_cols, jax.nn.sigmoid(gap), place_ref, out_refs)

    @pl.when(section != 0)
    def _():
        turn(rows_ref, turned_ref)
        for i, part in enumerate(down_rows.parts):
            down_rows.wait(i)
            a_ref[:, part] = jnp.transpose(dot_nn(down_ref[part, :], turned_ref[...])).astype(BF16)


def middle_kernel(x_refs, back_refs, gain_ref, router_ref, place_ref, pick_ref, info_ref, raw_ref,
                  gate_in, up_in, down_in,
                  active_ref, prob_ref, rg_ref,
                  x_ref, x_sems, gate_ref, up_ref, down_ref, hidden_sems, hidden_sems_b, width_sems, width_sems_b,
                  rows_ref, hidden_ref, d_gate_ref, d_up_ref, dprob_ref):
    @pl.when(lax.axis_index("section") == 1)
    def _():
        gate_loads = Loads(gate_in, gate_ref, hidden_sems, 1)
        up_loads = Loads(up_in, up_ref, hidden_sems_b, 1)
        fetches = piece_copies(x_refs, x_ref, x_sems)
        for copy in fetches:
            copy.start()
        start_pair(gate_loads, up_loads)
        for copy in fetches:
            copy.wait()
        select(pick_ref, x_ref, rows_ref)
        signs = info_ref[0]
        gap = norm_and_gap(rows_ref, gain_ref, router_ref, signs, hidden_ref)
        prob = jax.nn.sigmoid(gap)
        prob_ref[...] = jnp.broadcast_to(prob, prob_ref.shape)
        dprob_ref[...] = jnp.zeros_like(dprob_ref)
        for i, part in enumerate(gate_loads.parts):
            gate_loads.wait(i)
            up_loads.wait(i)
            gate_pre = dot_nn(hidden_ref[...], gate_ref[:, part])
            up_pre = dot_nn(hidden_ref[...], up_ref[:, part])
            grads_of(gate_pre, up_pre, raw_ref[:, part].astype(F32), prob, part, dprob_ref,
                     active_ref, d_gate_ref, d_up_ref)
        send_back(gate_ref, up_ref, None, None, d_gate_ref, d_up_ref, dprob_ref, gap, signs,
                  hidden_ref, router_ref, place_ref, back_refs, rg_ref)


def last_kernel(u_refs, out_refs, router_ref, place_ref, pick_ref, info_ref, hidden_ref, prob_ref,
                rg_in_ref, a_ref, b_ref, active_ref, gate_in, up_in, down_in,
                rg_ref,
                x_ref, x_sems, gate_ref, up_ref, down_ref, hidden_sems, hidden_sems_b, width_sems, width_sems_b,
                rows_ref, turned_ref, d_gate_ref, d_up_ref, dprob_ref):
    section = lax.axis_index("section")

    @pl.when(section == 0)
    def _():
        down_rows = Loads(down_in, down_ref, hidden_sems, 0)
        gate_loads = Loads(gate_in, gate_ref, width_sems, 0)
        up_loads = Loads(up_in, up_ref, width_sems_b, 0)
        fetches = piece_copies(u_refs, x_ref, x_sems)
        for copy in fetches:
            copy.start()
        down_rows.start_all()
        start_pair(gate_loads, up_loads)
        for copy in fetches:
            copy.wait()
        select(pick_ref, x_ref, rows_ref)
        turn(rows_ref, turned_ref)
        gap = pick_lane(info_ref[1], 0)
        prob = jax.nn.sigmoid(gap)
        dprob_ref[...] = jnp.zeros_like(dprob_ref)
        for i, part in enumerate(down_rows.parts):
            down_rows.wait(i)
            d_raw = jnp.transpose(dot_nn(down_ref[part, :], turned_ref[...]))
            grads_of(a_ref[:, part].astype(F32), b_ref[:, part].astype(F32), d_raw, prob, part,
                     dprob_ref, None, d_gate_ref, d_up_ref)
        send_back(gate_ref, up_ref, gate_loads, up_loads, d_gate_ref, d_up_ref, dprob_ref, gap,
                  info_ref[0], hidden_ref, router_ref, place_ref, out_refs, rg_ref)

    @pl.when(section != 0)
    def _():
        down_cols = Loads(down_in, down_ref, width_sems, 1)
        down_cols.start_all()
        send_down(active_ref, down_ref, down_cols, pick_lane(prob_ref[...], 0), place_ref, out_refs)
        rg_ref[...] = rg_in_ref[...]


def with_pieces(body, count, inputs, groups, *refs):
    ins, rest = refs[:inputs], refs[inputs:]
    body(ins[:count], rest[:groups], *ins[count:], *rest[groups:])


def expert_call(body, pieces, small, weights, outs, scratch, flops):
    width, hidden_units = weights[0].shape
    shape = jax.ShapeDtypeStruct
    groups = lax.axis_size("dp")
    tokens = sum(p.shape[0] for p in pieces)
    outs = [shape((tokens // groups, width), BF16)] * groups + outs
    sems = lambda total: pltpu.SemaphoreType.DMA((max(1, total // 256),))
    scratch = [
        pltpu.VMEM((tokens, pieces[0].shape[1]), BF16), pltpu.SemaphoreType.DMA((len(pieces),)),
        *[pltpu.VMEM(w.shape, BF16) for w in weights],
        sems(hidden_units), sems(hidden_units), sems(width), sems(width),
    ] + scratch
    held = sum(w.size * w.dtype.itemsize for w in weights)
    block, outside = pl.BlockSpec(memory_space=pltpu.VMEM), pl.BlockSpec(memory_space=pl.ANY)
    in_specs = [outside] * len(pieces) + [block] * len(small) + [outside] * len(weights)
    results = pl.pallas_call(
        functools.partial(with_pieces, body, len(pieces), len(in_specs), groups),
        in_specs=in_specs,
        out_specs=[block] * len(outs),
        out_shape=outs,
        scratch_shapes=scratch,
        cost_estimate=pl.CostEstimate(flops=flops, bytes_accessed=held, transcendentals=0),
        compiler_params=pltpu.CompilerParams(
            vmem_limit_bytes=held + 6 * 2**20 + 4 * tokens * width * 2
        ),
    )(*pieces, *small, *weights)
    return results[:groups], *results[groups:]


def moved(block, axes, target):
    sizes = [lax.axis_size(a) for a in axes]
    spots = [()]
    for n in sizes:
        spots = [spot + (i,) for spot in spots for i in range(n)]
    number = {spot: i for i, spot in enumerate(spots)}
    pairs = [(number[spot], number[target(*spot)]) for spot in spots if target(*spot) in number]
    return lax.ppermute(block, axes, pairs)


def flips():
    bits = lax.axis_size("dp").bit_length() - 1
    return [1 << b for b in reversed(range(bits))]


def flipped(block, bit):
    return moved(block, ("dp",), lambda d: (d ^ bit,))


def gathered(block, distance):
    count = lax.axis_size("expert")
    if distance == 0:
        parts = [block] + [
            moved(block, ("expert",), lambda e, k=k: ((e + k) % count,)) for k in range(1, count)
        ]
    else:
        parts = [
            moved(block, ("section", "expert"), lambda s, e, k=k: (s + distance, (e + k) % count))
            for k in range(count)
        ]
    groups = [parts]
    for bit in flips():
        groups = groups + [[flipped(part, bit) for part in group] for group in groups]
    return [part for group in groups for part in group]


def combined(pieces):
    count = lax.axis_size("expert")
    own = pieces[0].shape[0] // count
    add = lambda kept, came: (kept.astype(F32) + came.astype(F32)).astype(BF16)
    cut = lambda group: [group[k * own:(k + 1) * own] for k in range(count)]
    order = list(reversed(flips()))
    half = len(pieces) // 2
    came = [flipped(group, order[0]) for group in pieces[half:]]
    groups = [
        [add(*pair) for pair in zip(cut(kept), cut(got))] for kept, got in zip(pieces[:half], came)
    ]
    for bit in order[1:]:
        groups = lax.optimization_barrier(groups)
        half = len(groups) // 2
        groups = [
            [add(kept, flipped(sent, bit)) for kept, sent in zip(*pair)]
            for pair in zip(groups[:half], groups[half:])
        ]
    parts = groups[0]
    total = parts[0].astype(F32)
    for k in range(1, count):
        total = total + moved(parts[k], ("expert",), lambda e, k=k: ((e - k) % count,)).astype(F32)
    return total


def summed(block):
    for bit in flips():
        block = block + flipped(block, bit)
    count = lax.axis_size("expert")
    for bit in [1 << b for b in range(count.bit_length() - 1)]:
        block = block + moved(block, ("expert",), lambda e, bit=bit: (e ^ bit,))
    return block


def sent_on(block, distance):
    return moved(block, ("section",), lambda s: (s + distance,))


def input_grad(layer_in, upstream, d_hidden, gain_row):
    values = layer_in.astype(F32)
    inv_rms = lax.rsqrt(jnp.mean(values * values, axis=-1, keepdims=True) + EPSILON)
    weighted = gain_row * d_hidden
    mean = jnp.mean(values * weighted, axis=-1, keepdims=True)
    cubed = inv_rms * inv_rms * inv_rms
    d_in = upstream.astype(F32) + inv_rms * weighted - values * cubed * mean
    return d_in.astype(BF16)


def per_device(inputs, cotangent, norm_gain, router, w_gate, w_up, w_down, routes):
    section = lax.axis_index("section")
    at_start = section == 0
    micro, toks, width = inputs.shape
    experts, top_k = router.shape[2], routes.shape[3]
    capacity = 3 * top_k * toks // (2 * experts)
    peers = lax.axis_size("expert") * lax.axis_size("dp")
    own = micro * toks
    tokens, rows = peers * own, peers * micro * capacity
    weights = (w_gate[0, 0], w_up[0, 0], w_down[0, 0])
    hidden_units = weights[0].shape[1]
    gain_row = norm_gain[0].astype(F32)
    router_w = jnp.pad(router[0], ((0, 0), (0, LANES - experts)))
    kept = -(-experts // 8) * 8
    shape = jax.ShapeDtypeStruct
    dot_flops = 2 * rows * width * hidden_units
    row_block, turned = pltpu.VMEM((rows, width), BF16), pltpu.VMEM((width, rows), BF16)
    d_block, lane_block = pltpu.VMEM((hidden_units, rows), BF16), pltpu.VMEM((rows, LANES), F32)

    mine = jnp.where(at_start, inputs, cotangent).reshape(own, width)
    tail = jnp.pad(routes[0].reshape(own, top_k).astype(BF16), ((0, 0), (0, LANES - top_k)))
    payload = jnp.concatenate([mine, tail], axis=1)
    out, place, pick, hidden, info, stash_a, stash_b = expert_call(
        first_kernel, gathered(payload, 0), [norm_gain, router_w], weights,
        [shape((tokens, rows), BF16), shape((rows, tokens), BF16),
         shape((rows, width), BF16), shape((2, rows, LANES), F32),
         shape((rows, hidden_units), BF16), shape((rows, hidden_units), BF16)],
        [row_block, turned, pltpu.VMEM((rows, hidden_units), BF16)],
        3 * dot_flops,
    )
    acts_start = (mine.astype(F32) + combined(out)).astype(BF16)

    back, active, prob, rg = expert_call(
        middle_kernel, gathered(acts_start, 1),
        [norm_gain, router_w, place, pick, info, stash_a], weights,
        [shape((rows, hidden_units), BF16), shape((rows, LANES), F32), shape((kept, width), F32)],
        [row_block, row_block, d_block, d_block, lane_block],
        4 * dot_flops,
    )
    arrived = sent_on(acts_start, 1)
    grads_end = input_grad(arrived, mine, combined(back), gain_row)

    out, rg = expert_call(
        last_kernel, gathered(grads_end, -1),
        [router_w, place, pick, info, hidden, prob, rg, stash_a, stash_b, active], weights,
        [shape((kept, width), F32)],
        [row_block, turned, d_block, d_block, lane_block],
        3 * dot_flops,
    )
    total = combined(out)
    upstream = sent_on(grads_end, -1)
    router_total = summed(rg)[:experts].T
    grads_start = input_grad(mine, upstream, total, gain_row)
    acts_end = (arrived.astype(F32) + total).astype(BF16)
    acts = jnp.where(at_start, acts_start, acts_end).reshape(1, micro, toks, width)
    grads = jnp.where(at_start, grads_start, grads_end).reshape(1, micro, toks, width)
    return acts, grads, router_total[None]


def solution(mesh):
    placed = (
        P(None, GROUP, None),
        P(None, GROUP, None),
        P("section", None),
        P("section", None, None),
        P("section", "expert", None, "dp"),
        P("section", "expert", None, "dp"),
        P("section", "expert", "dp", None),
        P("section", None, GROUP, None),
    )
    return jax.shard_map(
        per_device,
        mesh=mesh,
        in_specs=placed,
        out_specs=(
            P("section", None, GROUP, None),
            P("section", None, GROUP, None),
            P("section", None, None),
        ),
        check_vma=False,
    )
```

```python
import functools

import jax
import jax.numpy as jnp
from jax import lax
from jax.experimental import pallas as pl
from jax.experimental.pallas import tpu as pltpu
from jax.sharding import PartitionSpec as P

EPSILON = 1e-05
LANES = 128
GROUP = ("expert", "dp")
F32 = jnp.float32
BF16 = jnp.bfloat16


def dot_nn(a, b):
    return jnp.dot(a, b, preferred_element_type=F32)


def dot_nt(a, b):
    return lax.dot_general(a, b, (((1,), (1,)), ((), ())), preferred_element_type=F32)


def chunks(total):
    step = next(c for c in (512, 384, 256, 128) if total % c == 0)
    return [pl.ds(start, step) for start in range(0, total, step)]


def lanes_like(rows):
    return lax.broadcasted_iota(jnp.int32, (rows, LANES), 1)


def pick_lane(block, lane):
    return jnp.sum(jnp.where(lanes_like(block.shape[0]) == lane, block, 0.0), axis=1, keepdims=True)


def hi_lo(block):
    high = block.astype(BF16)
    return high, (block - high.astype(F32)).astype(BF16)


def place_rows(tail, me, place_ref, pick_ref):
    tokens, rows = place_ref.shape
    wide = -(-rows // LANES) * LANES
    first, second = pick_lane(tail, 0), pick_lane(tail, 1)
    mine = jnp.broadcast_to(((first == me) | (second == me)).astype(F32), (tokens, wide))
    row = lax.broadcasted_iota(jnp.int32, (tokens, tokens), 0)
    col = lax.broadcasted_iota(jnp.int32, (tokens, tokens), 1)
    earlier = dot_nn((col < row).astype(F32).astype(BF16), mine.astype(BF16))
    slot = lax.broadcasted_iota(jnp.int32, (tokens, wide), 1).astype(F32)
    place = jnp.where((earlier == slot) & (mine > 0.5), 1.0, 0.0)
    place_ref[...] = place[:, :rows].astype(BF16)
    pick_ref[...] = jnp.transpose(place)[:rows].astype(BF16)


def signs_of(tail, me):
    first, second = pick_lane(tail, 0), pick_lane(tail, 1)
    other = first + second - me
    lane = lanes_like(tail.shape[0]).astype(F32)
    both = (lane == me).astype(F32) - (lane == other).astype(F32)
    return jnp.where(first != second, both, 0.0)


def norm_and_gap(rows_ref, gain_ref, router_ref, signs, hidden_ref):
    rows, width = rows_ref.shape

    def square(i, part, total):
        values = rows_ref[:, part].astype(F32)
        return total + jnp.sum(values * values, axis=1, keepdims=True)

    squares = tiles(width, square, jnp.zeros((rows, 1), F32))
    inv_rms = lax.rsqrt(squares / width + EPSILON)

    def scale(i, part, total):
        hidden = (rows_ref[:, part].astype(F32) * inv_rms * gain_ref[:, part].astype(F32)).astype(BF16)
        hidden_ref[:, part] = hidden
        return total + dot_nn(hidden, router_ref[part, :])

    logits = tiles(width, scale, jnp.zeros((rows, LANES), F32))
    return jnp.sum(logits * signs, axis=1, keepdims=True)


def tiles(total, body, carry=0):
    step = next(c for c in (256, 128) if total % c == 0)

    def one(i, carry):
        return body(i, pl.ds(pl.multiple_of(i * step, step), step), carry)

    return lax.fori_loop(0, total // step, one, carry)


class Loads:
    def __init__(self, source, target, sems, axis):
        self.source, self.target, self.sems, self.axis = source, target, sems, axis
        self.count, self.total = sems.shape[0], target.shape[axis]

    def copy(self, i):
        step = self.total // self.count
        part = pl.ds(pl.multiple_of(i * step, step), step)
        spot = (slice(None), part) if self.axis else (part,)
        return pltpu.make_async_copy(self.source.at[spot], self.target.at[spot], self.sems.at[i])

    def wait(self, i):
        self.copy(i).wait()


def start_all(*loads):
    def one(i, carry):
        for load in loads:
            load.copy(i).start()
        return carry

    lax.fori_loop(0, loads[0].count, one, 0)


def select(pick_ref, x_ref, rows_ref, turned_ref=None):
    def body(i, part, carry):
        rows = dot_nn(pick_ref[...], x_ref[:, part])
        rows_ref[:, part] = rows.astype(BF16)
        if turned_ref is not None:
            turned_ref[part, :] = jnp.transpose(rows).astype(BF16)
        return carry

    tiles(rows_ref.shape[1], body)


def piece_copies(x_refs, x_ref, sems):
    start, copies = 0, []
    for i, ref in enumerate(x_refs):
        copies.append(pltpu.make_async_copy(ref, x_ref.at[pl.ds(start, ref.shape[0])], sems.at[i]))
        start += ref.shape[0]
    return copies


def fetch(x_refs, x_ref, sems):
    copies = piece_copies(x_refs, x_ref, sems)
    for copy in copies:
        copy.start()
    for copy in copies:
        copy.wait()


def spread(place_ref, rows, out_refs, part):
    piece = out_refs[0].shape[0]
    block = dot_nn(place_ref[...], rows).astype(BF16)
    for i, out_ref in enumerate(out_refs):
        out_ref[:, part] = block[i * piece:(i + 1) * piece]


def send_down(active_ref, down_ref, down_loads, prob, place_ref, out_refs):
    def body(i, part, carry):
        down_loads.wait(i)
        rows = dot_nn(active_ref[...], down_ref[:, part]) * prob
        spread(place_ref, rows.astype(BF16), out_refs, part)
        return carry

    tiles(down_ref.shape[1], body)


def grads_of(gate_pre, up_pre, d_raw, prob, part, dprob_ref, active_ref, d_gate_ref, d_up_ref):
    gate_sig = jax.nn.sigmoid(gate_pre)
    act = gate_pre * gate_sig
    active = (act * up_pre).astype(BF16)
    if active_ref is not None:
        active_ref[:, part] = active
    gain = jnp.sum(active.astype(F32) * d_raw, axis=1, keepdims=True)
    dprob_ref[...] += jnp.broadcast_to(gain, dprob_ref.shape)
    d_active = d_raw * prob
    d_gate = d_active * up_pre * gate_sig * (1.0 + gate_pre * (1.0 - gate_sig))
    d_gate_ref[part, :] = jnp.transpose(d_gate).astype(BF16)
    d_up_ref[part, :] = jnp.transpose(d_active * act).astype(BF16)


def send_back(gate_ref, up_ref, gate_loads, up_loads, d_gate_ref, d_up_ref, dprob_ref, gap, signs,
              hidden_ref, router_ref, place_ref, out_refs, rg_ref):
    c = jax.nn.sigmoid(gap) * jax.nn.sigmoid(-gap) * dprob_ref[...] * signs
    c_high, c_low = hi_lo(c)
    t_high, t_low = hi_lo(jnp.transpose(c)[:rg_ref.shape[0]])

    def body(i, part, carry):
        if gate_loads is not None:
            gate_loads.wait(i)
            up_loads.wait(i)
        turned = dot_nn(gate_ref[part, :], d_gate_ref[...]) + dot_nn(up_ref[part, :], d_up_ref[...])
        extra = dot_nt(c_high, router_ref[part, :]) + dot_nt(c_low, router_ref[part, :])
        spread(place_ref, (jnp.transpose(turned) + extra).astype(BF16), out_refs, part)
        hidden = hidden_ref[:, part]
        rg_ref[:, part] = dot_nn(t_high, hidden) + dot_nn(t_low, hidden)
        return carry

    tiles(gate_ref.shape[0], body)


def first_kernel(x_refs, out_refs, gain_ref, router_ref, gate_in, up_in, down_in,
                 place_ref, pick_ref, hidden_ref, info_ref, a_ref, b_ref,
                 x_ref, x_sems, gate_ref, up_ref, down_ref, hidden_sems, hidden_sems_b, width_sems, width_sems_b,
                 rows_ref, turned_ref, active_ref):
    section = lax.axis_index("section")
    width = gain_ref.shape[1]
    gate_loads = Loads(gate_in, gate_ref, hidden_sems, 1)
    up_loads = Loads(up_in, up_ref, hidden_sems_b, 1)
    down_cols = Loads(down_in, down_ref, width_sems, 1)
    down_rows = Loads(down_in, down_ref, hidden_sems, 0)
    fetches = piece_copies(x_refs, x_ref, x_sems)
    for copy in fetches:
        copy.start()

    @pl.when(section == 0)
    def _():
        start_all(gate_loads, up_loads)
        start_all(down_cols)

    @pl.when(section != 0)
    def _():
        start_all(down_rows)

    for copy in fetches:
        copy.wait()
    me = lax.axis_index("expert").astype(F32)
    tail = x_ref[:, width:]
    place_rows(tail.astype(F32), me, place_ref, pick_ref)
    select(pick_ref, x_ref, rows_ref, turned_ref)
    info_ref[0] = signs_of(dot_nn(pick_ref[...], tail), me)

    @pl.when(section == 0)
    def _():
        gap = norm_and_gap(rows_ref, gain_ref, router_ref, info_ref[0], hidden_ref)
        info_ref[1] = jnp.broadcast_to(gap, info_ref.shape[1:])

        def body(i, part, carry):
            gate_loads.wait(i)
            up_loads.wait(i)
            gate_pre = dot_nn(hidden_ref[...], gate_ref[:, part])
            up_pre = dot_nn(hidden_ref[...], up_ref[:, part])
            a_ref[:, part] = gate_pre.astype(BF16)
            b_ref[:, part] = up_pre.astype(BF16)
            active_ref[:, part] = (gate_pre * jax.nn.sigmoid(gate_pre) * up_pre).astype(BF16)
            return carry

        tiles(gate_ref.shape[1], body)
        send_down(active_ref, down_ref, down_cols, jax.nn.sigmoid(gap), place_ref, out_refs)

    @pl.when(section != 0)
    def _():
        def body(i, part, carry):
            down_rows.wait(i)
            a_ref[:, part] = jnp.transpose(dot_nn(down_ref[part, :], turned_ref[...])).astype(BF16)
            return carry

        tiles(down_ref.shape[0], body)


def middle_kernel(x_refs, back_refs, gain_ref, router_ref, place_ref, pick_ref, info_ref, raw_ref,
                  gate_in, up_in, down_in,
                  active_ref, prob_ref, rg_ref,
                  x_ref, x_sems, gate_ref, up_ref, down_ref, hidden_sems, hidden_sems_b, width_sems, width_sems_b,
                  rows_ref, hidden_ref, d_gate_ref, d_up_ref, dprob_ref):
    @pl.when(lax.axis_index("section") == 1)
    def _():
        gate_loads = Loads(gate_in, gate_ref, hidden_sems, 1)
        up_loads = Loads(up_in, up_ref, hidden_sems_b, 1)
        fetches = piece_copies(x_refs, x_ref, x_sems)
        for copy in fetches:
            copy.start()
        start_all(gate_loads, up_loads)
        for copy in fetches:
            copy.wait()
        select(pick_ref, x_ref, rows_ref)
        signs = info_ref[0]
        gap = norm_and_gap(rows_ref, gain_ref, router_ref, signs, hidden_ref)
        prob = jax.nn.sigmoid(gap)
        prob_ref[...] = jnp.broadcast_to(prob, prob_ref.shape)
        dprob_ref[...] = jnp.zeros_like(dprob_ref)

        def body(i, part, carry):
            gate_loads.wait(i)
            up_loads.wait(i)
            gate_pre = dot_nn(hidden_ref[...], gate_ref[:, part])
            up_pre = dot_nn(hidden_ref[...], up_ref[:, part])
            grads_of(gate_pre, up_pre, raw_ref[:, part].astype(F32), prob, part, dprob_ref,
                     active_ref, d_gate_ref, d_up_ref)
            return carry

        tiles(gate_ref.shape[1], body)
        send_back(gate_ref, up_ref, None, None, d_gate_ref, d_up_ref, dprob_ref, gap, signs,
                  hidden_ref, router_ref, place_ref, back_refs, rg_ref)


def last_kernel(u_refs, out_refs, router_ref, place_ref, pick_ref, info_ref, hidden_ref, prob_ref,
                rg_in_ref, a_ref, b_ref, active_ref, gate_in, up_in, down_in,
                rg_ref,
                x_ref, x_sems, gate_ref, up_ref, down_ref, hidden_sems, hidden_sems_b, width_sems, width_sems_b,
                rows_ref, turned_ref, d_gate_ref, d_up_ref, dprob_ref):
    section = lax.axis_index("section")

    @pl.when(section == 0)
    def _():
        down_rows = Loads(down_in, down_ref, hidden_sems, 0)
        gate_loads = Loads(gate_in, gate_ref, width_sems, 0)
        up_loads = Loads(up_in, up_ref, width_sems_b, 0)
        fetches = piece_copies(u_refs, x_ref, x_sems)
        for copy in fetches:
            copy.start()
        start_all(down_rows)
        start_all(gate_loads, up_loads)
        for copy in fetches:
            copy.wait()
        select(pick_ref, x_ref, rows_ref, turned_ref)
        gap = pick_lane(info_ref[1], 0)
        prob = jax.nn.sigmoid(gap)
        dprob_ref[...] = jnp.zeros_like(dprob_ref)

        def body(i, part, carry):
            down_rows.wait(i)
            d_raw = jnp.transpose(dot_nn(down_ref[part, :], turned_ref[...]))
            grads_of(a_ref[:, part].astype(F32), b_ref[:, part].astype(F32), d_raw, prob, part,
                     dprob_ref, None, d_gate_ref, d_up_ref)
            return carry

        tiles(down_ref.shape[0], body)
        send_back(gate_ref, up_ref, gate_loads, up_loads, d_gate_ref, d_up_ref, dprob_ref, gap,
                  info_ref[0], hidden_ref, router_ref, place_ref, out_refs, rg_ref)

    @pl.when(section != 0)
    def _():
        down_cols = Loads(down_in, down_ref, width_sems, 1)
        start_all(down_cols)
        send_down(active_ref, down_ref, down_cols, pick_lane(prob_ref[...], 0), place_ref, out_refs)
        rg_ref[...] = rg_in_ref[...]


def with_pieces(body, count, inputs, groups, *refs):
    ins, rest = refs[:inputs], refs[inputs:]
    body(ins[:count], rest[:groups], *ins[count:], *rest[groups:])


def expert_call(body, pieces, small, weights, outs, scratch, flops):
    width, hidden_units = weights[0].shape
    shape = jax.ShapeDtypeStruct
    groups = lax.axis_size("dp")
    tokens = sum(p.shape[0] for p in pieces)
    outs = [shape((tokens // groups, width), BF16)] * groups + outs
    sems = lambda total: pltpu.SemaphoreType.DMA((max(1, total // 256),))
    scratch = [
        pltpu.VMEM((tokens, pieces[0].shape[1]), BF16), pltpu.SemaphoreType.DMA((len(pieces),)),
        *[pltpu.VMEM(w.shape, BF16) for w in weights],
        sems(hidden_units), sems(hidden_units), sems(width), sems(width),
    ] + scratch
    held = sum(w.size * w.dtype.itemsize for w in weights)
    block, outside = pl.BlockSpec(memory_space=pltpu.VMEM), pl.BlockSpec(memory_space=pl.ANY)
    in_specs = [outside] * len(pieces) + [block] * len(small) + [outside] * len(weights)
    results = pl.pallas_call(
        functools.partial(with_pieces, body, len(pieces), len(in_specs), groups),
        in_specs=in_specs,
        out_specs=[block] * len(outs),
        out_shape=outs,
        scratch_shapes=scratch,
        cost_estimate=pl.CostEstimate(flops=flops, bytes_accessed=held, transcendentals=0),
        compiler_params=pltpu.CompilerParams(
            vmem_limit_bytes=held + 6 * 2**20 + 4 * tokens * width * 2
        ),
    )(*pieces, *small, *weights)
    return results[:groups], *results[groups:]


def moved(block, axes, target):
    sizes = [lax.axis_size(a) for a in axes]
    spots = [()]
    for n in sizes:
        spots = [spot + (i,) for spot in spots for i in range(n)]
    number = {spot: i for i, spot in enumerate(spots)}
    pairs = [(number[spot], number[target(*spot)]) for spot in spots if target(*spot) in number]
    return lax.ppermute(block, axes, pairs)


def flips():
    bits = lax.axis_size("dp").bit_length() - 1
    return [1 << b for b in reversed(range(bits))]


def flipped(block, bit):
    return moved(block, ("dp",), lambda d: (d ^ bit,))


def gathered(block, distance):
    count = lax.axis_size("expert")
    if distance == 0:
        parts = [block] + [
            moved(block, ("expert",), lambda e, k=k: ((e + k) % count,)) for k in range(1, count)
        ]
    else:
        parts = [
            moved(block, ("section", "expert"), lambda s, e, k=k: (s + distance, (e + k) % count))
            for k in range(count)
        ]
    groups = [parts]
    for bit in flips():
        groups = groups + [[flipped(part, bit) for part in group] for group in groups]
    return [part for group in groups for part in group]


def combined(pieces):
    count = lax.axis_size("expert")
    own = pieces[0].shape[0] // count
    add = lambda kept, came: (kept.astype(F32) + came.astype(F32)).astype(BF16)
    cut = lambda group: [group[k * own:(k + 1) * own] for k in range(count)]
    order = list(reversed(flips()))
    half = len(pieces) // 2
    came = [flipped(group, order[0]) for group in pieces[half:]]
    groups = [
        [add(*pair) for pair in zip(cut(kept), cut(got))] for kept, got in zip(pieces[:half], came)
    ]
    for bit in order[1:]:
        groups = lax.optimization_barrier(groups)
        half = len(groups) // 2
        groups = [
            [add(kept, flipped(sent, bit)) for kept, sent in zip(*pair)]
            for pair in zip(groups[:half], groups[half:])
        ]
    parts = groups[0]
    total = parts[0].astype(F32)
    for k in range(1, count):
        total = total + moved(parts[k], ("expert",), lambda e, k=k: ((e - k) % count,)).astype(F32)
    return total


def summed(block):
    for bit in flips():
        block = block + flipped(block, bit)
    count = lax.axis_size("expert")
    for bit in [1 << b for b in range(count.bit_length() - 1)]:
        block = block + moved(block, ("expert",), lambda e, bit=bit: (e ^ bit,))
    return block


def sent_on(block, distance):
    return moved(block, ("section",), lambda s: (s + distance,))


def input_grad(layer_in, upstream, d_hidden, gain_row):
    values = layer_in.astype(F32)
    inv_rms = lax.rsqrt(jnp.mean(values * values, axis=-1, keepdims=True) + EPSILON)
    weighted = gain_row * d_hidden
    mean = jnp.mean(values * weighted, axis=-1, keepdims=True)
    cubed = inv_rms * inv_rms * inv_rms
    d_in = upstream.astype(F32) + inv_rms * weighted - values * cubed * mean
    return d_in.astype(BF16)


def per_device(inputs, cotangent, norm_gain, router, w_gate, w_up, w_down, routes):
    section = lax.axis_index("section")
    at_start = section == 0
    micro, toks, width = inputs.shape
    experts, top_k = router.shape[2], routes.shape[3]
    capacity = 3 * top_k * toks // (2 * experts)
    peers = lax.axis_size("expert") * lax.axis_size("dp")
    own = micro * toks
    tokens, rows = peers * own, peers * micro * capacity
    weights = (w_gate[0, 0], w_up[0, 0], w_down[0, 0])
    hidden_units = weights[0].shape[1]
    gain_row = norm_gain[0].astype(F32)
    router_w = jnp.pad(router[0], ((0, 0), (0, LANES - experts)))
    kept = -(-experts // 8) * 8
    shape = jax.ShapeDtypeStruct
    dot_flops = 2 * rows * width * hidden_units
    row_block, turned = pltpu.VMEM((rows, width), BF16), pltpu.VMEM((width, rows), BF16)
    d_block, lane_block = pltpu.VMEM((hidden_units, rows), BF16), pltpu.VMEM((rows, LANES), F32)

    mine = jnp.where(at_start, inputs, cotangent).reshape(own, width)
    tail = jnp.pad(routes[0].reshape(own, top_k).astype(BF16), ((0, 0), (0, LANES - top_k)))
    payload = jnp.concatenate([mine, tail], axis=1)
    out, place, pick, hidden, info, stash_a, stash_b = expert_call(
        first_kernel, gathered(payload, 0), [norm_gain, router_w], weights,
        [shape((tokens, rows), BF16), shape((rows, tokens), BF16),
         shape((rows, width), BF16), shape((2, rows, LANES), F32),
         shape((rows, hidden_units), BF16), shape((rows, hidden_units), BF16)],
        [row_block, turned, pltpu.VMEM((rows, hidden_units), BF16)],
        3 * dot_flops,
    )
    acts_start = (mine.astype(F32) + combined(out)).astype(BF16)

    back, active, prob, rg = expert_call(
        middle_kernel, gathered(acts_start, 1),
        [norm_gain, router_w, place, pick, info, stash_a], weights,
        [shape((rows, hidden_units), BF16), shape((rows, LANES), F32), shape((kept, width), F32)],
        [row_block, row_block, d_block, d_block, lane_block],
        4 * dot_flops,
    )
    arrived = sent_on(acts_start, 1)
    grads_end = input_grad(arrived, mine, combined(back), gain_row)

    out, rg = expert_call(
        last_kernel, gathered(grads_end, -1),
        [router_w, place, pick, info, hidden, prob, rg, stash_a, stash_b, active], weights,
        [shape((kept, width), F32)],
        [row_block, turned, d_block, d_block, lane_block],
        3 * dot_flops,
    )
    total = combined(out)
    upstream = sent_on(grads_end, -1)
    router_total = summed(rg)[:experts].T
    grads_start = input_grad(mine, upstream, total, gain_row)
    acts_end = (arrived.astype(F32) + total).astype(BF16)
    acts = jnp.where(at_start, acts_start, acts_end).reshape(1, micro, toks, width)
    grads = jnp.where(at_start, grads_start, grads_end).reshape(1, micro, toks, width)
    return acts, grads, router_total[None]


def solution(mesh):
    placed = (
        P(None, GROUP, None),
        P(None, GROUP, None),
        P("section", None),
        P("section", None, None),
        P("section", "expert", None, "dp"),
        P("section", "expert", None, "dp"),
        P("section", "expert", "dp", None),
        P("section", None, GROUP, None),
    )
    return jax.shard_map(
        per_device,
        mesh=mesh,
        in_specs=placed,
        out_specs=(
            P("section", None, GROUP, None),
            P("section", None, GROUP, None),
            P("section", None, None),
        ),
        check_vma=False,
    )
```

```python
import functools

import jax
import jax.numpy as jnp
from jax import lax
from jax.experimental import pallas as pl
from jax.experimental.pallas import tpu as pltpu
from jax.sharding import PartitionSpec as P

EPSILON = 1e-05
LANES = 128
GROUP = ("expert", "dp")
F32 = jnp.float32
BF16 = jnp.bfloat16


def dot_nn(a, b):
    return jnp.dot(a, b, preferred_element_type=F32)


def dot_nt(a, b):
    return lax.dot_general(a, b, (((1,), (1,)), ((), ())), preferred_element_type=F32)


def lanes_like(rows):
    return lax.broadcasted_iota(jnp.int32, (rows, LANES), 1)


def pick_lane(block, lane):
    return jnp.sum(jnp.where(lanes_like(block.shape[0]) == lane, block, 0.0), axis=1, keepdims=True)


def hi_lo(block):
    high = block.astype(BF16)
    return high, (block - high.astype(F32)).astype(BF16)


def place_rows(tail, me, place_ref, pick_ref):
    tokens, rows = place_ref.shape
    wide = -(-rows // LANES) * LANES
    first, second = pick_lane(tail, 0), pick_lane(tail, 1)
    mine = jnp.broadcast_to(((first == me) | (second == me)).astype(F32), (tokens, wide))
    row = lax.broadcasted_iota(jnp.int32, (tokens, tokens), 0)
    col = lax.broadcasted_iota(jnp.int32, (tokens, tokens), 1)
    earlier = dot_nn((col < row).astype(F32).astype(BF16), mine.astype(BF16))
    slot = lax.broadcasted_iota(jnp.int32, (tokens, wide), 1).astype(F32)
    place = jnp.where((earlier == slot) & (mine > 0.5), 1.0, 0.0)
    place_ref[...] = place[:, :rows].astype(BF16)
    pick_ref[...] = jnp.transpose(place)[:rows].astype(BF16)


def signs_of(tail, me):
    first, second = pick_lane(tail, 0), pick_lane(tail, 1)
    other = first + second - me
    lane = lanes_like(tail.shape[0]).astype(F32)
    both = (lane == me).astype(F32) - (lane == other).astype(F32)
    return jnp.where(first != second, both, 0.0)


def norm_and_gap(rows_ref, gain_ref, router_ref, signs, hidden_ref):
    rows, width = rows_ref.shape

    def square(i, part, total):
        values = rows_ref[:, part].astype(F32)
        return total + jnp.sum(values * values, axis=1, keepdims=True)

    squares = tiles(width, square, jnp.zeros((rows, 1), F32))
    inv_rms = lax.rsqrt(squares / width + EPSILON)

    def scale(i, part, total):
        hidden = (rows_ref[:, part].astype(F32) * inv_rms * gain_ref[:, part].astype(F32)).astype(BF16)
        hidden_ref[:, part] = hidden
        return total + dot_nn(hidden, router_ref[part, :])

    logits = tiles(width, scale, jnp.zeros((rows, LANES), F32))
    return jnp.sum(logits * signs, axis=1, keepdims=True)


def tile_of(total, most=1024):
    return next(c for c in (1024, 512, 256, 128) if c <= most and total % c == 0)


def tiles(total, body, carry=0, most=1024):
    step = tile_of(total, most)

    def one(i, carry):
        return body(i, pl.ds(pl.multiple_of(i * step, step), step), carry)

    return lax.fori_loop(0, total // step, one, carry)


class Loads:
    def __init__(self, source, target, sems, axis):
        self.source, self.target, self.sems, self.axis = source, target, sems, axis
        self.count, self.total = sems.shape[0], target.shape[axis]

    def copy(self, i):
        step = self.total // self.count
        part = pl.ds(pl.multiple_of(i * step, step), step)
        spot = (slice(None), part) if self.axis else (part,)
        return pltpu.make_async_copy(self.source.at[spot], self.target.at[spot], self.sems.at[i])

    def wait(self, i):
        self.copy(i).wait()


def start_all(*loads):
    def one(i, carry):
        for load in loads:
            load.copy(i).start()
        return carry

    lax.fori_loop(0, loads[0].count, one, 0)


def select(pick_ref, x_ref, rows_ref):
    def body(i, part, carry):
        rows_ref[:, part] = dot_nn(pick_ref[...], x_ref[:, part]).astype(BF16)
        return carry

    tiles(rows_ref.shape[1], body)


def piece_copies(x_refs, x_ref, sems):
    start, copies = 0, []
    for i, ref in enumerate(x_refs):
        copies.append(pltpu.make_async_copy(ref, x_ref.at[pl.ds(start, ref.shape[0])], sems.at[i]))
        start += ref.shape[0]
    return copies


def fetch(x_refs, x_ref, sems):
    copies = piece_copies(x_refs, x_ref, sems)
    for copy in copies:
        copy.start()
    for copy in copies:
        copy.wait()


def spread(place_ref, rows, out_refs, part):
    piece = out_refs[0].shape[0]
    block = dot_nn(place_ref[...], rows).astype(BF16)
    for i, out_ref in enumerate(out_refs):
        out_ref[:, part] = block[i * piece:(i + 1) * piece]


def send_down(active_ref, down_ref, down_loads, prob, place_ref, out_refs):
    def body(i, part, carry):
        down_loads.wait(i)
        rows = dot_nn(active_ref[...], down_ref[:, part]) * prob
        spread(place_ref, rows.astype(BF16), out_refs, part)
        return carry

    tiles(down_ref.shape[1], body)


def grads_of(gate_pre, up_pre, d_raw, prob, part, dprob_ref, active_ref, d_gate_ref, d_up_ref):
    gate_sig = jax.nn.sigmoid(gate_pre)
    act = gate_pre * gate_sig
    active = (act * up_pre).astype(BF16)
    if active_ref is not None:
        active_ref[:, part] = active
    gain = jnp.sum(active.astype(F32) * d_raw, axis=1, keepdims=True)
    dprob_ref[...] += jnp.broadcast_to(gain, dprob_ref.shape)
    d_active = d_raw * prob
    d_gate = d_active * up_pre * gate_sig * (1.0 + gate_pre * (1.0 - gate_sig))
    d_gate_ref[:, part] = d_gate.astype(BF16)
    d_up_ref[:, part] = (d_active * act).astype(BF16)


def send_back(gate_ref, up_ref, gate_loads, up_loads, d_gate_ref, d_up_ref, dprob_ref, gap, signs,
              hidden_ref, router_ref, place_ref, out_refs, rg_ref):
    c = jax.nn.sigmoid(gap) * jax.nn.sigmoid(-gap) * dprob_ref[...] * signs
    c_high, c_low = hi_lo(c)
    t_high, t_low = hi_lo(jnp.transpose(c)[:rg_ref.shape[0]])

    def body(i, part, carry):
        if gate_loads is not None:
            gate_loads.wait(i)
            up_loads.wait(i)
        back = dot_nt(d_gate_ref[...], gate_ref[part, :]) + dot_nt(d_up_ref[...], up_ref[part, :])
        extra = dot_nt(c_high, router_ref[part, :]) + dot_nt(c_low, router_ref[part, :])
        spread(place_ref, (back + extra).astype(BF16), out_refs, part)
        hidden = hidden_ref[:, part]
        rg_ref[:, part] = dot_nn(t_high, hidden) + dot_nn(t_low, hidden)
        return carry

    tiles(gate_ref.shape[0], body)


def first_kernel(x_refs, out_refs, gain_ref, router_ref, gate_in, up_in, down_in,
                 place_ref, pick_ref, hidden_ref, info_ref, a_ref, b_ref,
                 x_ref, x_sems, gate_ref, up_ref, down_ref, gate_sems, up_sems, rows_sems, cols_sems,
                 rows_ref, active_ref):
    section = lax.axis_index("section")
    width = gain_ref.shape[1]
    gate_loads = Loads(gate_in, gate_ref, gate_sems, 1)
    up_loads = Loads(up_in, up_ref, up_sems, 1)
    down_cols = Loads(down_in, down_ref, cols_sems, 1)
    down_rows = Loads(down_in, down_ref, rows_sems, 0)
    fetches = piece_copies(x_refs, x_ref, x_sems)
    for copy in fetches:
        copy.start()

    @pl.when(section == 0)
    def _():
        start_all(gate_loads, up_loads)
        start_all(down_cols)

    @pl.when(section != 0)
    def _():
        start_all(down_rows)

    for copy in fetches:
        copy.wait()
    me = lax.axis_index("expert").astype(F32)
    tail = x_ref[:, width:]
    place_rows(tail.astype(F32), me, place_ref, pick_ref)
    select(pick_ref, x_ref, rows_ref)
    info_ref[0] = signs_of(dot_nn(pick_ref[...], tail), me)

    @pl.when(section == 0)
    def _():
        gap = norm_and_gap(rows_ref, gain_ref, router_ref, info_ref[0], hidden_ref)
        info_ref[1] = jnp.broadcast_to(gap, info_ref.shape[1:])

        def body(i, part, carry):
            gate_loads.wait(i)
            up_loads.wait(i)
            gate_pre = dot_nn(hidden_ref[...], gate_ref[:, part])
            up_pre = dot_nn(hidden_ref[...], up_ref[:, part])
            a_ref[:, part] = gate_pre.astype(BF16)
            b_ref[:, part] = up_pre.astype(BF16)
            active_ref[:, part] = (gate_pre * jax.nn.sigmoid(gate_pre) * up_pre).astype(BF16)
            return carry

        tiles(gate_ref.shape[1], body, most=512)
        send_down(active_ref, down_ref, down_cols, jax.nn.sigmoid(gap), place_ref, out_refs)

    @pl.when(section != 0)
    def _():
        def body(i, part, carry):
            down_rows.wait(i)
            a_ref[:, part] = dot_nt(rows_ref[...], down_ref[part, :]).astype(BF16)
            return carry

        tiles(down_ref.shape[0], body)


def middle_kernel(x_refs, back_refs, gain_ref, router_ref, place_ref, pick_ref, info_ref, raw_ref,
                  gate_in, up_in, down_in,
                  active_ref, prob_ref, rg_ref,
                  x_ref, x_sems, gate_ref, up_ref, down_ref, gate_sems, up_sems, rows_sems, cols_sems,
                  rows_ref, hidden_ref, d_gate_ref, d_up_ref, dprob_ref):
    @pl.when(lax.axis_index("section") == 1)
    def _():
        gate_loads = Loads(gate_in, gate_ref, gate_sems, 1)
        up_loads = Loads(up_in, up_ref, up_sems, 1)
        fetches = piece_copies(x_refs, x_ref, x_sems)
        for copy in fetches:
            copy.start()
        start_all(gate_loads, up_loads)
        for copy in fetches:
            copy.wait()
        select(pick_ref, x_ref, rows_ref)
        signs = info_ref[0]
        gap = norm_and_gap(rows_ref, gain_ref, router_ref, signs, hidden_ref)
        prob = jax.nn.sigmoid(gap)
        prob_ref[...] = jnp.broadcast_to(prob, prob_ref.shape)
        dprob_ref[...] = jnp.zeros_like(dprob_ref)

        def body(i, part, carry):
            gate_loads.wait(i)
            up_loads.wait(i)
            gate_pre = dot_nn(hidden_ref[...], gate_ref[:, part])
            up_pre = dot_nn(hidden_ref[...], up_ref[:, part])
            grads_of(gate_pre, up_pre, raw_ref[:, part].astype(F32), prob, part, dprob_ref,
                     active_ref, d_gate_ref, d_up_ref)
            return carry

        tiles(gate_ref.shape[1], body, most=512)
        send_back(gate_ref, up_ref, None, None, d_gate_ref, d_up_ref, dprob_ref, gap, signs,
                  hidden_ref, router_ref, place_ref, back_refs, rg_ref)


def last_kernel(u_refs, out_refs, router_ref, place_ref, pick_ref, info_ref, hidden_ref, prob_ref,
                rg_in_ref, a_ref, b_ref, active_ref, gate_in, up_in, down_in,
                rg_ref,
                x_ref, x_sems, gate_ref, up_ref, down_ref, gate_sems, up_sems, rows_sems, cols_sems,
                rows_ref, d_gate_ref, d_up_ref, dprob_ref):
    section = lax.axis_index("section")

    @pl.when(section == 0)
    def _():
        down_rows = Loads(down_in, down_ref, rows_sems, 0)
        gate_loads = Loads(gate_in, gate_ref, gate_sems, 0)
        up_loads = Loads(up_in, up_ref, up_sems, 0)
        fetches = piece_copies(u_refs, x_ref, x_sems)
        for copy in fetches:
            copy.start()
        start_all(down_rows)
        start_all(gate_loads, up_loads)
        for copy in fetches:
            copy.wait()
        select(pick_ref, x_ref, rows_ref)
        gap = pick_lane(info_ref[1], 0)
        prob = jax.nn.sigmoid(gap)
        dprob_ref[...] = jnp.zeros_like(dprob_ref)

        def body(i, part, carry):
            down_rows.wait(i)
            d_raw = dot_nt(rows_ref[...], down_ref[part, :])
            grads_of(a_ref[:, part].astype(F32), b_ref[:, part].astype(F32), d_raw, prob, part,
                     dprob_ref, None, d_gate_ref, d_up_ref)
            return carry

        tiles(down_ref.shape[0], body)
        send_back(gate_ref, up_ref, gate_loads, up_loads, d_gate_ref, d_up_ref, dprob_ref, gap,
                  info_ref[0], hidden_ref, router_ref, place_ref, out_refs, rg_ref)

    @pl.when(section != 0)
    def _():
        down_cols = Loads(down_in, down_ref, cols_sems, 1)
        start_all(down_cols)
        send_down(active_ref, down_ref, down_cols, pick_lane(prob_ref[...], 0), place_ref, out_refs)
        rg_ref[...] = rg_in_ref[...]


def with_pieces(body, count, inputs, groups, *refs):
    ins, rest = refs[:inputs], refs[inputs:]
    body(ins[:count], rest[:groups], *ins[count:], *rest[groups:])


def expert_call(body, pieces, small, weights, outs, scratch, flops, by_rows=False):
    width, hidden_units = weights[0].shape
    shape = jax.ShapeDtypeStruct
    groups = lax.axis_size("dp")
    tokens = sum(p.shape[0] for p in pieces)
    outs = [shape((tokens // groups, width), BF16)] * groups + outs
    sems = lambda total, most: pltpu.SemaphoreType.DMA((total // tile_of(total, most),))
    pair = sems(width, 1024) if by_rows else sems(hidden_units, 512)
    scratch = [
        pltpu.VMEM((tokens, pieces[0].shape[1]), BF16), pltpu.SemaphoreType.DMA((len(pieces),)),
        *[pltpu.VMEM(w.shape, BF16) for w in weights],
        pair, pair, sems(hidden_units, 1024), sems(width, 1024),
    ] + scratch
    held = sum(w.size * w.dtype.itemsize for w in weights)
    block, outside = pl.BlockSpec(memory_space=pltpu.VMEM), pl.BlockSpec(memory_space=pl.ANY)
    in_specs = [outside] * len(pieces) + [block] * len(small) + [outside] * len(weights)
    results = pl.pallas_call(
        functools.partial(with_pieces, body, len(pieces), len(in_specs), groups),
        in_specs=in_specs,
        out_specs=[block] * len(outs),
        out_shape=outs,
        scratch_shapes=scratch,
        cost_estimate=pl.CostEstimate(flops=flops, bytes_accessed=held, transcendentals=0),
        compiler_params=pltpu.CompilerParams(
            vmem_limit_bytes=held + 6 * 2**20 + 4 * tokens * width * 2
        ),
    )(*pieces, *small, *weights)
    return results[:groups], *results[groups:]


def moved(block, axes, target):
    sizes = [lax.axis_size(a) for a in axes]
    spots = [()]
    for n in sizes:
        spots = [spot + (i,) for spot in spots for i in range(n)]
    number = {spot: i for i, spot in enumerate(spots)}
    pairs = [(number[spot], number[target(*spot)]) for spot in spots if target(*spot) in number]
    return lax.ppermute(block, axes, pairs)


def flips():
    bits = lax.axis_size("dp").bit_length() - 1
    return [1 << b for b in reversed(range(bits))]


def flipped(block, bit):
    return moved(block, ("dp",), lambda d: (d ^ bit,))


def gathered(block, distance):
    count = lax.axis_size("expert")
    if distance == 0:
        parts = [block] + [
            moved(block, ("expert",), lambda e, k=k: ((e + k) % count,)) for k in range(1, count)
        ]
    else:
        parts = [
            moved(block, ("section", "expert"), lambda s, e, k=k: (s + distance, (e + k) % count))
            for k in range(count)
        ]
    groups = [parts]
    for bit in flips():
        groups = groups + [[flipped(part, bit) for part in group] for group in groups]
    return [part for group in groups for part in group]


def combined(pieces):
    count = lax.axis_size("expert")
    own = pieces[0].shape[0] // count
    add = lambda kept, came: (kept.astype(F32) + came.astype(F32)).astype(BF16)
    cut = lambda group: [group[k * own:(k + 1) * own] for k in range(count)]
    order = list(reversed(flips()))
    half = len(pieces) // 2
    came = [flipped(group, order[0]) for group in pieces[half:]]
    groups = [
        [add(*pair) for pair in zip(cut(kept), cut(got))] for kept, got in zip(pieces[:half], came)
    ]
    for bit in order[1:]:
        groups = lax.optimization_barrier(groups)
        half = len(groups) // 2
        groups = [
            [add(kept, flipped(sent, bit)) for kept, sent in zip(*pair)]
            for pair in zip(groups[:half], groups[half:])
        ]
    parts = groups[0]
    total = parts[0].astype(F32)
    for k in range(1, count):
        total = total + moved(parts[k], ("expert",), lambda e, k=k: ((e - k) % count,)).astype(F32)
    return total


def summed(block):
    for bit in flips():
        block = block + flipped(block, bit)
    count = lax.axis_size("expert")
    for bit in [1 << b for b in range(count.bit_length() - 1)]:
        block = block + moved(block, ("expert",), lambda e, bit=bit: (e ^ bit,))
    return block


def sent_on(block, distance):
    return moved(block, ("section",), lambda s: (s + distance,))


def input_grad(layer_in, upstream, d_hidden, gain_row):
    values = layer_in.astype(F32)
    inv_rms = lax.rsqrt(jnp.mean(values * values, axis=-1, keepdims=True) + EPSILON)
    weighted = gain_row * d_hidden
    mean = jnp.mean(values * weighted, axis=-1, keepdims=True)
    cubed = inv_rms * inv_rms * inv_rms
    d_in = upstream.astype(F32) + inv_rms * weighted - values * cubed * mean
    return d_in.astype(BF16)


def per_device(inputs, cotangent, norm_gain, router, w_gate, w_up, w_down, routes):
    section = lax.axis_index("section")
    at_start = section == 0
    micro, toks, width = inputs.shape
    experts, top_k = router.shape[2], routes.shape[3]
    capacity = 3 * top_k * toks // (2 * experts)
    peers = lax.axis_size("expert") * lax.axis_size("dp")
    own = micro * toks
    tokens, rows = peers * own, peers * micro * capacity
    weights = (w_gate[0, 0], w_up[0, 0], w_down[0, 0])
    hidden_units = weights[0].shape[1]
    gain_row = norm_gain[0].astype(F32)
    router_w = jnp.pad(router[0], ((0, 0), (0, LANES - experts)))
    kept = -(-experts // 8) * 8
    shape = jax.ShapeDtypeStruct
    dot_flops = 2 * rows * width * hidden_units
    row_block, lane_block = pltpu.VMEM((rows, width), BF16), pltpu.VMEM((rows, LANES), F32)
    d_block = pltpu.VMEM((rows, hidden_units), BF16)

    mine = jnp.where(at_start, inputs, cotangent).reshape(own, width)
    tail = jnp.pad(routes[0].reshape(own, top_k).astype(BF16), ((0, 0), (0, LANES - top_k)))
    payload = jnp.concatenate([mine, tail], axis=1)
    out, place, pick, hidden, info, stash_a, stash_b = expert_call(
        first_kernel, gathered(payload, 0), [norm_gain, router_w], weights,
        [shape((tokens, rows), BF16), shape((rows, tokens), BF16),
         shape((rows, width), BF16), shape((2, rows, LANES), F32),
         shape((rows, hidden_units), BF16), shape((rows, hidden_units), BF16)],
        [row_block, d_block],
        3 * dot_flops,
    )
    acts_start = (mine.astype(F32) + combined(out)).astype(BF16)

    back, active, prob, rg = expert_call(
        middle_kernel, gathered(acts_start, 1),
        [norm_gain, router_w, place, pick, info, stash_a], weights,
        [shape((rows, hidden_units), BF16), shape((rows, LANES), F32), shape((kept, width), F32)],
        [row_block, row_block, d_block, d_block, lane_block],
        4 * dot_flops,
    )
    arrived = sent_on(acts_start, 1)
    grads_end = input_grad(arrived, mine, combined(back), gain_row)

    out, rg = expert_call(
        last_kernel, gathered(grads_end, -1),
        [router_w, place, pick, info, hidden, prob, rg, stash_a, stash_b, active], weights,
        [shape((kept, width), F32)],
        [row_block, d_block, d_block, lane_block],
        3 * dot_flops, by_rows=True,
    )
    total = combined(out)
    upstream = sent_on(grads_end, -1)
    router_total = summed(rg)[:experts].T
    grads_start = input_grad(mine, upstream, total, gain_row)
    acts_end = (arrived.astype(F32) + total).astype(BF16)
    acts = jnp.where(at_start, acts_start, acts_end).reshape(1, micro, toks, width)
    grads = jnp.where(at_start, grads_start, grads_end).reshape(1, micro, toks, width)
    return acts, grads, router_total[None]


def solution(mesh):
    placed = (
        P(None, GROUP, None),
        P(None, GROUP, None),
        P("section", None),
        P("section", None, None),
        P("section", "expert", None, "dp"),
        P("section", "expert", None, "dp"),
        P("section", "expert", "dp", None),
        P("section", None, GROUP, None),
    )
    return jax.shard_map(
        per_device,
        mesh=mesh,
        in_specs=placed,
        out_specs=(
            P("section", None, GROUP, None),
            P("section", None, GROUP, None),
            P("section", None, None),
        ),
        check_vma=False,
    )
```

```python
import functools

import jax
import jax.numpy as jnp
from jax import lax
from jax.experimental import pallas as pl
from jax.experimental.pallas import tpu as pltpu
from jax.sharding import PartitionSpec as P

EPSILON = 1e-05
LANES = 128
GROUP = ("expert", "dp")
F32 = jnp.float32
BF16 = jnp.bfloat16


def dot_nn(a, b):
    return jnp.dot(a, b, preferred_element_type=F32)


def dot_nt(a, b):
    return lax.dot_general(a, b, (((1,), (1,)), ((), ())), preferred_element_type=F32)


def lanes_like(rows):
    return lax.broadcasted_iota(jnp.int32, (rows, LANES), 1)


def pick_lane(block, lane):
    return jnp.sum(jnp.where(lanes_like(block.shape[0]) == lane, block, 0.0), axis=1, keepdims=True)


def hi_lo(block):
    high = block.astype(BF16)
    return high, (block - high.astype(F32)).astype(BF16)


def place_rows(tail, me, place_ref, pick_ref):
    tokens, rows = place_ref.shape
    wide = -(-rows // LANES) * LANES
    first, second = pick_lane(tail, 0), pick_lane(tail, 1)
    mine = jnp.broadcast_to(((first == me) | (second == me)).astype(F32), (tokens, wide))
    row = lax.broadcasted_iota(jnp.int32, (tokens, tokens), 0)
    col = lax.broadcasted_iota(jnp.int32, (tokens, tokens), 1)
    earlier = dot_nn((col < row).astype(F32).astype(BF16), mine.astype(BF16))
    slot = lax.broadcasted_iota(jnp.int32, (tokens, wide), 1).astype(F32)
    place = jnp.where((earlier == slot) & (mine > 0.5), 1.0, 0.0)
    place_ref[...] = place[:, :rows].astype(BF16)
    pick_ref[...] = jnp.transpose(place)[:rows].astype(BF16)


def signs_of(tail, me):
    first, second = pick_lane(tail, 0), pick_lane(tail, 1)
    other = first + second - me
    lane = lanes_like(tail.shape[0]).astype(F32)
    both = (lane == me).astype(F32) - (lane == other).astype(F32)
    return jnp.where(first != second, both, 0.0)


def norm_and_gap(rows_ref, gain_ref, router_ref, signs, hidden_ref):
    rows, width = rows_ref.shape

    def square(i, part, total):
        values = rows_ref[:, part].astype(F32)
        return total + jnp.sum(values * values, axis=1, keepdims=True)

    squares = tiles(width, square, jnp.zeros((rows, 1), F32))
    inv_rms = lax.rsqrt(squares / width + EPSILON)

    def scale(i, part, total):
        hidden = (rows_ref[:, part].astype(F32) * inv_rms * gain_ref[:, part].astype(F32)).astype(BF16)
        hidden_ref[:, part] = hidden
        return total + dot_nt(hidden, router_ref[:, part])

    logits = tiles(width, scale, jnp.zeros((rows, LANES), F32))
    return jnp.sum(logits * signs, axis=1, keepdims=True)


def tile_of(total, most=1024):
    return next(c for c in (1024, 512, 256, 128) if c <= most and total % c == 0)


def tiles(total, body, carry=0, most=1024):
    step = tile_of(total, most)

    def one(i, carry):
        return body(i, pl.ds(pl.multiple_of(i * step, step), step), carry)

    return lax.fori_loop(0, total // step, one, carry)


class Loads:
    def __init__(self, source, target, sems, axis):
        self.source, self.target, self.sems, self.axis = source, target, sems, axis
        self.count, self.total = sems.shape[0], target.shape[axis]

    def copy(self, i):
        step = self.total // self.count
        part = pl.ds(pl.multiple_of(i * step, step), step)
        spot = (slice(None), part) if self.axis else (part,)
        return pltpu.make_async_copy(self.source.at[spot], self.target.at[spot], self.sems.at[i])

    def wait(self, i):
        self.copy(i).wait()


def start_all(*loads):
    def one(i, carry):
        for load in loads:
            load.copy(i).start()
        return carry

    lax.fori_loop(0, loads[0].count, one, 0)


def select(pick_ref, x_ref, rows_ref):
    def body(i, part, carry):
        rows_ref[:, part] = dot_nn(pick_ref[...], x_ref[:, part]).astype(BF16)
        return carry

    tiles(rows_ref.shape[1], body)


def piece_copies(x_refs, x_ref, sems):
    start, copies = 0, []
    for i, ref in enumerate(x_refs):
        copies.append(pltpu.make_async_copy(ref, x_ref.at[pl.ds(start, ref.shape[0])], sems.at[i]))
        start += ref.shape[0]
    return copies


def fetch(x_refs, x_ref, sems):
    copies = piece_copies(x_refs, x_ref, sems)
    for copy in copies:
        copy.start()
    for copy in copies:
        copy.wait()


def spread(place_ref, rows, out_refs, part):
    piece = out_refs[0].shape[0]
    block = dot_nn(place_ref[...], rows).astype(BF16)
    for i, out_ref in enumerate(out_refs):
        out_ref[:, part] = block[i * piece:(i + 1) * piece]


def send_down(active_ref, down_ref, down_loads, prob, place_ref, out_refs):
    def body(i, part, carry):
        down_loads.wait(i)
        rows = dot_nn(active_ref[...], down_ref[:, part]) * prob
        spread(place_ref, rows.astype(BF16), out_refs, part)
        return carry

    tiles(down_ref.shape[1], body)


def grads_of(gate_pre, up_pre, d_raw, prob, part, dprob_ref, active_ref, d_gate_ref, d_up_ref):
    gate_sig = jax.nn.sigmoid(gate_pre)
    act = gate_pre * gate_sig
    active = (act * up_pre).astype(BF16)
    if active_ref is not None:
        active_ref[:, part] = active
    gain = jnp.sum(active.astype(F32) * d_raw, axis=1, keepdims=True)
    dprob_ref[...] += jnp.broadcast_to(gain, dprob_ref.shape)
    d_active = d_raw * prob
    d_gate = d_active * up_pre * gate_sig * (1.0 + gate_pre * (1.0 - gate_sig))
    d_gate_ref[:, part] = d_gate.astype(BF16)
    d_up_ref[:, part] = (d_active * act).astype(BF16)


def send_back(gate_ref, up_ref, gate_loads, up_loads, d_gate_ref, d_up_ref, dprob_ref, gap, signs,
              hidden_ref, router_ref, place_ref, out_refs, rg_ref):
    c = jax.nn.sigmoid(gap) * jax.nn.sigmoid(-gap) * dprob_ref[...] * signs
    c_high, c_low = hi_lo(c)
    t_high, t_low = hi_lo(jnp.transpose(c)[:rg_ref.shape[0]])

    def body(i, part, carry):
        if gate_loads is not None:
            gate_loads.wait(i)
            up_loads.wait(i)
        back = dot_nt(d_gate_ref[...], gate_ref[part, :]) + dot_nt(d_up_ref[...], up_ref[part, :])
        extra = dot_nn(c_high, router_ref[:, part]) + dot_nn(c_low, router_ref[:, part])
        spread(place_ref, (back + extra).astype(BF16), out_refs, part)
        hidden = hidden_ref[:, part]
        rg_ref[:, part] = dot_nn(t_high, hidden) + dot_nn(t_low, hidden)
        return carry

    tiles(gate_ref.shape[0], body)


def first_kernel(x_refs, out_refs, gain_ref, router_ref, gate_in, up_in, down_in,
                 place_ref, pick_ref, hidden_ref, info_ref, a_ref, b_ref,
                 x_ref, x_sems, gate_ref, up_ref, down_ref, gate_sems, up_sems, rows_sems, cols_sems,
                 rows_ref, active_ref):
    section = lax.axis_index("section")
    width = gain_ref.shape[1]
    gate_loads = Loads(gate_in, gate_ref, gate_sems, 1)
    up_loads = Loads(up_in, up_ref, up_sems, 1)
    down_cols = Loads(down_in, down_ref, cols_sems, 1)
    down_rows = Loads(down_in, down_ref, rows_sems, 0)
    fetches = piece_copies(x_refs, x_ref, x_sems)
    for copy in fetches:
        copy.start()

    @pl.when(section == 0)
    def _():
        start_all(gate_loads, up_loads)
        start_all(down_cols)

    @pl.when(section != 0)
    def _():
        start_all(down_rows)

    for copy in fetches:
        copy.wait()
    me = lax.axis_index("expert").astype(F32)
    tail = x_ref[:, width:]
    place_rows(tail.astype(F32), me, place_ref, pick_ref)
    select(pick_ref, x_ref, rows_ref)
    info_ref[0] = signs_of(dot_nn(pick_ref[...], tail), me)

    @pl.when(section == 0)
    def _():
        gap = norm_and_gap(rows_ref, gain_ref, router_ref, info_ref[0], hidden_ref)
        info_ref[1] = jnp.broadcast_to(gap, info_ref.shape[1:])

        def body(i, part, carry):
            gate_loads.wait(i)
            up_loads.wait(i)
            gate_pre = dot_nn(hidden_ref[...], gate_ref[:, part])
            up_pre = dot_nn(hidden_ref[...], up_ref[:, part])
            a_ref[:, part] = gate_pre.astype(BF16)
            b_ref[:, part] = up_pre.astype(BF16)
            active_ref[:, part] = (gate_pre * jax.nn.sigmoid(gate_pre) * up_pre).astype(BF16)
            return carry

        tiles(gate_ref.shape[1], body, most=512)
        send_down(active_ref, down_ref, down_cols, jax.nn.sigmoid(gap), place_ref, out_refs)

    @pl.when(section != 0)
    def _():
        def body(i, part, carry):
            down_rows.wait(i)
            a_ref[:, part] = dot_nt(rows_ref[...], down_ref[part, :]).astype(BF16)
            return carry

        tiles(down_ref.shape[0], body)


def middle_kernel(x_refs, back_refs, gain_ref, router_ref, place_ref, pick_ref, info_ref, raw_ref,
                  gate_in, up_in, down_in,
                  active_ref, prob_ref, rg_ref,
                  x_ref, x_sems, gate_ref, up_ref, down_ref, gate_sems, up_sems, rows_sems, cols_sems,
                  rows_ref, hidden_ref, d_gate_ref, d_up_ref, dprob_ref):
    @pl.when(lax.axis_index("section") == 1)
    def _():
        gate_loads = Loads(gate_in, gate_ref, gate_sems, 1)
        up_loads = Loads(up_in, up_ref, up_sems, 1)
        fetches = piece_copies(x_refs, x_ref, x_sems)
        for copy in fetches:
            copy.start()
        start_all(gate_loads, up_loads)
        for copy in fetches:
            copy.wait()
        select(pick_ref, x_ref, rows_ref)
        signs = info_ref[0]
        gap = norm_and_gap(rows_ref, gain_ref, router_ref, signs, hidden_ref)
        prob = jax.nn.sigmoid(gap)
        prob_ref[...] = jnp.broadcast_to(prob, prob_ref.shape)
        dprob_ref[...] = jnp.zeros_like(dprob_ref)

        def body(i, part, carry):
            gate_loads.wait(i)
            up_loads.wait(i)
            gate_pre = dot_nn(hidden_ref[...], gate_ref[:, part])
            up_pre = dot_nn(hidden_ref[...], up_ref[:, part])
            grads_of(gate_pre, up_pre, raw_ref[:, part].astype(F32), prob, part, dprob_ref,
                     active_ref, d_gate_ref, d_up_ref)
            return carry

        tiles(gate_ref.shape[1], body, most=512)
        send_back(gate_ref, up_ref, None, None, d_gate_ref, d_up_ref, dprob_ref, gap, signs,
                  hidden_ref, router_ref, place_ref, back_refs, rg_ref)


def last_kernel(u_refs, out_refs, router_ref, place_ref, pick_ref, info_ref, hidden_ref, prob_ref,
                rg_in_ref, a_ref, b_ref, active_ref, gate_in, up_in, down_in,
                rg_ref,
                x_ref, x_sems, gate_ref, up_ref, down_ref, gate_sems, up_sems, rows_sems, cols_sems,
                rows_ref, d_gate_ref, d_up_ref, dprob_ref):
    section = lax.axis_index("section")

    @pl.when(section == 0)
    def _():
        down_rows = Loads(down_in, down_ref, rows_sems, 0)
        gate_loads = Loads(gate_in, gate_ref, gate_sems, 0)
        up_loads = Loads(up_in, up_ref, up_sems, 0)
        fetches = piece_copies(u_refs, x_ref, x_sems)
        for copy in fetches:
            copy.start()
        start_all(down_rows)
        start_all(gate_loads, up_loads)
        for copy in fetches:
            copy.wait()
        select(pick_ref, x_ref, rows_ref)
        gap = pick_lane(info_ref[1], 0)
        prob = jax.nn.sigmoid(gap)
        dprob_ref[...] = jnp.zeros_like(dprob_ref)

        def body(i, part, carry):
            down_rows.wait(i)
            d_raw = dot_nt(rows_ref[...], down_ref[part, :])
            grads_of(a_ref[:, part].astype(F32), b_ref[:, part].astype(F32), d_raw, prob, part,
                     dprob_ref, None, d_gate_ref, d_up_ref)
            return carry

        tiles(down_ref.shape[0], body)
        send_back(gate_ref, up_ref, gate_loads, up_loads, d_gate_ref, d_up_ref, dprob_ref, gap,
                  info_ref[0], hidden_ref, router_ref, place_ref, out_refs, rg_ref)

    @pl.when(section != 0)
    def _():
        down_cols = Loads(down_in, down_ref, cols_sems, 1)
        start_all(down_cols)
        send_down(active_ref, down_ref, down_cols, pick_lane(prob_ref[...], 0), place_ref, out_refs)
        rg_ref[...] = rg_in_ref[...]


def with_pieces(body, count, inputs, groups, *refs):
    ins, rest = refs[:inputs], refs[inputs:]
    body(ins[:count], rest[:groups], *ins[count:], *rest[groups:])


def expert_call(body, pieces, small, weights, outs, scratch, flops, by_rows=False):
    width, hidden_units = weights[0].shape
    shape = jax.ShapeDtypeStruct
    groups = lax.axis_size("dp")
    tokens = sum(p.shape[0] for p in pieces)
    outs = [shape((tokens // groups, width), BF16)] * groups + outs
    sems = lambda total, most: pltpu.SemaphoreType.DMA((total // tile_of(total, most),))
    pair = sems(width, 1024) if by_rows else sems(hidden_units, 512)
    scratch = [
        pltpu.VMEM((tokens, pieces[0].shape[1]), BF16), pltpu.SemaphoreType.DMA((len(pieces),)),
        *[pltpu.VMEM(w.shape, BF16) for w in weights],
        pair, pair, sems(hidden_units, 1024), sems(width, 1024),
    ] + scratch
    held = sum(w.size * w.dtype.itemsize for w in weights)
    block, outside = pl.BlockSpec(memory_space=pltpu.VMEM), pl.BlockSpec(memory_space=pl.ANY)
    in_specs = [outside] * len(pieces) + [block] * len(small) + [outside] * len(weights)
    results = pl.pallas_call(
        functools.partial(with_pieces, body, len(pieces), len(in_specs), groups),
        in_specs=in_specs,
        out_specs=[block] * len(outs),
        out_shape=outs,
        scratch_shapes=scratch,
        cost_estimate=pl.CostEstimate(flops=flops, bytes_accessed=held, transcendentals=0),
        compiler_params=pltpu.CompilerParams(
            vmem_limit_bytes=held + 6 * 2**20 + 4 * tokens * width * 2
        ),
    )(*pieces, *small, *weights)
    return results[:groups], *results[groups:]


def moved(block, axes, target):
    sizes = [lax.axis_size(a) for a in axes]
    spots = [()]
    for n in sizes:
        spots = [spot + (i,) for spot in spots for i in range(n)]
    number = {spot: i for i, spot in enumerate(spots)}
    pairs = [(number[spot], number[target(*spot)]) for spot in spots if target(*spot) in number]
    return lax.ppermute(block, axes, pairs)


def flips():
    bits = lax.axis_size("dp").bit_length() - 1
    return [1 << b for b in reversed(range(bits))]


def flipped(block, bit):
    return moved(block, ("dp",), lambda d: (d ^ bit,))


def gathered(block, distance):
    count = lax.axis_size("expert")
    if distance == 0:
        parts = [block] + [
            moved(block, ("expert",), lambda e, k=k: ((e + k) % count,)) for k in range(1, count)
        ]
    else:
        parts = [
            moved(block, ("section", "expert"), lambda s, e, k=k: (s + distance, (e + k) % count))
            for k in range(count)
        ]
    groups = [parts]
    for bit in flips():
        groups = groups + [[flipped(part, bit) for part in group] for group in groups]
    return [part for group in groups for part in group]


def combined(pieces, late=None):
    count = lax.axis_size("expert")
    own = pieces[0].shape[0] // count
    add = lambda kept, came: (kept.astype(F32) + came.astype(F32)).astype(BF16)
    cut = lambda group: [group[k * own:(k + 1) * own] for k in range(count)]
    order = list(reversed(flips()))
    half = len(pieces) // 2
    came = [flipped(group, order[0]) for group in pieces[half:]]
    groups = [
        [add(*pair) for pair in zip(cut(kept), cut(got))] for kept, got in zip(pieces[:half], came)
    ]
    for bit in order[1:]:
        groups, late = lax.optimization_barrier((groups, late))
        half = len(groups) // 2
        groups = [
            [add(kept, flipped(sent, bit)) for kept, sent in zip(*pair)]
            for pair in zip(groups[:half], groups[half:])
        ]
    parts = groups[0]
    total = parts[0].astype(F32)
    for k in range(1, count):
        total = total + moved(parts[k], ("expert",), lambda e, k=k: ((e - k) % count,)).astype(F32)
    return total, late


def summed(block):
    for bit in flips():
        block = block + flipped(block, bit)
    count = lax.axis_size("expert")
    for bit in [1 << b for b in range(count.bit_length() - 1)]:
        block = block + moved(block, ("expert",), lambda e, bit=bit: (e ^ bit,))
    return block


def input_grad(layer_in, upstream, d_hidden, gain_row):
    values = layer_in.astype(F32)
    inv_rms = lax.rsqrt(jnp.mean(values * values, axis=-1, keepdims=True) + EPSILON)
    weighted = gain_row * d_hidden
    mean = jnp.mean(values * weighted, axis=-1, keepdims=True)
    cubed = inv_rms * inv_rms * inv_rms
    d_in = upstream.astype(F32) + inv_rms * weighted - values * cubed * mean
    return d_in.astype(BF16)


def per_device(inputs, cotangent, norm_gain, router, w_gate, w_up, w_down, routes):
    section = lax.axis_index("section")
    at_start = section == 0
    micro, toks, width = inputs.shape
    experts, top_k = router.shape[2], routes.shape[3]
    capacity = 3 * top_k * toks // (2 * experts)
    peers = lax.axis_size("expert") * lax.axis_size("dp")
    own = micro * toks
    tokens, rows = peers * own, peers * micro * capacity
    weights = (w_gate[0, 0], w_up[0, 0], w_down[0, 0])
    hidden_units = weights[0].shape[1]
    gain_row = norm_gain[0].astype(F32)
    router_w = jnp.pad(router[0].T, ((0, LANES - experts), (0, 0)))
    kept = -(-experts // 8) * 8
    shape = jax.ShapeDtypeStruct
    dot_flops = 2 * rows * width * hidden_units
    row_block, lane_block = pltpu.VMEM((rows, width), BF16), pltpu.VMEM((rows, LANES), F32)
    d_block = pltpu.VMEM((rows, hidden_units), BF16)

    mine = jnp.where(at_start, inputs, cotangent).reshape(own, width)
    tail = jnp.pad(routes[0].reshape(own, top_k).astype(BF16), ((0, 0), (0, LANES - top_k)))
    payload = jnp.concatenate([mine, tail], axis=1)
    out, place, pick, hidden, info, stash_a, stash_b = expert_call(
        first_kernel, gathered(payload, 0), [norm_gain, router_w], weights,
        [shape((tokens, rows), BF16), shape((rows, tokens), BF16),
         shape((rows, width), BF16), shape((2, rows, LANES), F32),
         shape((rows, hidden_units), BF16), shape((rows, hidden_units), BF16)],
        [row_block, d_block],
        3 * dot_flops,
    )
    acts_start = (mine.astype(F32) + combined(out)[0]).astype(BF16)

    pieces = gathered(acts_start, 1)
    arrived = pieces[0]
    back, active, prob, rg = expert_call(
        middle_kernel, pieces,
        [norm_gain, router_w, place, pick, info, stash_a], weights,
        [shape((rows, hidden_units), BF16), shape((rows, LANES), F32), shape((kept, width), F32)],
        [row_block, row_block, d_block, d_block, lane_block],
        4 * dot_flops,
    )
    grads_end = input_grad(arrived, mine, combined(back)[0], gain_row)

    pieces = gathered(grads_end, -1)
    upstream = pieces[0]
    out, rg = expert_call(
        last_kernel, pieces,
        [router_w, place, pick, info, hidden, prob, rg, stash_a, stash_b, active], weights,
        [shape((kept, width), F32)],
        [row_block, d_block, d_block, lane_block],
        3 * dot_flops, by_rows=True,
    )
    total, rg = combined(out, rg)
    router_total = summed(rg)[:experts].T
    grads_start = input_grad(mine, upstream, total, gain_row)
    acts_end = (arrived.astype(F32) + total).astype(BF16)
    acts = jnp.where(at_start, acts_start, acts_end).reshape(1, micro, toks, width)
    grads = jnp.where(at_start, grads_start, grads_end).reshape(1, micro, toks, width)
    return acts, grads, router_total[None]


def solution(mesh):
    placed = (
        P(None, GROUP, None),
        P(None, GROUP, None),
        P("section", None),
        P("section", None, None),
        P("section", "expert", None, "dp"),
        P("section", "expert", None, "dp"),
        P("section", "expert", "dp", None),
        P("section", None, GROUP, None),
    )
    return jax.shard_map(
        per_device,
        mesh=mesh,
        in_specs=placed,
        out_specs=(
            P("section", None, GROUP, None),
            P("section", None, GROUP, None),
            P("section", None, None),
        ),
        check_vma=False,
    )
```

```python
import functools

import jax
import jax.numpy as jnp
from jax import lax
from jax.experimental import pallas as pl
from jax.experimental.pallas import tpu as pltpu
from jax.sharding import PartitionSpec as P

EPSILON = 1e-05
LANES = 128
GROUP = ("expert", "dp")
F32 = jnp.float32
BF16 = jnp.bfloat16


def dot_nn(a, b):
    return jnp.dot(a, b, preferred_element_type=F32)


def dot_nt(a, b):
    return lax.dot_general(a, b, (((1,), (1,)), ((), ())), preferred_element_type=F32)


def lanes_like(rows):
    return lax.broadcasted_iota(jnp.int32, (rows, LANES), 1)


def pick_lane(block, lane):
    return jnp.sum(jnp.where(lanes_like(block.shape[0]) == lane, block, 0.0), axis=1, keepdims=True)


def hi_lo(block):
    high = block.astype(BF16)
    return high, (block - high.astype(F32)).astype(BF16)


def place_rows(tail, me, place_ref, pick_ref):
    tokens, rows = place_ref.shape
    wide = -(-rows // LANES) * LANES
    first, second = pick_lane(tail, 0), pick_lane(tail, 1)
    mine = jnp.broadcast_to(((first == me) | (second == me)).astype(F32), (tokens, wide))
    row = lax.broadcasted_iota(jnp.int32, (tokens, tokens), 0)
    col = lax.broadcasted_iota(jnp.int32, (tokens, tokens), 1)
    earlier = dot_nn((col < row).astype(F32).astype(BF16), mine.astype(BF16))
    slot = lax.broadcasted_iota(jnp.int32, (tokens, wide), 1).astype(F32)
    place = jnp.where((earlier == slot) & (mine > 0.5), 1.0, 0.0)
    place_ref[...] = place[:, :rows].astype(BF16)
    pick_ref[...] = jnp.transpose(place)[:rows].astype(BF16)


def signs_of(tail, me):
    first, second = pick_lane(tail, 0), pick_lane(tail, 1)
    other = first + second - me
    lane = lanes_like(tail.shape[0]).astype(F32)
    both = (lane == me).astype(F32) - (lane == other).astype(F32)
    return jnp.where(first != second, both, 0.0)


def norm_and_gap(rows_ref, gain_ref, router_ref, signs, hidden_ref):
    rows, width = rows_ref.shape

    def square(i, part, total):
        values = rows_ref[:, part].astype(F32)
        return total + jnp.sum(values * values, axis=1, keepdims=True)

    squares = tiles(width, square, jnp.zeros((rows, 1), F32))
    inv_rms = lax.rsqrt(squares / width + EPSILON)

    def scale(i, part, total):
        hidden = (rows_ref[:, part].astype(F32) * inv_rms * gain_ref[:, part].astype(F32)).astype(BF16)
        hidden_ref[:, part] = hidden
        return total + dot_nt(hidden, router_ref[:, part])

    logits = tiles(width, scale, jnp.zeros((rows, LANES), F32))
    return jnp.sum(logits * signs, axis=1, keepdims=True)


def tile_of(total, most=1024):
    return next(c for c in (1024, 512, 256, 128) if c <= most and total % c == 0)


def tiles(total, body, carry=0, most=1024):
    step = tile_of(total, most)

    def one(i, carry):
        return body(i, pl.ds(pl.multiple_of(i * step, step), step), carry)

    return lax.fori_loop(0, total // step, one, carry)


class Loads:
    def __init__(self, source, target, sems, axis):
        self.source, self.target, self.sems, self.axis = source, target, sems, axis
        self.count, self.total = sems.shape[0], target.shape[axis]

    def copy(self, i):
        step = self.total // self.count
        part = pl.ds(pl.multiple_of(i * step, step), step)
        spot = (slice(None), part) if self.axis else (part,)
        return pltpu.make_async_copy(self.source.at[spot], self.target.at[spot], self.sems.at[i])

    def wait(self, i):
        self.copy(i).wait()


def start_all(*loads):
    def one(i, carry):
        for load in loads:
            load.copy(i).start()
        return carry

    lax.fori_loop(0, loads[0].count, one, 0)


def select(pick_ref, x_ref, rows_ref):
    def body(i, part, carry):
        rows_ref[:, part] = dot_nn(pick_ref[...], x_ref[:, part]).astype(BF16)
        return carry

    tiles(rows_ref.shape[1], body)


def piece_copies(x_refs, x_ref, sems):
    start, copies = 0, []
    for i, ref in enumerate(x_refs):
        copies.append(pltpu.make_async_copy(ref, x_ref.at[pl.ds(start, ref.shape[0])], sems.at[i]))
        start += ref.shape[0]
    return copies


def fetch(x_refs, x_ref, sems):
    copies = piece_copies(x_refs, x_ref, sems)
    for copy in copies:
        copy.start()
    for copy in copies:
        copy.wait()


def spread(place_ref, rows, out_refs, part):
    piece = out_refs[0].shape[0]
    block = dot_nn(place_ref[...], rows).astype(BF16)
    for i, out_ref in enumerate(out_refs):
        out_ref[:, part] = block[i * piece:(i + 1) * piece]


def send_down(active_ref, down_ref, down_loads, prob, place_ref, out_refs):
    def body(i, part, carry):
        down_loads.wait(i)
        rows = dot_nn(active_ref[...], down_ref[:, part]) * prob
        spread(place_ref, rows.astype(BF16), out_refs, part)
        return carry

    tiles(down_ref.shape[1], body)


def grads_of(gate_pre, up_pre, d_raw, prob, part, dprob_ref, active_ref, d_gate_ref, d_up_ref):
    gate_sig = jax.nn.sigmoid(gate_pre)
    act = gate_pre * gate_sig
    active = (act * up_pre).astype(BF16)
    if active_ref is not None:
        active_ref[:, part] = active
    gain = jnp.sum(active.astype(F32) * d_raw, axis=1, keepdims=True)
    dprob_ref[...] += jnp.broadcast_to(gain, dprob_ref.shape)
    d_active = d_raw * prob
    d_gate = d_active * up_pre * gate_sig * (1.0 + gate_pre * (1.0 - gate_sig))
    d_gate_ref[:, part] = d_gate.astype(BF16)
    d_up_ref[:, part] = (d_active * act).astype(BF16)


def send_back(gate_ref, up_ref, gate_loads, up_loads, d_gate_ref, d_up_ref, dprob_ref, gap, signs,
              hidden_ref, router_ref, place_ref, out_refs, rg_ref):
    c = jax.nn.sigmoid(gap) * jax.nn.sigmoid(-gap) * dprob_ref[...] * signs
    c_high, c_low = hi_lo(c)
    t_high, t_low = hi_lo(jnp.transpose(c)[:rg_ref.shape[0]])

    def body(i, part, carry):
        if gate_loads is not None:
            gate_loads.wait(i)
            up_loads.wait(i)
        back = dot_nt(d_gate_ref[...], gate_ref[part, :]) + dot_nt(d_up_ref[...], up_ref[part, :])
        extra = dot_nn(c_high, router_ref[:, part]) + dot_nn(c_low, router_ref[:, part])
        spread(place_ref, (back + extra).astype(BF16), out_refs, part)
        hidden = hidden_ref[:, part]
        rg_ref[:, part] = dot_nn(t_high, hidden) + dot_nn(t_low, hidden)
        return carry

    tiles(gate_ref.shape[0], body)


def first_kernel(x_refs, out_refs, gain_ref, router_ref, gate_in, up_in, down_in,
                 place_ref, pick_ref, hidden_ref, info_ref, a_ref, b_ref,
                 x_ref, x_sems, gate_ref, up_ref, down_ref, gate_sems, up_sems, rows_sems, cols_sems,
                 rows_ref, active_ref):
    section = lax.axis_index("section")
    width = gain_ref.shape[1]
    gate_loads = Loads(gate_in, gate_ref, gate_sems, 1)
    up_loads = Loads(up_in, up_ref, up_sems, 1)
    down_cols = Loads(down_in, down_ref, cols_sems, 1)
    down_rows = Loads(down_in, down_ref, rows_sems, 0)
    fetches = piece_copies(x_refs, x_ref, x_sems)
    for copy in fetches:
        copy.start()

    @pl.when(section == 0)
    def _():
        start_all(gate_loads, up_loads)
        start_all(down_cols)

    @pl.when(section != 0)
    def _():
        start_all(down_rows)

    for copy in fetches:
        copy.wait()
    me = lax.axis_index("expert").astype(F32)
    tail = x_ref[:, width:]
    place_rows(tail.astype(F32), me, place_ref, pick_ref)
    select(pick_ref, x_ref, rows_ref)
    info_ref[0] = signs_of(dot_nn(pick_ref[...], tail), me)

    @pl.when(section == 0)
    def _():
        gap = norm_and_gap(rows_ref, gain_ref, router_ref, info_ref[0], hidden_ref)
        info_ref[1] = jnp.broadcast_to(gap, info_ref.shape[1:])

        def body(i, part, carry):
            gate_loads.wait(i)
            up_loads.wait(i)
            gate_pre = dot_nn(hidden_ref[...], gate_ref[:, part])
            up_pre = dot_nn(hidden_ref[...], up_ref[:, part])
            a_ref[:, part] = gate_pre.astype(BF16)
            b_ref[:, part] = up_pre.astype(BF16)
            active_ref[:, part] = (gate_pre * jax.nn.sigmoid(gate_pre) * up_pre).astype(BF16)
            return carry

        tiles(gate_ref.shape[1], body, most=512)
        send_down(active_ref, down_ref, down_cols, jax.nn.sigmoid(gap), place_ref, out_refs)

    @pl.when(section != 0)
    def _():
        def body(i, part, carry):
            down_rows.wait(i)
            a_ref[:, part] = dot_nt(rows_ref[...], down_ref[part, :]).astype(BF16)
            return carry

        tiles(down_ref.shape[0], body)


def middle_kernel(x_refs, back_refs, gain_ref, router_ref, place_ref, pick_ref, info_ref, raw_ref,
                  gate_in, up_in, down_in,
                  active_ref, prob_ref, rg_ref,
                  x_ref, x_sems, gate_ref, up_ref, down_ref, gate_sems, up_sems, rows_sems, cols_sems,
                  rows_ref, hidden_ref, d_gate_ref, d_up_ref, dprob_ref):
    @pl.when(lax.axis_index("section") == 1)
    def _():
        gate_loads = Loads(gate_in, gate_ref, gate_sems, 1)
        up_loads = Loads(up_in, up_ref, up_sems, 1)
        fetches = piece_copies(x_refs, x_ref, x_sems)
        for copy in fetches:
            copy.start()
        start_all(gate_loads, up_loads)
        for copy in fetches:
            copy.wait()
        select(pick_ref, x_ref, rows_ref)
        signs = info_ref[0]
        gap = norm_and_gap(rows_ref, gain_ref, router_ref, signs, hidden_ref)
        prob = jax.nn.sigmoid(gap)
        prob_ref[...] = jnp.broadcast_to(prob, prob_ref.shape)
        dprob_ref[...] = jnp.zeros_like(dprob_ref)

        def body(i, part, carry):
            gate_loads.wait(i)
            up_loads.wait(i)
            gate_pre = dot_nn(hidden_ref[...], gate_ref[:, part])
            up_pre = dot_nn(hidden_ref[...], up_ref[:, part])
            grads_of(gate_pre, up_pre, raw_ref[:, part].astype(F32), prob, part, dprob_ref,
                     active_ref, d_gate_ref, d_up_ref)
            return carry

        tiles(gate_ref.shape[1], body, most=512)
        send_back(gate_ref, up_ref, None, None, d_gate_ref, d_up_ref, dprob_ref, gap, signs,
                  hidden_ref, router_ref, place_ref, back_refs, rg_ref)


def last_kernel(u_refs, out_refs, router_ref, place_ref, pick_ref, info_ref, hidden_ref, prob_ref,
                rg_in_ref, a_ref, b_ref, active_ref, gate_in, up_in, down_in,
                rg_ref,
                x_ref, x_sems, gate_ref, up_ref, down_ref, gate_sems, up_sems, rows_sems, cols_sems,
                rows_ref, d_gate_ref, d_up_ref, dprob_ref):
    section = lax.axis_index("section")

    @pl.when(section == 0)
    def _():
        down_rows = Loads(down_in, down_ref, rows_sems, 0)
        gate_loads = Loads(gate_in, gate_ref, gate_sems, 0)
        up_loads = Loads(up_in, up_ref, up_sems, 0)
        fetches = piece_copies(u_refs, x_ref, x_sems)
        for copy in fetches:
            copy.start()
        start_all(down_rows)
        start_all(gate_loads, up_loads)
        for copy in fetches:
            copy.wait()
        select(pick_ref, x_ref, rows_ref)
        gap = pick_lane(info_ref[1], 0)
        prob = jax.nn.sigmoid(gap)
        dprob_ref[...] = jnp.zeros_like(dprob_ref)

        def body(i, part, carry):
            down_rows.wait(i)
            d_raw = dot_nt(rows_ref[...], down_ref[part, :])
            grads_of(a_ref[:, part].astype(F32), b_ref[:, part].astype(F32), d_raw, prob, part,
                     dprob_ref, None, d_gate_ref, d_up_ref)
            return carry

        tiles(down_ref.shape[0], body)
        send_back(gate_ref, up_ref, gate_loads, up_loads, d_gate_ref, d_up_ref, dprob_ref, gap,
                  info_ref[0], hidden_ref, router_ref, place_ref, out_refs, rg_ref)

    @pl.when(section != 0)
    def _():
        down_cols = Loads(down_in, down_ref, cols_sems, 1)
        start_all(down_cols)
        send_down(active_ref, down_ref, down_cols, pick_lane(prob_ref[...], 0), place_ref, out_refs)
        rg_ref[...] = rg_in_ref[...]


def with_pieces(body, count, inputs, groups, *refs):
    ins, rest = refs[:inputs], refs[inputs:]
    body(ins[:count], rest[:groups], *ins[count:], *rest[groups:])


def expert_call(body, pieces, small, weights, outs, scratch, flops, by_rows=False):
    width, hidden_units = weights[0].shape
    shape = jax.ShapeDtypeStruct
    groups = lax.axis_size("dp")
    tokens = sum(p.shape[0] for p in pieces)
    outs = [shape((tokens // groups, width), BF16)] * groups + outs
    sems = lambda total, most: pltpu.SemaphoreType.DMA((total // tile_of(total, most),))
    pair = sems(width, 1024) if by_rows else sems(hidden_units, 512)
    scratch = [
        pltpu.VMEM((tokens, pieces[0].shape[1]), BF16), pltpu.SemaphoreType.DMA((len(pieces),)),
        *[pltpu.VMEM(w.shape, BF16) for w in weights],
        pair, pair, sems(hidden_units, 1024), sems(width, 1024),
    ] + scratch
    held = sum(w.size * w.dtype.itemsize for w in weights)
    block, outside = pl.BlockSpec(memory_space=pltpu.VMEM), pl.BlockSpec(memory_space=pl.ANY)
    in_specs = [outside] * len(pieces) + [block] * len(small) + [outside] * len(weights)
    results = pl.pallas_call(
        functools.partial(with_pieces, body, len(pieces), len(in_specs), groups),
        in_specs=in_specs,
        out_specs=[block] * len(outs),
        out_shape=outs,
        scratch_shapes=scratch,
        cost_estimate=pl.CostEstimate(flops=flops, bytes_accessed=held, transcendentals=0),
        compiler_params=pltpu.CompilerParams(
            vmem_limit_bytes=held + 6 * 2**20 + 4 * tokens * width * 2
        ),
    )(*pieces, *small, *weights)
    return results[:groups], *results[groups:]


def moved(block, axes, target):
    sizes = [lax.axis_size(a) for a in axes]
    spots = [()]
    for n in sizes:
        spots = [spot + (i,) for spot in spots for i in range(n)]
    number = {spot: i for i, spot in enumerate(spots)}
    pairs = [(number[spot], number[target(*spot)]) for spot in spots if target(*spot) in number]
    return lax.ppermute(block, axes, pairs)


def flips():
    bits = lax.axis_size("dp").bit_length() - 1
    return [1 << b for b in reversed(range(bits))]


def flipped(block, bit):
    return moved(block, ("dp",), lambda d: (d ^ bit,))


def gathered(block):
    count = lax.axis_size("expert")
    parts = [block] + [
        moved(block, ("expert",), lambda e, k=k: ((e + k) % count,)) for k in range(1, count)
    ]
    groups = [parts]
    for bit in flips():
        groups = groups + [[flipped(part, bit) for part in group] for group in groups]
    return [part for group in groups for part in group]


def combined(pieces, hop=0, late=None):
    count = lax.axis_size("expert")
    own = pieces[0].shape[0] // count
    add = lambda kept, came: (kept.astype(F32) + came.astype(F32)).astype(BF16)
    cut = lambda group: [group[k * own:(k + 1) * own] for k in range(count)]
    order = list(reversed(flips()))
    half = len(pieces) // 2
    came = [flipped(group, order[0]) for group in pieces[half:]]
    groups = [
        [add(*pair) for pair in zip(cut(kept), cut(got))] for kept, got in zip(pieces[:half], came)
    ]
    for bit in order[1:]:
        groups, late = lax.optimization_barrier((groups, late))
        half = len(groups) // 2
        groups = [
            [add(kept, flipped(sent, bit)) for kept, sent in zip(*pair)]
            for pair in zip(groups[:half], groups[half:])
        ]
    total = 0.0
    for k, part in enumerate(groups[0]):
        if hop:
            part = moved(part, ("section", "expert"), lambda s, e, k=k: (s + hop, (e - k) % count))
        elif k:
            part = moved(part, ("expert",), lambda e, k=k: ((e - k) % count,))
        total = total + part.astype(F32)
    return total, late


def summed(block):
    for bit in reversed(flips()):
        block = block + flipped(block, bit)
    count = lax.axis_size("expert")
    total = block
    for k in range(1, count):
        total = total + moved(block, ("expert",), lambda e, k=k: ((e + k) % count,))
    return total


def across(block, distance):
    return moved(block, ("section",), lambda s: (s + distance,))


def swapped(block):
    return moved(block, ("section",), lambda s: (lax.axis_size("section") - 1 - s,))


def input_grad(layer_in, upstream, d_hidden, gain_row):
    values = layer_in.astype(F32)
    inv_rms = lax.rsqrt(jnp.mean(values * values, axis=-1, keepdims=True) + EPSILON)
    weighted = gain_row * d_hidden
    mean = jnp.mean(values * weighted, axis=-1, keepdims=True)
    cubed = inv_rms * inv_rms * inv_rms
    d_in = upstream.astype(F32) + inv_rms * weighted - values * cubed * mean
    return d_in.astype(BF16)


def per_device(inputs, cotangent, norm_gain, router, w_gate, w_up, w_down, routes):
    section = lax.axis_index("section")
    at_start = section == 0
    micro, toks, width = inputs.shape
    experts, top_k = router.shape[2], routes.shape[3]
    capacity = 3 * top_k * toks // (2 * experts)
    peers = lax.axis_size("expert") * lax.axis_size("dp")
    own = micro * toks
    tokens, rows = peers * own, peers * micro * capacity
    weights = (w_gate[0, 0], w_up[0, 0], w_down[0, 0])
    hidden_units = weights[0].shape[1]
    gain_row = norm_gain[0].astype(F32)
    router_w = jnp.pad(router[0].T, ((0, LANES - experts), (0, 0)))
    kept = -(-experts // 8) * 8
    shape = jax.ShapeDtypeStruct
    dot_flops = 2 * rows * width * hidden_units
    row_block, lane_block = pltpu.VMEM((rows, width), BF16), pltpu.VMEM((rows, LANES), F32)
    d_block = pltpu.VMEM((rows, hidden_units), BF16)

    mine = jnp.where(at_start, inputs, cotangent).reshape(own, width)
    tail = jnp.pad(routes[0].reshape(own, top_k).astype(BF16), ((0, 0), (0, LANES - top_k)))
    payload = jnp.concatenate([mine, tail], axis=1)
    theirs, their_gain = swapped(mine), swapped(norm_gain)[0].astype(F32)
    out, place, pick, hidden, info, stash_a, stash_b = expert_call(
        first_kernel, gathered(payload), [norm_gain, router_w], weights,
        [shape((tokens, rows), BF16), shape((rows, tokens), BF16),
         shape((rows, width), BF16), shape((2, rows, LANES), F32),
         shape((rows, hidden_units), BF16), shape((rows, hidden_units), BF16)],
        [row_block, d_block],
        3 * dot_flops,
    )
    acts_mid = (theirs.astype(F32) + combined(out, 1)[0]).astype(BF16)

    back, active, prob, rg = expert_call(
        middle_kernel, gathered(acts_mid),
        [norm_gain, router_w, place, pick, info, stash_a], weights,
        [shape((rows, hidden_units), BF16), shape((rows, LANES), F32), shape((kept, width), F32)],
        [row_block, row_block, d_block, d_block, lane_block],
        4 * dot_flops,
    )
    acts_start = across(acts_mid, -1)
    grads_mid = input_grad(acts_start, theirs, combined(back, -1)[0], their_gain)

    out, rg = expert_call(
        last_kernel, gathered(grads_mid),
        [router_w, place, pick, info, hidden, prob, rg, stash_a, stash_b, active], weights,
        [shape((kept, width), F32)],
        [row_block, d_block, d_block, lane_block],
        3 * dot_flops, by_rows=True,
    )
    grads_end = across(grads_mid, 1)
    total, rg = combined(out, late=rg)
    router_total = summed(rg)[:experts].T
    grads_start = input_grad(mine, grads_mid, total, gain_row)
    acts_end = (acts_mid.astype(F32) + total).astype(BF16)
    acts = jnp.where(at_start, acts_start, acts_end).reshape(1, micro, toks, width)
    grads = jnp.where(at_start, grads_start, grads_end).reshape(1, micro, toks, width)
    return acts, grads, router_total[None]


def solution(mesh):
    placed = (
        P(None, GROUP, None),
        P(None, GROUP, None),
        P("section", None),
        P("section", None, None),
        P("section", "expert", None, "dp"),
        P("section", "expert", None, "dp"),
        P("section", "expert", "dp", None),
        P("section", None, GROUP, None),
    )
    return jax.shard_map(
        per_device,
        mesh=mesh,
        in_specs=placed,
        out_specs=(
            P("section", None, GROUP, None),
            P("section", None, GROUP, None),
            P("section", None, None),
        ),
        check_vma=False,
    )
```

```python
import functools

import jax
import jax.numpy as jnp
from jax import lax
from jax.experimental import pallas as pl
from jax.experimental.pallas import tpu as pltpu
from jax.sharding import PartitionSpec as P

EPSILON = 1e-05
LANES = 128
GROUP = ("expert", "dp")
F32 = jnp.float32
BF16 = jnp.bfloat16


def dot_nn(a, b):
    return jnp.dot(a, b, preferred_element_type=F32)


def dot_nt(a, b):
    return lax.dot_general(a, b, (((1,), (1,)), ((), ())), preferred_element_type=F32)


def lanes_like(rows):
    return lax.broadcasted_iota(jnp.int32, (rows, LANES), 1)


def pick_lane(block, lane):
    return jnp.sum(jnp.where(lanes_like(block.shape[0]) == lane, block, 0.0), axis=1, keepdims=True)


def hi_lo(block):
    high = block.astype(BF16)
    return high, (block - high.astype(F32)).astype(BF16)


def place_rows(tail, me, place_ref, pick_ref):
    tokens, rows = place_ref.shape
    wide = -(-rows // LANES) * LANES
    first, second = pick_lane(tail, 0), pick_lane(tail, 1)
    mine = jnp.broadcast_to(((first == me) | (second == me)).astype(F32), (tokens, wide))
    row = lax.broadcasted_iota(jnp.int32, (tokens, tokens), 0)
    col = lax.broadcasted_iota(jnp.int32, (tokens, tokens), 1)
    earlier = dot_nn((col < row).astype(F32).astype(BF16), mine.astype(BF16))
    slot = lax.broadcasted_iota(jnp.int32, (tokens, wide), 1).astype(F32)
    place = jnp.where((earlier == slot) & (mine > 0.5), 1.0, 0.0)
    place_ref[...] = place[:, :rows].astype(BF16)
    pick_ref[...] = jnp.transpose(place)[:rows].astype(BF16)


def signs_of(tail, me):
    first, second = pick_lane(tail, 0), pick_lane(tail, 1)
    other = first + second - me
    lane = lanes_like(tail.shape[0]).astype(F32)
    both = (lane == me).astype(F32) - (lane == other).astype(F32)
    return jnp.where(first != second, both, 0.0)


def norm_and_gap(rows_ref, gain_ref, router_ref, signs, hidden_ref):
    rows, width = rows_ref.shape

    def square(i, part, total):
        values = rows_ref[:, part].astype(F32)
        return total + jnp.sum(values * values, axis=1, keepdims=True)

    squares = tiles(width, square, jnp.zeros((rows, 1), F32))
    inv_rms = lax.rsqrt(squares / width + EPSILON)

    def scale(i, part, total):
        hidden = (rows_ref[:, part].astype(F32) * inv_rms * gain_ref[:, part].astype(F32)).astype(BF16)
        hidden_ref[:, part] = hidden
        return total + dot_nt(hidden, router_ref[:, part])

    logits = tiles(width, scale, jnp.zeros((rows, LANES), F32))
    return jnp.sum(logits * signs, axis=1, keepdims=True)


def tile_of(total, most=1024):
    return next(c for c in (1024, 512, 256, 128) if c <= most and total % c == 0)


def tiles(total, body, carry=0, most=1024):
    step = tile_of(total, most)

    def one(i, carry):
        return body(i, pl.ds(pl.multiple_of(i * step, step), step), carry)

    return lax.fori_loop(0, total // step, one, carry)


class Loads:
    def __init__(self, source, target, sems, axis):
        self.source, self.target, self.sems, self.axis = source, target, sems, axis
        self.count, self.total = sems.shape[0], target.shape[axis]

    def copy(self, i):
        step = self.total // self.count
        part = pl.ds(pl.multiple_of(i * step, step), step)
        spot = (slice(None), part) if self.axis else (part,)
        return pltpu.make_async_copy(self.source.at[spot], self.target.at[spot], self.sems.at[i])

    def wait(self, i):
        self.copy(i).wait()


def start_all(*loads):
    def one(i, carry):
        for load in loads:
            load.copy(i).start()
        return carry

    lax.fori_loop(0, loads[0].count, one, 0)


def select(pick_ref, x_ref, rows_ref):
    def body(i, part, carry):
        rows_ref[:, part] = dot_nn(pick_ref[...], x_ref[:, part]).astype(BF16)
        return carry

    tiles(rows_ref.shape[1], body)


def piece_copies(x_refs, x_ref, sems):
    start, copies = 0, []
    for i, ref in enumerate(x_refs):
        copies.append(pltpu.make_async_copy(ref, x_ref.at[pl.ds(start, ref.shape[0])], sems.at[i]))
        start += ref.shape[0]
    return copies


def fetch(x_refs, x_ref, sems):
    copies = piece_copies(x_refs, x_ref, sems)
    for copy in copies:
        copy.start()
    for copy in copies:
        copy.wait()


def spread(place_ref, rows, out_refs, part):
    piece = out_refs[0].shape[0]
    block = dot_nn(place_ref[...], rows).astype(BF16)
    for i, out_ref in enumerate(out_refs):
        out_ref[:, part] = block[i * piece:(i + 1) * piece]


def send_down(active_ref, down_ref, down_loads, prob, place_ref, out_refs):
    def body(i, part, carry):
        down_loads.wait(i)
        rows = dot_nn(active_ref[...], down_ref[:, part]) * prob
        spread(place_ref, rows.astype(BF16), out_refs, part)
        return carry

    tiles(down_ref.shape[1], body)


def grads_of(gate_pre, up_pre, d_raw, prob, part, dprob_ref, active_ref, d_gate_ref, d_up_ref):
    gate_sig = jax.nn.sigmoid(gate_pre)
    act = gate_pre * gate_sig
    active = (act * up_pre).astype(BF16)
    if active_ref is not None:
        active_ref[:, part] = active
    gain = jnp.sum(active.astype(F32) * d_raw, axis=1, keepdims=True)
    dprob_ref[...] += jnp.broadcast_to(gain, dprob_ref.shape)
    d_active = d_raw * prob
    d_gate = d_active * up_pre * gate_sig * (1.0 + gate_pre * (1.0 - gate_sig))
    d_gate_ref[:, part] = d_gate.astype(BF16)
    d_up_ref[:, part] = (d_active * act).astype(BF16)


def send_back(gate_ref, up_ref, gate_loads, up_loads, d_gate_ref, d_up_ref, dprob_ref, gap, signs,
              hidden_ref, router_ref, place_ref, out_refs, rg_ref):
    c = jax.nn.sigmoid(gap) * jax.nn.sigmoid(-gap) * dprob_ref[...] * signs
    c_high, c_low = hi_lo(c)
    t_high, t_low = hi_lo(jnp.transpose(c)[:rg_ref.shape[0]])

    def body(i, part, carry):
        if gate_loads is not None:
            gate_loads.wait(i)
            up_loads.wait(i)
        back = dot_nt(d_gate_ref[...], gate_ref[part, :]) + dot_nt(d_up_ref[...], up_ref[part, :])
        extra = dot_nn(c_high, router_ref[:, part]) + dot_nn(c_low, router_ref[:, part])
        spread(place_ref, (back + extra).astype(BF16), out_refs, part)
        hidden = hidden_ref[:, part]
        rg_ref[:, part] = dot_nn(t_high, hidden) + dot_nn(t_low, hidden)
        return carry

    tiles(gate_ref.shape[0], body)


def first_kernel(x_refs, out_refs, gain_ref, router_ref, gate_in, up_in, down_in,
                 place_ref, pick_ref, hidden_ref, info_ref, a_ref, b_ref,
                 x_ref, x_sems, gate_ref, up_ref, down_ref, gate_sems, up_sems, rows_sems, cols_sems,
                 rows_ref, active_ref):
    section = lax.axis_index("section")
    width = gain_ref.shape[1]
    gate_loads = Loads(gate_in, gate_ref, gate_sems, 1)
    up_loads = Loads(up_in, up_ref, up_sems, 1)
    down_cols = Loads(down_in, down_ref, cols_sems, 1)
    down_rows = Loads(down_in, down_ref, rows_sems, 0)
    fetches = piece_copies(x_refs, x_ref, x_sems)
    for copy in fetches:
        copy.start()

    @pl.when(section == 0)
    def _():
        start_all(gate_loads, up_loads)
        start_all(down_cols)

    @pl.when(section != 0)
    def _():
        start_all(down_rows)

    for copy in fetches:
        copy.wait()
    me = lax.axis_index("expert").astype(F32)
    tail = x_ref[:, width:]
    place_rows(tail.astype(F32), me, place_ref, pick_ref)
    select(pick_ref, x_ref, rows_ref)
    info_ref[0] = signs_of(dot_nn(pick_ref[...], tail), me)

    @pl.when(section == 0)
    def _():
        gap = norm_and_gap(rows_ref, gain_ref, router_ref, info_ref[0], hidden_ref)
        info_ref[1] = jnp.broadcast_to(gap, info_ref.shape[1:])

        def body(i, part, carry):
            gate_loads.wait(i)
            up_loads.wait(i)
            gate_pre = dot_nn(hidden_ref[...], gate_ref[:, part])
            up_pre = dot_nn(hidden_ref[...], up_ref[:, part])
            a_ref[:, part] = gate_pre.astype(BF16)
            b_ref[:, part] = up_pre.astype(BF16)
            active_ref[:, part] = (gate_pre * jax.nn.sigmoid(gate_pre) * up_pre).astype(BF16)
            return carry

        tiles(gate_ref.shape[1], body, most=512)
        send_down(active_ref, down_ref, down_cols, jax.nn.sigmoid(gap), place_ref, out_refs)

    @pl.when(section != 0)
    def _():
        def body(i, part, carry):
            down_rows.wait(i)
            a_ref[:, part] = dot_nt(rows_ref[...], down_ref[part, :]).astype(BF16)
            return carry

        tiles(down_ref.shape[0], body)


def middle_kernel(x_refs, back_refs, gain_ref, router_ref, place_ref, pick_ref, info_ref, raw_ref,
                  gate_in, up_in, down_in,
                  active_ref, prob_ref, rg_ref,
                  x_ref, x_sems, gate_ref, up_ref, down_ref, gate_sems, up_sems, rows_sems, cols_sems,
                  rows_ref, hidden_ref, d_gate_ref, d_up_ref, dprob_ref):
    @pl.when(lax.axis_index("section") == 1)
    def _():
        gate_loads = Loads(gate_in, gate_ref, gate_sems, 1)
        up_loads = Loads(up_in, up_ref, up_sems, 1)
        fetches = piece_copies(x_refs, x_ref, x_sems)
        for copy in fetches:
            copy.start()
        start_all(gate_loads, up_loads)
        for copy in fetches:
            copy.wait()
        select(pick_ref, x_ref, rows_ref)
        signs = info_ref[0]
        gap = norm_and_gap(rows_ref, gain_ref, router_ref, signs, hidden_ref)
        prob = jax.nn.sigmoid(gap)
        prob_ref[...] = jnp.broadcast_to(prob, prob_ref.shape)
        dprob_ref[...] = jnp.zeros_like(dprob_ref)

        def body(i, part, carry):
            gate_loads.wait(i)
            up_loads.wait(i)
            gate_pre = dot_nn(hidden_ref[...], gate_ref[:, part])
            up_pre = dot_nn(hidden_ref[...], up_ref[:, part])
            grads_of(gate_pre, up_pre, raw_ref[:, part].astype(F32), prob, part, dprob_ref,
                     active_ref, d_gate_ref, d_up_ref)
            return carry

        tiles(gate_ref.shape[1], body, most=512)
        send_back(gate_ref, up_ref, None, None, d_gate_ref, d_up_ref, dprob_ref, gap, signs,
                  hidden_ref, router_ref, place_ref, back_refs, rg_ref)


def last_kernel(u_refs, out_refs, router_ref, place_ref, pick_ref, info_ref, hidden_ref, prob_ref,
                rg_in_ref, a_ref, b_ref, active_ref, gate_in, up_in, down_in,
                rg_ref,
                x_ref, x_sems, gate_ref, up_ref, down_ref, gate_sems, up_sems, rows_sems, cols_sems,
                rows_ref, d_gate_ref, d_up_ref, dprob_ref):
    section = lax.axis_index("section")

    @pl.when(section == 0)
    def _():
        down_rows = Loads(down_in, down_ref, rows_sems, 0)
        gate_loads = Loads(gate_in, gate_ref, gate_sems, 0)
        up_loads = Loads(up_in, up_ref, up_sems, 0)
        fetches = piece_copies(u_refs, x_ref, x_sems)
        for copy in fetches:
            copy.start()
        start_all(down_rows)
        start_all(gate_loads, up_loads)
        for copy in fetches:
            copy.wait()
        select(pick_ref, x_ref, rows_ref)
        gap = pick_lane(info_ref[1], 0)
        prob = jax.nn.sigmoid(gap)
        dprob_ref[...] = jnp.zeros_like(dprob_ref)

        def body(i, part, carry):
            down_rows.wait(i)
            d_raw = dot_nt(rows_ref[...], down_ref[part, :])
            grads_of(a_ref[:, part].astype(F32), b_ref[:, part].astype(F32), d_raw, prob, part,
                     dprob_ref, None, d_gate_ref, d_up_ref)
            return carry

        tiles(down_ref.shape[0], body)
        send_back(gate_ref, up_ref, gate_loads, up_loads, d_gate_ref, d_up_ref, dprob_ref, gap,
                  info_ref[0], hidden_ref, router_ref, place_ref, out_refs, rg_ref)

    @pl.when(section != 0)
    def _():
        down_cols = Loads(down_in, down_ref, cols_sems, 1)
        start_all(down_cols)
        send_down(active_ref, down_ref, down_cols, pick_lane(prob_ref[...], 0), place_ref, out_refs)
        rg_ref[...] = rg_in_ref[...]


def with_pieces(body, count, inputs, groups, *refs):
    ins, rest = refs[:inputs], refs[inputs:]
    body(ins[:count], rest[:groups], *ins[count:], *rest[groups:])


def expert_call(body, pieces, small, weights, outs, scratch, flops, by_rows=False):
    width, hidden_units = weights[0].shape
    shape = jax.ShapeDtypeStruct
    groups = lax.axis_size("dp")
    tokens = sum(p.shape[0] for p in pieces)
    outs = [shape((tokens // groups, width), BF16)] * groups + outs
    sems = lambda total, most: pltpu.SemaphoreType.DMA((total // tile_of(total, most),))
    pair = sems(width, 1024) if by_rows else sems(hidden_units, 512)
    scratch = [
        pltpu.VMEM((tokens, pieces[0].shape[1]), BF16), pltpu.SemaphoreType.DMA((len(pieces),)),
        *[pltpu.VMEM(w.shape, BF16) for w in weights],
        pair, pair, sems(hidden_units, 1024), sems(width, 1024),
    ] + scratch
    held = sum(w.size * w.dtype.itemsize for w in weights)
    block, outside = pl.BlockSpec(memory_space=pltpu.VMEM), pl.BlockSpec(memory_space=pl.ANY)
    in_specs = [outside] * len(pieces) + [block] * len(small) + [outside] * len(weights)
    results = pl.pallas_call(
        functools.partial(with_pieces, body, len(pieces), len(in_specs), groups),
        in_specs=in_specs,
        out_specs=[block] * len(outs),
        out_shape=outs,
        scratch_shapes=scratch,
        cost_estimate=pl.CostEstimate(flops=flops, bytes_accessed=held, transcendentals=0),
        compiler_params=pltpu.CompilerParams(
            vmem_limit_bytes=held + 6 * 2**20 + 4 * tokens * width * 2
        ),
    )(*pieces, *small, *weights)
    return results[:groups], *results[groups:]


def moved(block, axes, target):
    sizes = [lax.axis_size(a) for a in axes]
    spots = [()]
    for n in sizes:
        spots = [spot + (i,) for spot in spots for i in range(n)]
    number = {spot: i for i, spot in enumerate(spots)}
    pairs = [(number[spot], number[target(*spot)]) for spot in spots if target(*spot) in number]
    return lax.ppermute(block, axes, pairs)


def flips():
    bits = lax.axis_size("dp").bit_length() - 1
    return [1 << b for b in reversed(range(bits))]


def flipped(block, bit):
    return moved(block, ("dp",), lambda d: (d ^ bit,))


def gathered(block):
    count = lax.axis_size("expert")
    parts = [block] + [
        moved(block, ("expert",), lambda e, k=k: ((e + k) % count,)) for k in range(1, count)
    ]
    groups = [parts]
    for bit in flips():
        groups = groups + [[flipped(part, bit) for part in group] for group in groups]
    return [part for group in groups for part in group]


def combined(pieces, hop=0, late=None):
    count = lax.axis_size("expert")
    own = pieces[0].shape[0] // count
    add = lambda kept, came: (kept.astype(F32) + came.astype(F32)).astype(BF16)
    cut = lambda group: [group[k * own:(k + 1) * own] for k in range(count)]
    order = list(reversed(flips()))
    half = len(pieces) // 2
    came = [flipped(group, order[0]) for group in pieces[half:]]
    groups = [
        [add(*pair) for pair in zip(cut(kept), cut(got))] for kept, got in zip(pieces[:half], came)
    ]
    for bit in order[1:]:
        groups, late = lax.optimization_barrier((groups, late))
        half = len(groups) // 2
        groups = [
            [add(kept, flipped(sent, bit)) for kept, sent in zip(*pair)]
            for pair in zip(groups[:half], groups[half:])
        ]
    total = 0.0
    for k, part in enumerate(groups[0]):
        if hop:
            part = moved(part, ("section", "expert"), lambda s, e, k=k: (s + hop, (e - k) % count))
        elif k:
            part = moved(part, ("expert",), lambda e, k=k: ((e - k) % count,))
        total = total + part.astype(F32)
    return total, late


def summed(block):
    for bit in reversed(flips()):
        block = block + flipped(block, bit)
    count = lax.axis_size("expert")
    total = block
    for k in range(1, count):
        total = total + moved(block, ("expert",), lambda e, k=k: ((e + k) % count,))
    return total


def across(block, distance):
    return moved(block, ("section",), lambda s: (s + distance,))


def swapped(block):
    return moved(block, ("section",), lambda s: (lax.axis_size("section") - 1 - s,))


def input_grad(layer_in, upstream, d_hidden, gain_row):
    values = layer_in.astype(F32)
    inv_rms = lax.rsqrt(jnp.mean(values * values, axis=-1, keepdims=True) + EPSILON)
    weighted = gain_row * d_hidden
    mean = jnp.mean(values * weighted, axis=-1, keepdims=True)
    cubed = inv_rms * inv_rms * inv_rms
    d_in = upstream.astype(F32) + inv_rms * weighted - values * cubed * mean
    return d_in.astype(BF16)


def per_device(inputs, cotangent, norm_gain, router, w_gate, w_up, w_down, routes):
    section = lax.axis_index("section")
    at_start = section == 0
    micro, toks, width = inputs.shape
    experts, top_k = router.shape[2], routes.shape[3]
    capacity = 3 * top_k * toks // (2 * experts)
    peers = lax.axis_size("expert") * lax.axis_size("dp")
    own = micro * toks
    tokens, rows = peers * own, peers * micro * capacity
    weights = (w_gate[0, 0], w_up[0, 0], w_down[0, 0])
    hidden_units = weights[0].shape[1]
    gain_row = norm_gain[0].astype(F32)
    router_w = jnp.pad(router[0].T, ((0, LANES - experts), (0, 0)))
    kept = -(-experts // 8) * 8
    shape = jax.ShapeDtypeStruct
    dot_flops = 2 * rows * width * hidden_units
    row_block, lane_block = pltpu.VMEM((rows, width), BF16), pltpu.VMEM((rows, LANES), F32)
    d_block = pltpu.VMEM((rows, hidden_units), BF16)

    mine = jnp.where(at_start, inputs, cotangent).reshape(own, width)
    tail = jnp.pad(routes[0].reshape(own, top_k).astype(BF16), ((0, 0), (0, LANES - top_k)))
    payload = jnp.concatenate([mine, tail], axis=1)
    theirs, their_gain = swapped(mine), swapped(norm_gain)[0].astype(F32)
    out, place, pick, hidden, info, stash_a, stash_b = expert_call(
        first_kernel, gathered(payload), [norm_gain, router_w], weights,
        [shape((tokens, rows), BF16), shape((rows, tokens), BF16),
         shape((rows, width), BF16), shape((2, rows, LANES), F32),
         shape((rows, hidden_units), BF16), shape((rows, hidden_units), BF16)],
        [row_block, d_block],
        3 * dot_flops,
    )
    acts_mid = (theirs.astype(F32) + combined(out, 1)[0]).astype(BF16)

    pieces, acts_start = lax.optimization_barrier((gathered(acts_mid), across(acts_mid, -1)))
    back, active, prob, rg = expert_call(
        middle_kernel, pieces,
        [norm_gain, router_w, place, pick, info, stash_a], weights,
        [shape((rows, hidden_units), BF16), shape((rows, LANES), F32), shape((kept, width), F32)],
        [row_block, row_block, d_block, d_block, lane_block],
        4 * dot_flops,
    )
    grads_mid = input_grad(acts_start, theirs, combined(back, -1)[0], their_gain)

    out, rg = expert_call(
        last_kernel, gathered(grads_mid),
        [router_w, place, pick, info, hidden, prob, rg, stash_a, stash_b, active], weights,
        [shape((kept, width), F32)],
        [row_block, d_block, d_block, lane_block],
        3 * dot_flops, by_rows=True,
    )
    grads_end = across(grads_mid, 1)
    total, rg = combined(out, late=rg)
    router_total = summed(rg)[:experts].T
    grads_start = input_grad(mine, grads_mid, total, gain_row)
    acts_end = (acts_mid.astype(F32) + total).astype(BF16)
    acts = jnp.where(at_start, acts_start, acts_end).reshape(1, micro, toks, width)
    grads = jnp.where(at_start, grads_start, grads_end).reshape(1, micro, toks, width)
    return acts, grads, router_total[None]


def solution(mesh):
    placed = (
        P(None, GROUP, None),
        P(None, GROUP, None),
        P("section", None),
        P("section", None, None),
        P("section", "expert", None, "dp"),
        P("section", "expert", None, "dp"),
        P("section", "expert", "dp", None),
        P("section", None, GROUP, None),
    )
    return jax.shard_map(
        per_device,
        mesh=mesh,
        in_specs=placed,
        out_specs=(
            P("section", None, GROUP, None),
            P("section", None, GROUP, None),
            P("section", None, None),
        ),
        check_vma=False,
    )
```

```python
import functools

import jax
import jax.numpy as jnp
from jax import lax
from jax.experimental import pallas as pl
from jax.experimental.pallas import tpu as pltpu
from jax.sharding import PartitionSpec as P

EPSILON = 1e-05
LANES = 128
GROUP = ("expert", "dp")
F32 = jnp.float32
BF16 = jnp.bfloat16


def dot_nn(a, b):
    return jnp.dot(a, b, preferred_element_type=F32)


def dot_nt(a, b):
    return lax.dot_general(a, b, (((1,), (1,)), ((), ())), preferred_element_type=F32)


def lanes_like(rows):
    return lax.broadcasted_iota(jnp.int32, (rows, LANES), 1)


def pick_lane(block, lane):
    return jnp.sum(jnp.where(lanes_like(block.shape[0]) == lane, block, 0.0), axis=1, keepdims=True)


def hi_lo(block):
    high = block.astype(BF16)
    return high, (block - high.astype(F32)).astype(BF16)


def place_rows(tail, me, place_ref, pick_ref):
    tokens, rows = place_ref.shape
    wide = -(-rows // LANES) * LANES
    first, second = pick_lane(tail, 0), pick_lane(tail, 1)
    mine = jnp.broadcast_to(((first == me) | (second == me)).astype(F32), (tokens, wide))
    row = lax.broadcasted_iota(jnp.int32, (tokens, tokens), 0)
    col = lax.broadcasted_iota(jnp.int32, (tokens, tokens), 1)
    earlier = dot_nn((col < row).astype(F32).astype(BF16), mine.astype(BF16))
    slot = lax.broadcasted_iota(jnp.int32, (tokens, wide), 1).astype(F32)
    place = jnp.where((earlier == slot) & (mine > 0.5), 1.0, 0.0)
    place_ref[...] = place[:, :rows].astype(BF16)
    pick_ref[...] = jnp.transpose(place)[:rows].astype(BF16)


def signs_of(tail, me):
    first, second = pick_lane(tail, 0), pick_lane(tail, 1)
    other = first + second - me
    lane = lanes_like(tail.shape[0]).astype(F32)
    both = (lane == me).astype(F32) - (lane == other).astype(F32)
    return jnp.where(first != second, both, 0.0)


def norm_and_gap(rows_ref, gain_ref, router_ref, signs, hidden_ref):
    rows, width = rows_ref.shape

    def square(i, part, total):
        values = rows_ref[:, part].astype(F32)
        return total + jnp.sum(values * values, axis=1, keepdims=True)

    squares = tiles(width, square, jnp.zeros((rows, 1), F32))
    inv_rms = lax.rsqrt(squares / width + EPSILON)

    def scale(i, part, total):
        hidden = (rows_ref[:, part].astype(F32) * inv_rms * gain_ref[:, part].astype(F32)).astype(BF16)
        hidden_ref[:, part] = hidden
        return total + dot_nt(hidden, router_ref[:, part])

    logits = tiles(width, scale, jnp.zeros((rows, LANES), F32))
    return jnp.sum(logits * signs, axis=1, keepdims=True)


def tile_of(total, most=1024):
    return next(c for c in (1024, 512, 256, 128) if c <= most and total % c == 0)


def tiles(total, body, carry=0, most=1024):
    step = tile_of(total, most)

    def one(i, carry):
        return body(i, pl.ds(pl.multiple_of(i * step, step), step), carry)

    return lax.fori_loop(0, total // step, one, carry)


class Loads:
    def __init__(self, source, target, sems, axis):
        self.source, self.target, self.sems, self.axis = source, target, sems, axis
        self.count, self.total = sems.shape[0], target.shape[axis]

    def copy(self, i):
        step = self.total // self.count
        part = pl.ds(pl.multiple_of(i * step, step), step)
        spot = (slice(None), part) if self.axis else (part,)
        return pltpu.make_async_copy(self.source.at[spot], self.target.at[spot], self.sems.at[i])

    def wait(self, i):
        self.copy(i).wait()


def start_all(*loads):
    def one(i, carry):
        for load in loads:
            load.copy(i).start()
        return carry

    lax.fori_loop(0, loads[0].count, one, 0)


def select(pick_ref, x_ref, rows_ref):
    def body(i, part, carry):
        rows_ref[:, part] = dot_nn(pick_ref[...], x_ref[:, part]).astype(BF16)
        return carry

    tiles(rows_ref.shape[1], body)


def piece_copies(x_refs, x_ref, sems):
    start, copies = 0, []
    for i, ref in enumerate(x_refs):
        copies.append(pltpu.make_async_copy(ref, x_ref.at[pl.ds(start, ref.shape[0])], sems.at[i]))
        start += ref.shape[0]
    return copies


def fetch(x_refs, x_ref, sems):
    copies = piece_copies(x_refs, x_ref, sems)
    for copy in copies:
        copy.start()
    for copy in copies:
        copy.wait()


def spread(place_ref, rows, out_refs, part):
    piece = out_refs[0].shape[0]
    block = dot_nn(place_ref[...], rows).astype(BF16)
    for i, out_ref in enumerate(out_refs):
        out_ref[:, part] = block[i * piece:(i + 1) * piece]


def send_down(active_ref, down_ref, down_loads, prob, place_ref, out_refs):
    def body(i, part, carry):
        down_loads.wait(i)
        rows = dot_nn(active_ref[...], down_ref[:, part]) * prob
        spread(place_ref, rows.astype(BF16), out_refs, part)
        return carry

    tiles(down_ref.shape[1], body)


def grads_of(gate_pre, up_pre, d_raw, prob, part, dprob_ref, active_ref, d_gate_ref, d_up_ref):
    gate_sig = jax.nn.sigmoid(gate_pre)
    act = gate_pre * gate_sig
    active = (act * up_pre).astype(BF16)
    if active_ref is not None:
        active_ref[:, part] = active
    gain = jnp.sum(active.astype(F32) * d_raw, axis=1, keepdims=True)
    dprob_ref[...] += jnp.broadcast_to(gain, dprob_ref.shape)
    d_active = d_raw * prob
    d_gate = d_active * up_pre * gate_sig * (1.0 + gate_pre * (1.0 - gate_sig))
    d_gate_ref[:, part] = d_gate.astype(BF16)
    d_up_ref[:, part] = (d_active * act).astype(BF16)


def send_back(gate_ref, up_ref, gate_loads, up_loads, d_gate_ref, d_up_ref, dprob_ref, gap, signs,
              hidden_ref, router_ref, place_ref, out_refs, rg_ref):
    c = jax.nn.sigmoid(gap) * jax.nn.sigmoid(-gap) * dprob_ref[...] * signs
    c_high, c_low = hi_lo(c)
    t_high, t_low = hi_lo(jnp.transpose(c)[:rg_ref.shape[0]])

    def body(i, part, carry):
        if gate_loads is not None:
            gate_loads.wait(i)
            up_loads.wait(i)
        back = dot_nt(d_gate_ref[...], gate_ref[part, :]) + dot_nt(d_up_ref[...], up_ref[part, :])
        extra = dot_nn(c_high, router_ref[:, part]) + dot_nn(c_low, router_ref[:, part])
        spread(place_ref, (back + extra).astype(BF16), out_refs, part)
        hidden = hidden_ref[:, part]
        rg_ref[:, part] = dot_nn(t_high, hidden) + dot_nn(t_low, hidden)
        return carry

    tiles(gate_ref.shape[0], body)


def first_kernel(x_refs, out_refs, gain_ref, router_ref, gate_in, up_in, down_in,
                 place_ref, pick_ref, hidden_ref, info_ref, a_ref, b_ref,
                 x_ref, x_sems, gate_ref, up_ref, down_ref, gate_sems, up_sems, rows_sems, cols_sems,
                 rows_ref, active_ref):
    section = lax.axis_index("section")
    width = gain_ref.shape[1]
    gate_loads = Loads(gate_in, gate_ref, gate_sems, 1)
    up_loads = Loads(up_in, up_ref, up_sems, 1)
    down_cols = Loads(down_in, down_ref, cols_sems, 1)
    down_rows = Loads(down_in, down_ref, rows_sems, 0)
    fetches = piece_copies(x_refs, x_ref, x_sems)
    for copy in fetches:
        copy.start()

    @pl.when(section == 0)
    def _():
        start_all(gate_loads, up_loads)
        start_all(down_cols)

    @pl.when(section != 0)
    def _():
        start_all(down_rows)

    for copy in fetches:
        copy.wait()
    me = lax.axis_index("expert").astype(F32)
    tail = x_ref[:, width:]
    place_rows(tail.astype(F32), me, place_ref, pick_ref)
    select(pick_ref, x_ref, rows_ref)
    info_ref[0] = signs_of(dot_nn(pick_ref[...], tail), me)

    @pl.when(section == 0)
    def _():
        gap = norm_and_gap(rows_ref, gain_ref, router_ref, info_ref[0], hidden_ref)
        info_ref[1] = jnp.broadcast_to(gap, info_ref.shape[1:])

        def body(i, part, carry):
            gate_loads.wait(i)
            up_loads.wait(i)
            gate_pre = dot_nn(hidden_ref[...], gate_ref[:, part])
            up_pre = dot_nn(hidden_ref[...], up_ref[:, part])
            a_ref[:, part] = gate_pre.astype(BF16)
            b_ref[:, part] = up_pre.astype(BF16)
            active_ref[:, part] = (gate_pre * jax.nn.sigmoid(gate_pre) * up_pre).astype(BF16)
            return carry

        tiles(gate_ref.shape[1], body, most=512)
        send_down(active_ref, down_ref, down_cols, jax.nn.sigmoid(gap), place_ref, out_refs)

    @pl.when(section != 0)
    def _():
        def body(i, part, carry):
            down_rows.wait(i)
            a_ref[:, part] = dot_nt(rows_ref[...], down_ref[part, :]).astype(BF16)
            return carry

        tiles(down_ref.shape[0], body)


def middle_kernel(x_refs, back_refs, gain_ref, router_ref, place_ref, pick_ref, info_ref, raw_ref,
                  gate_in, up_in, down_in,
                  active_ref, prob_ref, rg_ref,
                  x_ref, x_sems, gate_ref, up_ref, down_ref, gate_sems, up_sems, rows_sems, cols_sems,
                  rows_ref, hidden_ref, d_gate_ref, d_up_ref, dprob_ref):
    @pl.when(lax.axis_index("section") == 1)
    def _():
        gate_loads = Loads(gate_in, gate_ref, gate_sems, 1)
        up_loads = Loads(up_in, up_ref, up_sems, 1)
        fetches = piece_copies(x_refs, x_ref, x_sems)
        for copy in fetches:
            copy.start()
        start_all(gate_loads, up_loads)
        for copy in fetches:
            copy.wait()
        select(pick_ref, x_ref, rows_ref)
        signs = info_ref[0]
        gap = norm_and_gap(rows_ref, gain_ref, router_ref, signs, hidden_ref)
        prob = jax.nn.sigmoid(gap)
        prob_ref[...] = jnp.broadcast_to(prob, prob_ref.shape)
        dprob_ref[...] = jnp.zeros_like(dprob_ref)

        def body(i, part, carry):
            gate_loads.wait(i)
            up_loads.wait(i)
            gate_pre = dot_nn(hidden_ref[...], gate_ref[:, part])
            up_pre = dot_nn(hidden_ref[...], up_ref[:, part])
            grads_of(gate_pre, up_pre, raw_ref[:, part].astype(F32), prob, part, dprob_ref,
                     active_ref, d_gate_ref, d_up_ref)
            return carry

        tiles(gate_ref.shape[1], body, most=512)
        send_back(gate_ref, up_ref, None, None, d_gate_ref, d_up_ref, dprob_ref, gap, signs,
                  hidden_ref, router_ref, place_ref, back_refs, rg_ref)


def last_kernel(u_refs, out_refs, router_ref, place_ref, pick_ref, info_ref, hidden_ref, prob_ref,
                rg_in_ref, a_ref, b_ref, active_ref, gate_in, up_in, down_in,
                rg_ref,
                x_ref, x_sems, gate_ref, up_ref, down_ref, gate_sems, up_sems, rows_sems, cols_sems,
                rows_ref, d_gate_ref, d_up_ref, dprob_ref):
    section = lax.axis_index("section")

    @pl.when(section == 0)
    def _():
        down_rows = Loads(down_in, down_ref, rows_sems, 0)
        gate_loads = Loads(gate_in, gate_ref, gate_sems, 0)
        up_loads = Loads(up_in, up_ref, up_sems, 0)
        fetches = piece_copies(u_refs, x_ref, x_sems)
        for copy in fetches:
            copy.start()
        start_all(down_rows)
        start_all(gate_loads, up_loads)
        for copy in fetches:
            copy.wait()
        select(pick_ref, x_ref, rows_ref)
        gap = pick_lane(info_ref[1], 0)
        prob = jax.nn.sigmoid(gap)
        dprob_ref[...] = jnp.zeros_like(dprob_ref)

        def body(i, part, carry):
            down_rows.wait(i)
            d_raw = dot_nt(rows_ref[...], down_ref[part, :])
            grads_of(a_ref[:, part].astype(F32), b_ref[:, part].astype(F32), d_raw, prob, part,
                     dprob_ref, None, d_gate_ref, d_up_ref)
            return carry

        tiles(down_ref.shape[0], body)
        send_back(gate_ref, up_ref, gate_loads, up_loads, d_gate_ref, d_up_ref, dprob_ref, gap,
                  info_ref[0], hidden_ref, router_ref, place_ref, out_refs, rg_ref)

    @pl.when(section != 0)
    def _():
        down_cols = Loads(down_in, down_ref, cols_sems, 1)
        start_all(down_cols)
        send_down(active_ref, down_ref, down_cols, pick_lane(prob_ref[...], 0), place_ref, out_refs)
        rg_ref[...] = rg_in_ref[...]


def with_pieces(body, count, inputs, groups, *refs):
    ins, rest = refs[:inputs], refs[inputs:]
    body(ins[:count], rest[:groups], *ins[count:], *rest[groups:])


def expert_call(body, pieces, small, weights, outs, scratch, flops, by_rows=False):
    width, hidden_units = weights[0].shape
    shape = jax.ShapeDtypeStruct
    groups = lax.axis_size("dp")
    tokens = sum(p.shape[0] for p in pieces)
    outs = [shape((tokens // groups, width), BF16)] * groups + outs
    sems = lambda total, most: pltpu.SemaphoreType.DMA((total // tile_of(total, most),))
    pair = sems(width, 1024) if by_rows else sems(hidden_units, 512)
    scratch = [
        pltpu.VMEM((tokens, pieces[0].shape[1]), BF16), pltpu.SemaphoreType.DMA((len(pieces),)),
        *[pltpu.VMEM(w.shape, BF16) for w in weights],
        pair, pair, sems(hidden_units, 1024), sems(width, 1024),
    ] + scratch
    held = sum(w.size * w.dtype.itemsize for w in weights)
    block, outside = pl.BlockSpec(memory_space=pltpu.VMEM), pl.BlockSpec(memory_space=pl.ANY)
    in_specs = [outside] * len(pieces) + [block] * len(small) + [outside] * len(weights)
    results = pl.pallas_call(
        functools.partial(with_pieces, body, len(pieces), len(in_specs), groups),
        in_specs=in_specs,
        out_specs=[block] * len(outs),
        out_shape=outs,
        scratch_shapes=scratch,
        cost_estimate=pl.CostEstimate(flops=flops, bytes_accessed=held, transcendentals=0),
        compiler_params=pltpu.CompilerParams(
            vmem_limit_bytes=held + 6 * 2**20 + 4 * tokens * width * 2
        ),
    )(*pieces, *small, *weights)
    return results[:groups], *results[groups:]


def moved(block, axes, target):
    sizes = [lax.axis_size(a) for a in axes]
    spots = [()]
    for n in sizes:
        spots = [spot + (i,) for spot in spots for i in range(n)]
    number = {spot: i for i, spot in enumerate(spots)}
    pairs = [(number[spot], number[target(*spot)]) for spot in spots if target(*spot) in number]
    return lax.ppermute(block, axes, pairs)


def flips():
    bits = lax.axis_size("dp").bit_length() - 1
    return [1 << b for b in reversed(range(bits))]


def flipped(block, bit):
    return moved(block, ("dp",), lambda d: (d ^ bit,))


def gathered(block):
    count = lax.axis_size("expert")
    parts = [block] + [
        moved(block, ("expert",), lambda e, k=k: ((e + k) % count,)) for k in range(1, count)
    ]
    groups = [parts]
    for bit in flips():
        ahead = groups
        if bit == flips()[-1] and len(groups) > 1:
            ahead = [lax.optimization_barrier((parts, groups[1][-1]))[0]] + groups[1:]
        groups = groups + [[flipped(part, bit) for part in group] for group in ahead]
    return [part for group in groups for part in group]


def combined(pieces, hop=0, late=None):
    count = lax.axis_size("expert")
    own = pieces[0].shape[0] // count
    add = lambda kept, came: (kept.astype(F32) + came.astype(F32)).astype(BF16)
    cut = lambda group: [group[k * own:(k + 1) * own] for k in range(count)]
    order = list(reversed(flips()))
    half = len(pieces) // 2
    came = [flipped(group, order[0]) for group in pieces[half:]]
    groups = [
        [add(*pair) for pair in zip(cut(kept), cut(got))] for kept, got in zip(pieces[:half], came)
    ]
    for bit in order[1:]:
        groups, late = lax.optimization_barrier((groups, late))
        half = len(groups) // 2
        groups = [
            [add(kept, flipped(sent, bit)) for kept, sent in zip(*pair)]
            for pair in zip(groups[:half], groups[half:])
        ]
    total = 0.0
    for k, part in enumerate(groups[0]):
        if hop:
            part = moved(part, ("section", "expert"), lambda s, e, k=k: (s + hop, (e - k) % count))
        elif k:
            part = moved(part, ("expert",), lambda e, k=k: ((e - k) % count,))
        total = total + part.astype(F32)
    return total, late


def summed(block):
    for bit in reversed(flips()):
        block = block + flipped(block, bit)
    count = lax.axis_size("expert")
    total = block
    for k in range(1, count):
        total = total + moved(block, ("expert",), lambda e, k=k: ((e + k) % count,))
    return total


def across(block, distance):
    return moved(block, ("section",), lambda s: (s + distance,))


def swapped(block):
    return moved(block, ("section",), lambda s: (lax.axis_size("section") - 1 - s,))


def input_grad(layer_in, upstream, d_hidden, gain_row):
    values = layer_in.astype(F32)
    inv_rms = lax.rsqrt(jnp.mean(values * values, axis=-1, keepdims=True) + EPSILON)
    weighted = gain_row * d_hidden
    mean = jnp.mean(values * weighted, axis=-1, keepdims=True)
    cubed = inv_rms * inv_rms * inv_rms
    d_in = upstream.astype(F32) + inv_rms * weighted - values * cubed * mean
    return d_in.astype(BF16)


def per_device(inputs, cotangent, norm_gain, router, w_gate, w_up, w_down, routes):
    section = lax.axis_index("section")
    at_start = section == 0
    micro, toks, width = inputs.shape
    experts, top_k = router.shape[2], routes.shape[3]
    capacity = 3 * top_k * toks // (2 * experts)
    peers = lax.axis_size("expert") * lax.axis_size("dp")
    own = micro * toks
    tokens, rows = peers * own, peers * micro * capacity
    weights = (w_gate[0, 0], w_up[0, 0], w_down[0, 0])
    hidden_units = weights[0].shape[1]
    gain_row = norm_gain[0].astype(F32)
    router_w = jnp.pad(router[0].T, ((0, LANES - experts), (0, 0)))
    kept = -(-experts // 8) * 8
    shape = jax.ShapeDtypeStruct
    dot_flops = 2 * rows * width * hidden_units
    row_block, lane_block = pltpu.VMEM((rows, width), BF16), pltpu.VMEM((rows, LANES), F32)
    d_block = pltpu.VMEM((rows, hidden_units), BF16)

    mine = jnp.where(at_start, inputs, cotangent).reshape(own, width)
    tail = jnp.pad(routes[0].reshape(own, top_k).astype(BF16), ((0, 0), (0, LANES - top_k)))
    payload = jnp.concatenate([mine, tail], axis=1)
    with_gain = jnp.concatenate([mine, jnp.pad(norm_gain, ((0, 7), (0, 0)))], axis=0)
    pieces, swap = lax.optimization_barrier((gathered(payload), swapped(with_gain)))
    theirs, their_gain = swap[:own], swap[own].astype(F32)
    out, place, pick, hidden, info, stash_a, stash_b = expert_call(
        first_kernel, pieces, [norm_gain, router_w], weights,
        [shape((tokens, rows), BF16), shape((rows, tokens), BF16),
         shape((rows, width), BF16), shape((2, rows, LANES), F32),
         shape((rows, hidden_units), BF16), shape((rows, hidden_units), BF16)],
        [row_block, d_block],
        3 * dot_flops,
    )
    acts_mid = (theirs.astype(F32) + combined(out, 1)[0]).astype(BF16)

    pieces, acts_start = lax.optimization_barrier((gathered(acts_mid), across(acts_mid, -1)))
    back, active, prob, rg = expert_call(
        middle_kernel, pieces,
        [norm_gain, router_w, place, pick, info, stash_a], weights,
        [shape((rows, hidden_units), BF16), shape((rows, LANES), F32), shape((kept, width), F32)],
        [row_block, row_block, d_block, d_block, lane_block],
        4 * dot_flops,
    )
    grads_mid = input_grad(acts_start, theirs, combined(back, -1)[0], their_gain)

    out, rg = expert_call(
        last_kernel, gathered(grads_mid),
        [router_w, place, pick, info, hidden, prob, rg, stash_a, stash_b, active], weights,
        [shape((kept, width), F32)],
        [row_block, d_block, d_block, lane_block],
        3 * dot_flops, by_rows=True,
    )
    grads_end = across(grads_mid, 1)
    total, rg = combined(out, late=rg)
    router_total = summed(rg)[:experts].T
    grads_start = input_grad(mine, grads_mid, total, gain_row)
    acts_end = (acts_mid.astype(F32) + total).astype(BF16)
    acts = jnp.where(at_start, acts_start, acts_end).reshape(1, micro, toks, width)
    grads = jnp.where(at_start, grads_start, grads_end).reshape(1, micro, toks, width)
    return acts, grads, router_total[None]


def solution(mesh):
    placed = (
        P(None, GROUP, None),
        P(None, GROUP, None),
        P("section", None),
        P("section", None, None),
        P("section", "expert", None, "dp"),
        P("section", "expert", None, "dp"),
        P("section", "expert", "dp", None),
        P("section", None, GROUP, None),
    )
    return jax.shard_map(
        per_device,
        mesh=mesh,
        in_specs=placed,
        out_specs=(
            P("section", None, GROUP, None),
            P("section", None, GROUP, None),
            P("section", None, None),
        ),
        check_vma=False,
    )
```

```python
import functools

import jax
import jax.numpy as jnp
from jax import lax
from jax.experimental import pallas as pl
from jax.experimental.pallas import tpu as pltpu
from jax.sharding import PartitionSpec as P

EPSILON = 1e-05
LANES = 128
GROUP = ("expert", "dp")
F32 = jnp.float32
BF16 = jnp.bfloat16


def dot_nn(a, b):
    return jnp.dot(a, b, preferred_element_type=F32)


def dot_nt(a, b):
    return lax.dot_general(a, b, (((1,), (1,)), ((), ())), preferred_element_type=F32)


def lanes_like(rows):
    return lax.broadcasted_iota(jnp.int32, (rows, LANES), 1)


def pick_lane(block, lane):
    return jnp.sum(jnp.where(lanes_like(block.shape[0]) == lane, block, 0.0), axis=1, keepdims=True)


def hi_lo(block):
    high = block.astype(BF16)
    return high, (block - high.astype(F32)).astype(BF16)


def place_rows(tail, me, place_ref, pick_ref):
    tokens, rows = place_ref.shape
    wide = -(-rows // LANES) * LANES
    first, second = pick_lane(tail, 0), pick_lane(tail, 1)
    mine = jnp.broadcast_to(((first == me) | (second == me)).astype(F32), (tokens, wide))
    row = lax.broadcasted_iota(jnp.int32, (tokens, tokens), 0)
    col = lax.broadcasted_iota(jnp.int32, (tokens, tokens), 1)
    earlier = dot_nn((col < row).astype(F32).astype(BF16), mine.astype(BF16))
    slot = lax.broadcasted_iota(jnp.int32, (tokens, wide), 1).astype(F32)
    place = jnp.where((earlier == slot) & (mine > 0.5), 1.0, 0.0)
    place_ref[...] = place[:, :rows].astype(BF16)
    pick_ref[...] = jnp.transpose(place)[:rows].astype(BF16)


def signs_of(tail, me):
    first, second = pick_lane(tail, 0), pick_lane(tail, 1)
    other = first + second - me
    lane = lanes_like(tail.shape[0]).astype(F32)
    both = (lane == me).astype(F32) - (lane == other).astype(F32)
    return jnp.where(first != second, both, 0.0)


def norm_and_gap(rows_ref, router_ref, signs, hidden_ref):
    rows, width = rows_ref.shape

    def square(i, part, total):
        values = rows_ref[:, part].astype(F32)
        return total + jnp.sum(values * values, axis=1, keepdims=True)

    squares = tiles(width, square, jnp.zeros((rows, 1), F32))
    inv_rms = lax.rsqrt(squares / width + EPSILON)

    def scale(i, part, total):
        hidden = (rows_ref[:, part].astype(F32) * inv_rms * router_ref[LANES - 1:, part].astype(F32)).astype(BF16)
        hidden_ref[:, part] = hidden
        return total + dot_nt(hidden, router_ref[:, part])

    logits = tiles(width, scale, jnp.zeros((rows, LANES), F32))
    return jnp.sum(logits * signs, axis=1, keepdims=True)


def tile_of(total, most=1024):
    return next(c for c in (1024, 512, 256, 128) if c <= most and total % c == 0)


def tiles(total, body, carry=0, most=1024):
    step = tile_of(total, most)

    def one(i, carry):
        return body(i, pl.ds(pl.multiple_of(i * step, step), step), carry)

    return lax.fori_loop(0, total // step, one, carry)


class Loads:
    def __init__(self, source, target, sems, axis):
        self.source, self.target, self.sems, self.axis = source, target, sems, axis
        self.count, self.total = sems.shape[0], target.shape[axis]

    def copy(self, i):
        step = self.total // self.count
        part = pl.ds(pl.multiple_of(i * step, step), step)
        spot = (slice(None), part) if self.axis else (part,)
        return pltpu.make_async_copy(self.source.at[spot], self.target.at[spot], self.sems.at[i])

    def wait(self, i):
        self.copy(i).wait()


def start_all(*loads):
    def one(i, carry):
        for load in loads:
            load.copy(i).start()
        return carry

    lax.fori_loop(0, loads[0].count, one, 0)


def select(pick_ref, x_ref, rows_ref):
    def body(i, part, carry):
        rows_ref[:, part] = dot_nn(pick_ref[...], x_ref[:, part]).astype(BF16)
        return carry

    tiles(rows_ref.shape[1], body)


def piece_copies(x_refs, x_ref, sems):
    start, copies = 0, []
    for i, ref in enumerate(x_refs):
        copies.append(pltpu.make_async_copy(ref, x_ref.at[pl.ds(start, ref.shape[0])], sems.at[i]))
        start += ref.shape[0]
    return copies


def fetch(x_refs, x_ref, sems):
    copies = piece_copies(x_refs, x_ref, sems)
    for copy in copies:
        copy.start()
    for copy in copies:
        copy.wait()


def spread(place_ref, rows, out_refs, part):
    piece = out_refs[0].shape[0]
    block = dot_nn(place_ref[...], rows).astype(BF16)
    for i, out_ref in enumerate(out_refs):
        out_ref[:, part] = block[i * piece:(i + 1) * piece]


def send_down(active_ref, down_ref, down_loads, prob, place_ref, out_refs):
    def body(i, part, carry):
        down_loads.wait(i)
        rows = dot_nn(active_ref[...], down_ref[:, part]) * prob
        spread(place_ref, rows.astype(BF16), out_refs, part)
        return carry

    tiles(down_ref.shape[1], body)


def grads_of(gate_pre, up_pre, d_raw, prob, part, dprob_ref, active_ref, d_gate_ref, d_up_ref):
    gate_sig = jax.nn.sigmoid(gate_pre)
    act = gate_pre * gate_sig
    active = (act * up_pre).astype(BF16)
    if active_ref is not None:
        active_ref[:, part] = active
    gain = jnp.sum(active.astype(F32) * d_raw, axis=1, keepdims=True)
    dprob_ref[...] += jnp.broadcast_to(gain, dprob_ref.shape)
    d_active = d_raw * prob
    d_gate = d_active * up_pre * gate_sig * (1.0 + gate_pre * (1.0 - gate_sig))
    d_gate_ref[:, part] = d_gate.astype(BF16)
    d_up_ref[:, part] = (d_active * act).astype(BF16)


def turn_around(loads, source, target, stores, earlier):
    width = source.shape[0]
    step = tile_of(width)

    def body(i, part, carry):
        loads.wait(i)
        if earlier is not None:
            earlier.wait(i)
        for start in range(0, width, step):
            cols = pl.ds(start, step)
            target[part, cols] = jnp.transpose(source[cols, part])
        stores.copy(i).start()
        return carry

    tiles(source.shape[1], body, most=512)


def send_back(gate_ref, up_ref, gate_loads, up_loads, d_gate_ref, d_up_ref, dprob_ref, gap, signs,
              hidden_ref, router_ref, place_ref, out_refs, rg_ref):
    c = jax.nn.sigmoid(gap) * jax.nn.sigmoid(-gap) * dprob_ref[...] * signs
    c_high, c_low = hi_lo(c)
    t_high, t_low = hi_lo(jnp.transpose(c)[:rg_ref.shape[0]])

    def body(i, part, carry):
        if gate_loads is not None:
            gate_loads.wait(i)
            up_loads.wait(i)
        if gate_loads is not None:
            back = dot_nn(d_gate_ref[...], gate_ref[:, part]) + dot_nn(d_up_ref[...], up_ref[:, part])
        else:
            back = dot_nt(d_gate_ref[...], gate_ref[part, :]) + dot_nt(d_up_ref[...], up_ref[part, :])
        extra = dot_nn(c_high, router_ref[:, part]) + dot_nn(c_low, router_ref[:, part])
        spread(place_ref, (back + extra).astype(BF16), out_refs, part)
        hidden = hidden_ref[:, part]
        rg_ref[:, part] = dot_nn(t_high, hidden) + dot_nn(t_low, hidden)
        return carry

    tiles(router_ref.shape[1], body)


def first_kernel(x_refs, out_refs, router_ref, gate_in, up_in, down_in,
                 place_ref, pick_ref, hidden_ref, info_ref, a_ref, b_ref,
                 x_ref, x_sems, gate_ref, up_ref, down_ref, gate_sems, up_sems, rows_sems, cols_sems,
                 rows_ref, active_ref):
    section = lax.axis_index("section")
    width = router_ref.shape[1]
    gate_loads = Loads(gate_in, gate_ref, gate_sems, 1)
    up_loads = Loads(up_in, up_ref, up_sems, 1)
    down_cols = Loads(down_in, down_ref, cols_sems, 1)
    down_rows = Loads(down_in, down_ref, rows_sems, 0)
    fetches = piece_copies(x_refs, x_ref, x_sems)
    for copy in fetches:
        copy.start()

    @pl.when(section == 0)
    def _():
        start_all(gate_loads, up_loads)
        start_all(down_cols)

    @pl.when(section != 0)
    def _():
        start_all(down_rows)

    for copy in fetches:
        copy.wait()
    me = lax.axis_index("expert").astype(F32)
    tail = x_ref[:, width:]
    place_rows(tail.astype(F32), me, place_ref, pick_ref)
    select(pick_ref, x_ref, rows_ref)
    info_ref[0] = signs_of(dot_nn(pick_ref[...], tail), me)

    @pl.when(section == 0)
    def _():
        gap = norm_and_gap(rows_ref, router_ref, info_ref[0], hidden_ref)
        info_ref[1] = jnp.broadcast_to(gap, info_ref.shape[1:])

        def body(i, part, carry):
            gate_loads.wait(i)
            up_loads.wait(i)
            gate_pre = dot_nn(hidden_ref[...], gate_ref[:, part])
            up_pre = dot_nn(hidden_ref[...], up_ref[:, part])
            a_ref[:, part] = gate_pre.astype(BF16)
            b_ref[:, part] = up_pre.astype(BF16)
            active_ref[:, part] = (gate_pre * jax.nn.sigmoid(gate_pre) * up_pre).astype(BF16)
            return carry

        tiles(gate_ref.shape[1], body, most=512)
        send_down(active_ref, down_ref, down_cols, jax.nn.sigmoid(gap), place_ref, out_refs)

    @pl.when(section != 0)
    def _():
        def body(i, part, carry):
            down_rows.wait(i)
            a_ref[:, part] = dot_nt(rows_ref[...], down_ref[part, :]).astype(BF16)
            return carry

        tiles(down_ref.shape[0], body)


def middle_kernel(x_refs, back_refs, router_ref, place_ref, pick_ref, info_ref, raw_ref,
                  gate_in, up_in, down_in,
                  active_ref, prob_ref, rg_ref, gate_out, up_out,
                  x_ref, x_sems, gate_ref, up_ref, down_ref, gate_sems, up_sems, rows_sems, cols_sems,
                  rows_ref, hidden_ref, d_gate_ref, d_up_ref, dprob_ref, store_sems):
    section = lax.axis_index("section")

    @pl.when(section == 0)
    def _():
        gate_loads = Loads(gate_in, gate_ref, gate_sems, 1)
        up_loads = Loads(up_in, up_ref, up_sems, 1)
        start_all(gate_loads, up_loads)
        gate_stores = Loads(down_ref, gate_out, store_sems, 0)
        up_stores = Loads(down_ref, up_out, store_sems, 0)
        turn_around(gate_loads, gate_ref, down_ref, gate_stores, None)
        turn_around(up_loads, up_ref, down_ref, up_stores, gate_stores)
        lax.fori_loop(0, up_stores.count, lambda i, carry: (up_stores.wait(i), carry)[1], 0)

    @pl.when(section == 1)
    def _():
        gate_loads = Loads(gate_in, gate_ref, gate_sems, 1)
        up_loads = Loads(up_in, up_ref, up_sems, 1)
        fetches = piece_copies(x_refs, x_ref, x_sems)
        for copy in fetches:
            copy.start()
        start_all(gate_loads, up_loads)
        for copy in fetches:
            copy.wait()
        select(pick_ref, x_ref, rows_ref)
        signs = info_ref[0]
        gap = norm_and_gap(rows_ref, router_ref, signs, hidden_ref)
        prob = jax.nn.sigmoid(gap)
        prob_ref[...] = jnp.broadcast_to(prob, prob_ref.shape)
        dprob_ref[...] = jnp.zeros_like(dprob_ref)

        def body(i, part, carry):
            gate_loads.wait(i)
            up_loads.wait(i)
            gate_pre = dot_nn(hidden_ref[...], gate_ref[:, part])
            up_pre = dot_nn(hidden_ref[...], up_ref[:, part])
            grads_of(gate_pre, up_pre, raw_ref[:, part].astype(F32), prob, part, dprob_ref,
                     active_ref, d_gate_ref, d_up_ref)
            return carry

        tiles(gate_ref.shape[1], body, most=512)
        send_back(gate_ref, up_ref, None, None, d_gate_ref, d_up_ref, dprob_ref, gap, signs,
                  hidden_ref, router_ref, place_ref, back_refs, rg_ref)


def last_kernel(u_refs, out_refs, router_ref, place_ref, pick_ref, info_ref, hidden_ref, prob_ref,
                rg_in_ref, a_ref, b_ref, active_ref, gate_in, up_in, down_in,
                rg_ref,
                x_ref, x_sems, gate_ref, up_ref, down_ref, gate_sems, up_sems, rows_sems, cols_sems,
                rows_ref, d_gate_ref, d_up_ref, dprob_ref):
    section = lax.axis_index("section")

    @pl.when(section == 0)
    def _():
        down_rows = Loads(down_in, down_ref, rows_sems, 0)
        gate_loads = Loads(gate_in, gate_ref, gate_sems, 1)
        up_loads = Loads(up_in, up_ref, up_sems, 1)
        fetches = piece_copies(u_refs, x_ref, x_sems)
        for copy in fetches:
            copy.start()
        start_all(down_rows)
        start_all(gate_loads, up_loads)
        for copy in fetches:
            copy.wait()
        select(pick_ref, x_ref, rows_ref)
        gap = pick_lane(info_ref[1], 0)
        prob = jax.nn.sigmoid(gap)
        dprob_ref[...] = jnp.zeros_like(dprob_ref)

        def body(i, part, carry):
            down_rows.wait(i)
            d_raw = dot_nt(rows_ref[...], down_ref[part, :])
            grads_of(a_ref[:, part].astype(F32), b_ref[:, part].astype(F32), d_raw, prob, part,
                     dprob_ref, None, d_gate_ref, d_up_ref)
            return carry

        tiles(down_ref.shape[0], body)
        send_back(gate_ref, up_ref, gate_loads, up_loads, d_gate_ref, d_up_ref, dprob_ref, gap,
                  info_ref[0], hidden_ref, router_ref, place_ref, out_refs, rg_ref)

    @pl.when(section != 0)
    def _():
        down_cols = Loads(down_in, down_ref, cols_sems, 1)
        start_all(down_cols)
        send_down(active_ref, down_ref, down_cols, pick_lane(prob_ref[...], 0), place_ref, out_refs)
        rg_ref[...] = rg_in_ref[...]


def with_pieces(body, count, inputs, groups, *refs):
    ins, rest = refs[:inputs], refs[inputs:]
    body(ins[:count], rest[:groups], *ins[count:], *rest[groups:])


def expert_call(body, pieces, small, weights, outs, scratch, flops, far=(), by_rows=False):
    hidden_units, width = weights[2].shape
    shape = jax.ShapeDtypeStruct
    groups = lax.axis_size("dp")
    tokens = sum(p.shape[0] for p in pieces)
    outs = [shape((tokens // groups, width), BF16)] * groups + outs
    sems = lambda total, most: pltpu.SemaphoreType.DMA((total // tile_of(total, most),))
    pair = sems(width, 1024) if by_rows else sems(hidden_units, 512)
    scratch = [
        pltpu.VMEM((tokens, pieces[0].shape[1]), BF16), pltpu.SemaphoreType.DMA((len(pieces),)),
        *[pltpu.VMEM(w.shape, BF16) for w in weights],
        pair, pair, sems(hidden_units, 1024), sems(width, 1024),
    ] + scratch
    held = sum(w.size * w.dtype.itemsize for w in weights)
    block, outside = pl.BlockSpec(memory_space=pltpu.VMEM), pl.BlockSpec(memory_space=pl.ANY)
    in_specs = [outside] * len(pieces) + [block] * len(small) + [outside] * len(weights)
    results = pl.pallas_call(
        functools.partial(with_pieces, body, len(pieces), len(in_specs), groups),
        in_specs=in_specs,
        out_specs=[block] * len(outs) + [outside] * len(far),
        out_shape=outs + list(far),
        scratch_shapes=scratch,
        cost_estimate=pl.CostEstimate(flops=flops, bytes_accessed=held, transcendentals=0),
        compiler_params=pltpu.CompilerParams(
            vmem_limit_bytes=held + 6 * 2**20 + 4 * tokens * width * 2
        ),
    )(*pieces, *small, *weights)
    return results[:groups], *results[groups:]


def moved(block, axes, target):
    sizes = [lax.axis_size(a) for a in axes]
    spots = [()]
    for n in sizes:
        spots = [spot + (i,) for spot in spots for i in range(n)]
    number = {spot: i for i, spot in enumerate(spots)}
    pairs = [(number[spot], number[target(*spot)]) for spot in spots if target(*spot) in number]
    return lax.ppermute(block, axes, pairs)


def flips():
    bits = lax.axis_size("dp").bit_length() - 1
    return [1 << b for b in reversed(range(bits))]


def flipped(block, bit):
    return moved(block, ("dp",), lambda d: (d ^ bit,))


def gathered(block):
    count = lax.axis_size("expert")
    parts = [block] + [
        moved(block, ("expert",), lambda e, k=k: ((e + k) % count,)) for k in range(1, count)
    ]
    groups = [parts]
    for bit in flips():
        ahead = groups
        if bit == flips()[-1] and len(groups) > 1:
            ahead = [lax.optimization_barrier((parts, groups[1][-1]))[0]] + groups[1:]
        groups = groups + [[flipped(part, bit) for part in group] for group in ahead]
    return [part for group in groups for part in group]


def combined(pieces, hop=0, late=None):
    count = lax.axis_size("expert")
    own = pieces[0].shape[0] // count
    add = lambda kept, came: (kept.astype(F32) + came.astype(F32)).astype(BF16)
    cut = lambda group: [group[k * own:(k + 1) * own] for k in range(count)]
    order = list(reversed(flips()))
    half = len(pieces) // 2
    came = [flipped(group, order[0]) for group in pieces[half:]]
    groups = [
        [add(*pair) for pair in zip(cut(kept), cut(got))] for kept, got in zip(pieces[:half], came)
    ]
    for bit in order[1:]:
        groups, late = lax.optimization_barrier((groups, late))
        half = len(groups) // 2
        groups = [
            [add(kept, flipped(sent, bit)) for kept, sent in zip(*pair)]
            for pair in zip(groups[:half], groups[half:])
        ]
    total = 0.0
    for k, part in enumerate(groups[0]):
        if hop:
            part = moved(part, ("section", "expert"), lambda s, e, k=k: (s + hop, (e - k) % count))
        elif k:
            part = moved(part, ("expert",), lambda e, k=k: ((e - k) % count,))
        total = total + part.astype(F32)
    return total, late


def summed(block):
    for bit in reversed(flips()):
        block = block + flipped(block, bit)
    count = lax.axis_size("expert")
    total = block
    for k in range(1, count):
        total = total + moved(block, ("expert",), lambda e, k=k: ((e + k) % count,))
    return total


def across(block, distance):
    return moved(block, ("section",), lambda s: (s + distance,))


def swapped(block):
    return moved(block, ("section",), lambda s: (lax.axis_size("section") - 1 - s,))


def input_grad(layer_in, upstream, d_hidden, gain_row):
    values = layer_in.astype(F32)
    inv_rms = lax.rsqrt(jnp.mean(values * values, axis=-1, keepdims=True) + EPSILON)
    weighted = gain_row * d_hidden
    mean = jnp.mean(values * weighted, axis=-1, keepdims=True)
    cubed = inv_rms * inv_rms * inv_rms
    d_in = upstream.astype(F32) + inv_rms * weighted - values * cubed * mean
    return d_in.astype(BF16)


def per_device(inputs, cotangent, norm_gain, router, w_gate, w_up, w_down, routes):
    section = lax.axis_index("section")
    at_start = section == 0
    micro, toks, width = inputs.shape
    experts, top_k = router.shape[2], routes.shape[3]
    capacity = 3 * top_k * toks // (2 * experts)
    peers = lax.axis_size("expert") * lax.axis_size("dp")
    own = micro * toks
    tokens, rows = peers * own, peers * micro * capacity
    weights = (w_gate[0, 0], w_up[0, 0], w_down[0, 0])
    hidden_units = weights[0].shape[1]
    gain_row = norm_gain[0].astype(F32)
    blank = jnp.zeros((LANES - 1 - experts, width), BF16)
    router_w = jnp.concatenate([router[0].T, blank, norm_gain], axis=0)
    kept = -(-experts // 8) * 8
    shape = jax.ShapeDtypeStruct
    dot_flops = 2 * rows * width * hidden_units
    row_block, lane_block = pltpu.VMEM((rows, width), BF16), pltpu.VMEM((rows, LANES), F32)
    d_block = pltpu.VMEM((rows, hidden_units), BF16)

    mine = jnp.where(at_start, inputs, cotangent).reshape(own, width)
    tail = jnp.pad(routes[0].reshape(own, top_k).astype(BF16), ((0, 0), (0, LANES - top_k)))
    payload = jnp.concatenate([mine, tail], axis=1)
    with_gain = jnp.concatenate([mine, jnp.pad(norm_gain, ((0, 7), (0, 0)))], axis=0)
    pieces, swap = lax.optimization_barrier((gathered(payload), swapped(with_gain)))
    theirs, their_gain = swap[:own], swap[own].astype(F32)
    out, place, pick, hidden, info, stash_a, stash_b = expert_call(
        first_kernel, pieces, [router_w], weights,
        [shape((tokens, rows), BF16), shape((rows, tokens), BF16),
         shape((rows, width), BF16), shape((2, rows, LANES), F32),
         shape((rows, hidden_units), BF16), shape((rows, hidden_units), BF16)],
        [row_block, d_block],
        3 * dot_flops,
    )
    acts_mid = (theirs.astype(F32) + combined(out, 1)[0]).astype(BF16)

    pieces, acts_start = lax.optimization_barrier((gathered(acts_mid), across(acts_mid, -1)))
    back, active, prob, rg, gate_t, up_t = expert_call(
        middle_kernel, pieces,
        [router_w, place, pick, info, stash_a], weights,
        [shape((rows, hidden_units), BF16), shape((rows, LANES), F32), shape((kept, width), F32)],
        [row_block, row_block, d_block, d_block, lane_block,
         pltpu.SemaphoreType.DMA((hidden_units // tile_of(hidden_units, 512),))],
        4 * dot_flops, far=[shape((hidden_units, width), BF16)] * 2,
    )
    grads_mid = input_grad(acts_start, theirs, combined(back, -1)[0], their_gain)

    out, rg = expert_call(
        last_kernel, gathered(grads_mid),
        [router_w, place, pick, info, hidden, prob, rg, stash_a, stash_b, active],
        (gate_t, up_t, weights[2]),
        [shape((kept, width), F32)],
        [row_block, d_block, d_block, lane_block],
        3 * dot_flops, by_rows=True,
    )
    grads_end = across(grads_mid, 1)
    total, rg = combined(out, late=rg)
    router_total = summed(rg)[:experts].T
    grads_start = input_grad(mine, grads_mid, total, gain_row)
    acts_end = (acts_mid.astype(F32) + total).astype(BF16)
    acts = jnp.where(at_start, acts_start, acts_end).reshape(1, micro, toks, width)
    grads = jnp.where(at_start, grads_start, grads_end).reshape(1, micro, toks, width)
    return acts, grads, router_total[None]


def solution(mesh):
    placed = (
        P(None, GROUP, None),
        P(None, GROUP, None),
        P("section", None),
        P("section", None, None),
        P("section", "expert", None, "dp"),
        P("section", "expert", None, "dp"),
        P("section", "expert", "dp", None),
        P("section", None, GROUP, None),
    )
    return jax.shard_map(
        per_device,
        mesh=mesh,
        in_specs=placed,
        out_specs=(
            P("section", None, GROUP, None),
            P("section", None, GROUP, None),
            P("section", None, None),
        ),
        check_vma=False,
    )
```

```python
import functools

import jax
import jax.numpy as jnp
from jax import lax
from jax.experimental import pallas as pl
from jax.experimental.pallas import tpu as pltpu
from jax.sharding import PartitionSpec as P

EPSILON = 1e-05
LANES = 128
GROUP = ("expert", "dp")
F32 = jnp.float32
BF16 = jnp.bfloat16


def dot_nn(a, b):
    return jnp.dot(a, b, preferred_element_type=F32)


def dot_nt(a, b):
    return lax.dot_general(a, b, (((1,), (1,)), ((), ())), preferred_element_type=F32)


def lanes_like(rows):
    return lax.broadcasted_iota(jnp.int32, (rows, LANES), 1)


def pick_lane(block, lane):
    return jnp.sum(jnp.where(lanes_like(block.shape[0]) == lane, block, 0.0), axis=1, keepdims=True)


def hi_lo(block):
    high = block.astype(BF16)
    return high, (block - high.astype(F32)).astype(BF16)


def place_rows(tail, me, place_ref, pick_ref):
    tokens, rows = place_ref.shape
    wide = -(-rows // LANES) * LANES
    first, second = pick_lane(tail, 0), pick_lane(tail, 1)
    mine = jnp.broadcast_to(((first == me) | (second == me)).astype(F32), (tokens, wide))
    row = lax.broadcasted_iota(jnp.int32, (tokens, tokens), 0)
    col = lax.broadcasted_iota(jnp.int32, (tokens, tokens), 1)
    earlier = dot_nn((col < row).astype(F32).astype(BF16), mine.astype(BF16))
    slot = lax.broadcasted_iota(jnp.int32, (tokens, wide), 1).astype(F32)
    place = jnp.where((earlier == slot) & (mine > 0.5), 1.0, 0.0)
    place_ref[...] = place[:, :rows].astype(BF16)
    pick_ref[...] = jnp.transpose(place)[:rows].astype(BF16)


def signs_of(tail, me):
    first, second = pick_lane(tail, 0), pick_lane(tail, 1)
    other = first + second - me
    lane = lanes_like(tail.shape[0]).astype(F32)
    both = (lane == me).astype(F32) - (lane == other).astype(F32)
    return jnp.where(first != second, both, 0.0)


def norm_and_gap(rows_ref, squares, router_ref, signs, hidden_ref):
    rows, width = rows_ref.shape

    inv_rms = lax.rsqrt(squares / width + EPSILON)

    def scale(i, part, total):
        hidden = (rows_ref[:, part].astype(F32) * inv_rms * router_ref[LANES - 1:, part].astype(F32)).astype(BF16)
        hidden_ref[:, part] = hidden
        return total + dot_nt(hidden, router_ref[:, part])

    logits = tiles(width, scale, jnp.zeros((rows, LANES), F32))
    return jnp.sum(logits * signs, axis=1, keepdims=True)


def tile_of(total, most=1024):
    return next(c for c in (1024, 512, 256, 128) if c <= most and total % c == 0)


def tiles(total, body, carry=0, most=1024):
    step = tile_of(total, most)

    def one(i, carry):
        return body(i, pl.ds(pl.multiple_of(i * step, step), step), carry)

    return lax.fori_loop(0, total // step, one, carry)


class Loads:
    def __init__(self, source, target, sems, axis):
        self.source, self.target, self.sems, self.axis = source, target, sems, axis
        self.count, self.total = sems.shape[0], target.shape[axis]

    def copy(self, i):
        step = self.total // self.count
        part = pl.ds(pl.multiple_of(i * step, step), step)
        spot = (slice(None), part) if self.axis else (part,)
        return pltpu.make_async_copy(self.source.at[spot], self.target.at[spot], self.sems.at[i])

    def wait(self, i):
        self.copy(i).wait()


def start_all(*loads):
    def one(i, carry):
        for load in loads:
            load.copy(i).start()
        return carry

    lax.fori_loop(0, loads[0].count, one, 0)


def select(pick_ref, x_ref, rows_ref):
    def body(i, part, total):
        rows = dot_nn(pick_ref[...], x_ref[:, part])
        rows_ref[:, part] = rows.astype(BF16)
        return total + jnp.sum(rows * rows, axis=1, keepdims=True)

    return tiles(rows_ref.shape[1], body, jnp.zeros((rows_ref.shape[0], 1), F32))


def piece_copies(x_refs, x_ref, sems):
    start, copies = 0, []
    for i, ref in enumerate(x_refs):
        copies.append(pltpu.make_async_copy(ref, x_ref.at[pl.ds(start, ref.shape[0])], sems.at[i]))
        start += ref.shape[0]
    return copies


def fetch(x_refs, x_ref, sems):
    copies = piece_copies(x_refs, x_ref, sems)
    for copy in copies:
        copy.start()
    for copy in copies:
        copy.wait()


def spread(place_ref, rows, out_refs, part):
    piece = out_refs[0].shape[0]
    block = dot_nn(place_ref[...], rows).astype(BF16)
    for i, out_ref in enumerate(out_refs):
        out_ref[:, part] = block[i * piece:(i + 1) * piece]


def send_down(active_ref, down_ref, down_loads, prob, place_ref, out_refs):
    def body(i, part, carry):
        down_loads.wait(i)
        rows = dot_nn(active_ref[...], down_ref[:, part]) * prob
        spread(place_ref, rows.astype(BF16), out_refs, part)
        return carry

    tiles(down_ref.shape[1], body)


def grads_of(gate_pre, up_pre, d_raw, prob, part, dprob_ref, active_ref, d_gate_ref, d_up_ref):
    gate_sig = jax.nn.sigmoid(gate_pre)
    act = gate_pre * gate_sig
    active = (act * up_pre).astype(BF16)
    if active_ref is not None:
        active_ref[:, part] = active
    gain = jnp.sum(active.astype(F32) * d_raw, axis=1, keepdims=True)
    dprob_ref[...] += jnp.broadcast_to(gain, dprob_ref.shape)
    d_active = d_raw * prob
    d_gate = d_active * up_pre * gate_sig * (1.0 + gate_pre * (1.0 - gate_sig))
    d_gate_ref[:, part] = d_gate.astype(BF16)
    d_up_ref[:, part] = (d_active * act).astype(BF16)


def turn_around(loads, source, target, stores, earlier):
    width = source.shape[0]
    step = tile_of(width)

    def body(i, part, carry):
        loads.wait(i)
        if earlier is not None:
            earlier.wait(i)
        for start in range(0, width, step):
            cols = pl.ds(start, step)
            target[part, cols] = jnp.transpose(source[cols, part])
        stores.copy(i).start()
        return carry

    tiles(source.shape[1], body, most=512)


def send_back(gate_ref, up_ref, gate_loads, up_loads, d_gate_ref, d_up_ref, dprob_ref, gap, signs,
              hidden_ref, router_ref, place_ref, out_refs, rg_ref):
    c = jax.nn.sigmoid(gap) * jax.nn.sigmoid(-gap) * dprob_ref[...] * signs
    c_high, c_low = hi_lo(c)
    t_high, t_low = hi_lo(jnp.transpose(c)[:rg_ref.shape[0]])

    def body(i, part, carry):
        if gate_loads is not None:
            gate_loads.wait(i)
            up_loads.wait(i)
        if gate_loads is not None:
            back = dot_nn(d_gate_ref[...], gate_ref[:, part]) + dot_nn(d_up_ref[...], up_ref[:, part])
        else:
            back = dot_nt(d_gate_ref[...], gate_ref[part, :]) + dot_nt(d_up_ref[...], up_ref[part, :])
        extra = dot_nn(c_high, router_ref[:, part]) + dot_nn(c_low, router_ref[:, part])
        spread(place_ref, (back + extra).astype(BF16), out_refs, part)
        hidden = hidden_ref[:, part]
        rg_ref[:, part] = dot_nn(t_high, hidden) + dot_nn(t_low, hidden)
        return carry

    tiles(router_ref.shape[1], body)


def first_kernel(x_refs, out_refs, router_ref, gate_in, up_in, down_in,
                 place_ref, pick_ref, hidden_ref, info_ref, a_ref, b_ref,
                 x_ref, x_sems, gate_ref, up_ref, down_ref, gate_sems, up_sems, rows_sems, cols_sems,
                 rows_ref, active_ref):
    section = lax.axis_index("section")
    width = router_ref.shape[1]
    gate_loads = Loads(gate_in, gate_ref, gate_sems, 1)
    up_loads = Loads(up_in, up_ref, up_sems, 1)
    down_cols = Loads(down_in, down_ref, cols_sems, 1)
    down_rows = Loads(down_in, down_ref, rows_sems, 0)
    fetches = piece_copies(x_refs, x_ref, x_sems)
    for copy in fetches:
        copy.start()

    @pl.when(section == 0)
    def _():
        start_all(gate_loads, up_loads)
        start_all(down_cols)

    @pl.when(section != 0)
    def _():
        start_all(down_rows)

    for copy in fetches:
        copy.wait()
    me = lax.axis_index("expert").astype(F32)
    tail = x_ref[:, width:]
    place_rows(tail.astype(F32), me, place_ref, pick_ref)
    squares = select(pick_ref, x_ref, rows_ref)
    info_ref[0] = signs_of(dot_nn(pick_ref[...], tail), me)

    @pl.when(section == 0)
    def _():
        gap = norm_and_gap(rows_ref, squares, router_ref, info_ref[0], hidden_ref)
        info_ref[1] = jnp.broadcast_to(gap, info_ref.shape[1:])

        def body(i, part, carry):
            gate_loads.wait(i)
            up_loads.wait(i)
            gate_pre = dot_nn(hidden_ref[...], gate_ref[:, part])
            up_pre = dot_nn(hidden_ref[...], up_ref[:, part])
            a_ref[:, part] = gate_pre.astype(BF16)
            b_ref[:, part] = up_pre.astype(BF16)
            active_ref[:, part] = (gate_pre * jax.nn.sigmoid(gate_pre) * up_pre).astype(BF16)
            return carry

        tiles(gate_ref.shape[1], body, most=512)
        send_down(active_ref, down_ref, down_cols, jax.nn.sigmoid(gap), place_ref, out_refs)

    @pl.when(section != 0)
    def _():
        def body(i, part, carry):
            down_rows.wait(i)
            a_ref[:, part] = dot_nt(rows_ref[...], down_ref[part, :]).astype(BF16)
            return carry

        tiles(down_ref.shape[0], body)


def middle_kernel(x_refs, back_refs, router_ref, place_ref, pick_ref, info_ref, raw_ref,
                  gate_in, up_in, down_in,
                  active_ref, prob_ref, rg_ref, gate_out, up_out,
                  x_ref, x_sems, gate_ref, up_ref, down_ref, gate_sems, up_sems, rows_sems, cols_sems,
                  rows_ref, hidden_ref, d_gate_ref, d_up_ref, dprob_ref, store_sems):
    section = lax.axis_index("section")

    @pl.when(section == 0)
    def _():
        gate_loads = Loads(gate_in, gate_ref, gate_sems, 1)
        up_loads = Loads(up_in, up_ref, up_sems, 1)
        start_all(gate_loads, up_loads)
        gate_stores = Loads(down_ref, gate_out, store_sems, 0)
        up_stores = Loads(down_ref, up_out, store_sems, 0)
        turn_around(gate_loads, gate_ref, down_ref, gate_stores, None)
        turn_around(up_loads, up_ref, down_ref, up_stores, gate_stores)
        lax.fori_loop(0, up_stores.count, lambda i, carry: (up_stores.wait(i), carry)[1], 0)

    @pl.when(section == 1)
    def _():
        gate_loads = Loads(gate_in, gate_ref, gate_sems, 1)
        up_loads = Loads(up_in, up_ref, up_sems, 1)
        fetches = piece_copies(x_refs, x_ref, x_sems)
        for copy in fetches:
            copy.start()
        start_all(gate_loads, up_loads)
        for copy in fetches:
            copy.wait()
        squares = select(pick_ref, x_ref, rows_ref)
        signs = info_ref[0]
        gap = norm_and_gap(rows_ref, squares, router_ref, signs, hidden_ref)
        prob = jax.nn.sigmoid(gap)
        prob_ref[...] = jnp.broadcast_to(prob, prob_ref.shape)
        dprob_ref[...] = jnp.zeros_like(dprob_ref)

        def body(i, part, carry):
            gate_loads.wait(i)
            up_loads.wait(i)
            gate_pre = dot_nn(hidden_ref[...], gate_ref[:, part])
            up_pre = dot_nn(hidden_ref[...], up_ref[:, part])
            grads_of(gate_pre, up_pre, raw_ref[:, part].astype(F32), prob, part, dprob_ref,
                     active_ref, d_gate_ref, d_up_ref)
            return carry

        tiles(gate_ref.shape[1], body, most=512)
        send_back(gate_ref, up_ref, None, None, d_gate_ref, d_up_ref, dprob_ref, gap, signs,
                  hidden_ref, router_ref, place_ref, back_refs, rg_ref)


def last_kernel(u_refs, out_refs, router_ref, place_ref, pick_ref, info_ref, hidden_ref, prob_ref,
                rg_in_ref, a_ref, b_ref, active_ref, gate_in, up_in, down_in,
                rg_ref,
                x_ref, x_sems, gate_ref, up_ref, down_ref, gate_sems, up_sems, rows_sems, cols_sems,
                rows_ref, d_gate_ref, d_up_ref, dprob_ref):
    section = lax.axis_index("section")

    @pl.when(section == 0)
    def _():
        down_rows = Loads(down_in, down_ref, rows_sems, 0)
        gate_loads = Loads(gate_in, gate_ref, gate_sems, 1)
        up_loads = Loads(up_in, up_ref, up_sems, 1)
        fetches = piece_copies(u_refs, x_ref, x_sems)
        for copy in fetches:
            copy.start()
        start_all(down_rows)
        start_all(gate_loads, up_loads)
        for copy in fetches:
            copy.wait()
        select(pick_ref, x_ref, rows_ref)
        gap = pick_lane(info_ref[1], 0)
        prob = jax.nn.sigmoid(gap)
        dprob_ref[...] = jnp.zeros_like(dprob_ref)

        def body(i, part, carry):
            down_rows.wait(i)
            d_raw = dot_nt(rows_ref[...], down_ref[part, :])
            grads_of(a_ref[:, part].astype(F32), b_ref[:, part].astype(F32), d_raw, prob, part,
                     dprob_ref, None, d_gate_ref, d_up_ref)
            return carry

        tiles(down_ref.shape[0], body)
        send_back(gate_ref, up_ref, gate_loads, up_loads, d_gate_ref, d_up_ref, dprob_ref, gap,
                  info_ref[0], hidden_ref, router_ref, place_ref, out_refs, rg_ref)

    @pl.when(section != 0)
    def _():
        down_cols = Loads(down_in, down_ref, cols_sems, 1)
        start_all(down_cols)
        send_down(active_ref, down_ref, down_cols, pick_lane(prob_ref[...], 0), place_ref, out_refs)
        rg_ref[...] = rg_in_ref[...]


def with_pieces(body, count, inputs, groups, *refs):
    ins, rest = refs[:inputs], refs[inputs:]
    body(ins[:count], rest[:groups], *ins[count:], *rest[groups:])


def expert_call(body, pieces, small, weights, outs, scratch, flops, far=(), by_rows=False):
    hidden_units, width = weights[2].shape
    shape = jax.ShapeDtypeStruct
    groups = lax.axis_size("dp")
    tokens = sum(p.shape[0] for p in pieces)
    outs = [shape((tokens // groups, width), BF16)] * groups + outs
    sems = lambda total, most: pltpu.SemaphoreType.DMA((total // tile_of(total, most),))
    pair = sems(width, 1024) if by_rows else sems(hidden_units, 512)
    scratch = [
        pltpu.VMEM((tokens, pieces[0].shape[1]), BF16), pltpu.SemaphoreType.DMA((len(pieces),)),
        *[pltpu.VMEM(w.shape, BF16) for w in weights],
        pair, pair, sems(hidden_units, 1024), sems(width, 1024),
    ] + scratch
    held = sum(w.size * w.dtype.itemsize for w in weights)
    block, outside = pl.BlockSpec(memory_space=pltpu.VMEM), pl.BlockSpec(memory_space=pl.ANY)
    in_specs = [outside] * len(pieces) + [block] * len(small) + [outside] * len(weights)
    results = pl.pallas_call(
        functools.partial(with_pieces, body, len(pieces), len(in_specs), groups),
        in_specs=in_specs,
        out_specs=[block] * len(outs) + [outside] * len(far),
        out_shape=outs + list(far),
        scratch_shapes=scratch,
        cost_estimate=pl.CostEstimate(flops=flops, bytes_accessed=held, transcendentals=0),
        compiler_params=pltpu.CompilerParams(
            vmem_limit_bytes=held + 6 * 2**20 + 4 * tokens * width * 2
        ),
    )(*pieces, *small, *weights)
    return results[:groups], *results[groups:]


def moved(block, axes, target):
    sizes = [lax.axis_size(a) for a in axes]
    spots = [()]
    for n in sizes:
        spots = [spot + (i,) for spot in spots for i in range(n)]
    number = {spot: i for i, spot in enumerate(spots)}
    pairs = [(number[spot], number[target(*spot)]) for spot in spots if target(*spot) in number]
    return lax.ppermute(block, axes, pairs)


def flips():
    bits = lax.axis_size("dp").bit_length() - 1
    return [1 << b for b in reversed(range(bits))]


def flipped(block, bit):
    return moved(block, ("dp",), lambda d: (d ^ bit,))


def gathered(block):
    count = lax.axis_size("expert")
    parts = [block] + [
        moved(block, ("expert",), lambda e, k=k: ((e + k) % count,)) for k in range(1, count)
    ]
    groups = [parts]
    for bit in flips():
        ahead = groups
        if bit == flips()[-1] and len(groups) > 1:
            ahead = [lax.optimization_barrier((parts, groups[1][-1]))[0]] + groups[1:]
        groups = groups + [[flipped(part, bit) for part in group] for group in ahead]
    return [part for group in groups for part in group]


def combined(pieces, hop=0, late=None):
    count = lax.axis_size("expert")
    own = pieces[0].shape[0] // count
    add = lambda kept, came: (kept.astype(F32) + came.astype(F32)).astype(BF16)
    cut = lambda group: [group[k * own:(k + 1) * own] for k in range(count)]
    order = list(reversed(flips()))
    half = len(pieces) // 2
    came = [flipped(group, order[0]) for group in pieces[half:]]
    groups = [
        [add(*pair) for pair in zip(cut(kept), cut(got))] for kept, got in zip(pieces[:half], came)
    ]
    for bit in order[1:]:
        groups, late = lax.optimization_barrier((groups, late))
        half = len(groups) // 2
        groups = [
            [add(kept, flipped(sent, bit)) for kept, sent in zip(*pair)]
            for pair in zip(groups[:half], groups[half:])
        ]
    if late is not None:
        for bit in flips()[:-1]:
            late = late + flipped(late, bit)
    total = 0.0
    for k, part in enumerate(groups[0]):
        if hop:
            part = moved(part, ("section", "expert"), lambda s, e, k=k: (s + hop, (e - k) % count))
        elif k:
            part = moved(part, ("expert",), lambda e, k=k: ((e - k) % count,))
        if late is not None and k == count - 2:
            late = lax.optimization_barrier((part, late))[1]
        total = total + part.astype(F32)
    return total, late


def summed(block):
    count = lax.axis_size("expert")
    total = block
    for k in range(1, count):
        total = total + moved(block, ("expert",), lambda e, k=k: ((e + k) % count,))
    return total


def across(block, distance):
    return moved(block, ("section",), lambda s: (s + distance,))


def swapped(block):
    return moved(block, ("section",), lambda s: (lax.axis_size("section") - 1 - s,))


def input_grad(layer_in, upstream, d_hidden, gain_row):
    values = layer_in.astype(F32)
    inv_rms = lax.rsqrt(jnp.mean(values * values, axis=-1, keepdims=True) + EPSILON)
    weighted = gain_row * d_hidden
    mean = jnp.mean(values * weighted, axis=-1, keepdims=True)
    cubed = inv_rms * inv_rms * inv_rms
    d_in = upstream.astype(F32) + inv_rms * weighted - values * cubed * mean
    return d_in.astype(BF16)


def per_device(inputs, cotangent, norm_gain, router, w_gate, w_up, w_down, routes):
    section = lax.axis_index("section")
    at_start = section == 0
    micro, toks, width = inputs.shape
    experts, top_k = router.shape[2], routes.shape[3]
    capacity = 3 * top_k * toks // (2 * experts)
    peers = lax.axis_size("expert") * lax.axis_size("dp")
    own = micro * toks
    tokens, rows = peers * own, peers * micro * capacity
    weights = (w_gate[0, 0], w_up[0, 0], w_down[0, 0])
    hidden_units = weights[0].shape[1]
    gain_row = norm_gain[0].astype(F32)
    blank = jnp.zeros((LANES - 1 - experts, width), BF16)
    router_w = jnp.concatenate([router[0].T, blank, norm_gain], axis=0)
    shape = jax.ShapeDtypeStruct
    dot_flops = 2 * rows * width * hidden_units
    row_block, lane_block = pltpu.VMEM((rows, width), BF16), pltpu.VMEM((rows, LANES), F32)
    d_block = pltpu.VMEM((rows, hidden_units), BF16)

    mine = jnp.where(at_start, inputs, cotangent).reshape(own, width)
    tail = jnp.pad(routes[0].reshape(own, top_k).astype(BF16), ((0, 0), (0, LANES - top_k)))
    payload = jnp.concatenate([mine, tail], axis=1)
    with_gain = jnp.concatenate([mine, jnp.pad(norm_gain, ((0, 7), (0, 0)))], axis=0)
    pieces, swap = lax.optimization_barrier((gathered(payload), swapped(with_gain)))
    theirs, their_gain = swap[:own], swap[own].astype(F32)
    out, place, pick, hidden, info, stash_a, stash_b = expert_call(
        first_kernel, pieces, [router_w], weights,
        [shape((tokens, rows), BF16), shape((rows, tokens), BF16),
         shape((rows, width), BF16), shape((2, rows, LANES), F32),
         shape((rows, hidden_units), BF16), shape((rows, hidden_units), BF16)],
        [row_block, d_block],
        3 * dot_flops,
    )
    acts_mid = (theirs.astype(F32) + combined(out, 1)[0]).astype(BF16)

    pieces, acts_start = lax.optimization_barrier((gathered(acts_mid), across(acts_mid, -1)))
    back, active, prob, rg, gate_t, up_t = expert_call(
        middle_kernel, pieces,
        [router_w, place, pick, info, stash_a], weights,
        [shape((rows, hidden_units), BF16), shape((rows, LANES), F32), shape((experts, width), F32)],
        [row_block, row_block, d_block, d_block, lane_block,
         pltpu.SemaphoreType.DMA((hidden_units // tile_of(hidden_units, 512),))],
        4 * dot_flops, far=[shape((hidden_units, width), BF16)] * 2,
    )
    grads_mid = input_grad(acts_start, theirs, combined(back, -1)[0], their_gain)

    out, rg = expert_call(
        last_kernel, gathered(grads_mid),
        [router_w, place, pick, info, hidden, prob, rg, stash_a, stash_b, active],
        (gate_t, up_t, weights[2]),
        [shape((experts, width), F32)],
        [row_block, d_block, d_block, lane_block],
        3 * dot_flops, by_rows=True,
    )
    grads_end = across(grads_mid, 1)
    total, rg = combined(out, late=rg + flipped(rg, flips()[-1]))
    router_total = summed(rg).T
    grads_start = input_grad(mine, grads_mid, total, gain_row)
    acts_end = (acts_mid.astype(F32) + total).astype(BF16)
    acts = jnp.where(at_start, acts_start, acts_end).reshape(1, micro, toks, width)
    grads = jnp.where(at_start, grads_start, grads_end).reshape(1, micro, toks, width)
    return acts, grads, router_total[None]


def solution(mesh):
    placed = (
        P(None, GROUP, None),
        P(None, GROUP, None),
        P("section", None),
        P("section", None, None),
        P("section", "expert", None, "dp"),
        P("section", "expert", None, "dp"),
        P("section", "expert", "dp", None),
        P("section", None, GROUP, None),
    )
    return jax.shard_map(
        per_device,
        mesh=mesh,
        in_specs=placed,
        out_specs=(
            P("section", None, GROUP, None),
            P("section", None, GROUP, None),
            P("section", None, None),
        ),
        check_vma=False,
    )
```

```python
import functools

import jax
import jax.numpy as jnp
from jax import lax
from jax.experimental import pallas as pl
from jax.experimental.pallas import tpu as pltpu
from jax.sharding import PartitionSpec as P

EPSILON = 1e-05
LANES = 128
GROUP = ("expert", "dp")
F32 = jnp.float32
BF16 = jnp.bfloat16


def dot_nn(a, b):
    return jnp.dot(a, b, preferred_element_type=F32)


def dot_nt(a, b):
    return lax.dot_general(a, b, (((1,), (1,)), ((), ())), preferred_element_type=F32)


def lanes_like(rows):
    return lax.broadcasted_iota(jnp.int32, (rows, LANES), 1)


def pick_lane(block, lane):
    return jnp.sum(jnp.where(lanes_like(block.shape[0]) == lane, block, 0.0), axis=1, keepdims=True)


def hi_lo(block):
    high = block.astype(BF16)
    return high, (block - high.astype(F32)).astype(BF16)


def place_rows(tail, me, place_ref, pick_ref):
    tokens, rows = place_ref.shape
    wide = -(-rows // LANES) * LANES
    first, second = pick_lane(tail, 0), pick_lane(tail, 1)
    mine = jnp.broadcast_to(((first == me) | (second == me)).astype(F32), (tokens, wide))
    row = lax.broadcasted_iota(jnp.int32, (tokens, tokens), 0)
    col = lax.broadcasted_iota(jnp.int32, (tokens, tokens), 1)
    earlier = dot_nn((col < row).astype(F32).astype(BF16), mine.astype(BF16))
    slot = lax.broadcasted_iota(jnp.int32, (tokens, wide), 1).astype(F32)
    place = jnp.where((earlier == slot) & (mine > 0.5), 1.0, 0.0)
    place_ref[...] = place[:, :rows].astype(BF16)
    pick_ref[...] = jnp.transpose(place)[:rows].astype(BF16)


def signs_of(tail, me):
    first, second = pick_lane(tail, 0), pick_lane(tail, 1)
    other = first + second - me
    lane = lanes_like(tail.shape[0]).astype(F32)
    both = (lane == me).astype(F32) - (lane == other).astype(F32)
    return jnp.where(first != second, both, 0.0)


def norm_and_gap(rows_ref, squares, router_ref, signs, hidden_ref):
    rows, width = rows_ref.shape

    inv_rms = lax.rsqrt(squares / width + EPSILON)

    def scale(i, part, total):
        hidden = (rows_ref[:, part].astype(F32) * inv_rms * router_ref[LANES - 1:, part].astype(F32)).astype(BF16)
        hidden_ref[:, part] = hidden
        return total + dot_nt(hidden, router_ref[:, part])

    logits = tiles(width, scale, jnp.zeros((rows, LANES), F32))
    return jnp.sum(logits * signs, axis=1, keepdims=True)


def tile_of(total, most=1024):
    return next(c for c in (1024, 512, 256, 128) if c <= most and total % c == 0)


def tiles(total, body, carry=0, most=1024):
    step = tile_of(total, most)

    def one(i, carry):
        return body(i, pl.ds(pl.multiple_of(i * step, step), step), carry)

    return lax.fori_loop(0, total // step, one, carry)


class Loads:
    def __init__(self, source, target, sems, axis):
        self.source, self.target, self.sems, self.axis = source, target, sems, axis
        self.count, self.total = sems.shape[0], target.shape[axis]

    def copy(self, i):
        step = self.total // self.count
        part = pl.ds(pl.multiple_of(i * step, step), step)
        spot = (slice(None), part) if self.axis else (part,)
        return pltpu.make_async_copy(self.source.at[spot], self.target.at[spot], self.sems.at[i])

    def wait(self, i):
        self.copy(i).wait()


def start_all(*loads):
    def one(i, carry):
        for load in loads:
            load.copy(i).start()
        return carry

    lax.fori_loop(0, loads[0].count, one, 0)


def select(pick_ref, x_ref, rows_ref):
    def body(i, part, total):
        rows = dot_nn(pick_ref[...], x_ref[:, part])
        rows_ref[:, part] = rows.astype(BF16)
        return total + jnp.sum(rows * rows, axis=1, keepdims=True)

    return tiles(rows_ref.shape[1], body, jnp.zeros((rows_ref.shape[0], 1), F32))


def piece_copies(x_refs, x_ref, sems):
    start, copies = 0, []
    for i, ref in enumerate(x_refs):
        copies.append(pltpu.make_async_copy(ref, x_ref.at[pl.ds(start, ref.shape[0])], sems.at[i]))
        start += ref.shape[0]
    return copies


def fetch(x_refs, x_ref, sems):
    copies = piece_copies(x_refs, x_ref, sems)
    for copy in copies:
        copy.start()
    for copy in copies:
        copy.wait()


def spread(place_ref, rows, out_refs, part):
    piece = out_refs[0].shape[0]
    block = dot_nn(place_ref[...], rows).astype(BF16)
    for i, out_ref in enumerate(out_refs):
        out_ref[:, part] = block[i * piece:(i + 1) * piece]


def send_down(active_ref, down_ref, down_loads, prob, place_ref, out_refs):
    def body(i, part, carry):
        down_loads.wait(i)
        rows = dot_nn(active_ref[...], down_ref[:, part]) * prob
        spread(place_ref, rows.astype(BF16), out_refs, part)
        return carry

    tiles(down_ref.shape[1], body)


def grads_of(gate_pre, up_pre, d_raw, prob, part, dprob_ref, active_ref, d_gate_ref, d_up_ref):
    gate_sig = jax.nn.sigmoid(gate_pre)
    act = gate_pre * gate_sig
    active = (act * up_pre).astype(BF16)
    if active_ref is not None:
        active_ref[:, part] = active
    gain = jnp.sum(active.astype(F32) * d_raw, axis=1, keepdims=True)
    dprob_ref[...] += jnp.broadcast_to(gain, dprob_ref.shape)
    d_active = d_raw * prob
    d_gate = d_active * up_pre * gate_sig * (1.0 + gate_pre * (1.0 - gate_sig))
    d_gate_ref[:, part] = d_gate.astype(BF16)
    d_up_ref[:, part] = (d_active * act).astype(BF16)


def turn_part(source, target, part):
    width = source.shape[0]
    step = tile_of(width)
    for start in range(0, width, step):
        cols = pl.ds(start, step)
        target[part, cols] = jnp.transpose(source[cols, part])


def turn_around(loads, source, target, stores, earlier):
    def body(i, part, carry):
        loads.wait(i)
        if earlier is not None:
            earlier.wait(i)
        turn_part(source, target, part)
        stores.copy(i).start()
        return carry

    tiles(source.shape[1], body, most=512)


def send_back(gate_ref, up_ref, gate_loads, up_loads, d_gate_ref, d_up_ref, dprob_ref, gap, signs,
              hidden_ref, router_ref, place_ref, out_refs, rg_ref):
    c = jax.nn.sigmoid(gap) * jax.nn.sigmoid(-gap) * dprob_ref[...] * signs
    c_high, c_low = hi_lo(c)
    t_high, t_low = hi_lo(jnp.transpose(c)[:rg_ref.shape[0]])

    def body(i, part, carry):
        if gate_loads is not None:
            gate_loads.wait(i)
            up_loads.wait(i)
        back = dot_nn(d_gate_ref[...], gate_ref[:, part])
        if up_loads is not None:
            back = back + dot_nn(d_up_ref[...], up_ref[:, part])
        else:
            back = back + dot_nt(d_up_ref[...], up_ref[part, :])
        extra = dot_nn(c_high, router_ref[:, part]) + dot_nn(c_low, router_ref[:, part])
        spread(place_ref, (back + extra).astype(BF16), out_refs, part)
        hidden = hidden_ref[:, part]
        rg_ref[:, part] = dot_nn(t_high, hidden) + dot_nn(t_low, hidden)
        return carry

    tiles(router_ref.shape[1], body)


def first_kernel(x_refs, out_refs, router_ref, gate_in, up_in, down_in,
                 place_ref, pick_ref, hidden_ref, info_ref, a_ref, b_ref,
                 x_ref, x_sems, gate_ref, up_ref, down_ref, gate_sems, up_sems, rows_sems, cols_sems,
                 rows_ref, active_ref):
    section = lax.axis_index("section")
    width = router_ref.shape[1]
    gate_loads = Loads(gate_in, gate_ref, gate_sems, 1)
    up_loads = Loads(up_in, up_ref, up_sems, 1)
    down_cols = Loads(down_in, down_ref, cols_sems, 1)
    down_rows = Loads(down_in, down_ref, rows_sems, 0)
    fetches = piece_copies(x_refs, x_ref, x_sems)
    for copy in fetches:
        copy.start()

    @pl.when(section == 0)
    def _():
        start_all(gate_loads, up_loads)
        start_all(down_cols)

    @pl.when(section != 0)
    def _():
        start_all(down_rows)

    for copy in fetches:
        copy.wait()
    me = lax.axis_index("expert").astype(F32)
    tail = x_ref[:, width:]
    place_rows(tail.astype(F32), me, place_ref, pick_ref)
    squares = select(pick_ref, x_ref, rows_ref)
    info_ref[0] = signs_of(dot_nn(pick_ref[...], tail), me)

    @pl.when(section == 0)
    def _():
        gap = norm_and_gap(rows_ref, squares, router_ref, info_ref[0], hidden_ref)
        info_ref[1] = jnp.broadcast_to(gap, info_ref.shape[1:])

        def body(i, part, carry):
            gate_loads.wait(i)
            up_loads.wait(i)
            gate_pre = dot_nn(hidden_ref[...], gate_ref[:, part])
            up_pre = dot_nn(hidden_ref[...], up_ref[:, part])
            a_ref[:, part] = gate_pre.astype(BF16)
            b_ref[:, part] = up_pre.astype(BF16)
            active_ref[:, part] = (gate_pre * jax.nn.sigmoid(gate_pre) * up_pre).astype(BF16)
            return carry

        tiles(gate_ref.shape[1], body, most=512)
        send_down(active_ref, down_ref, down_cols, jax.nn.sigmoid(gap), place_ref, out_refs)

    @pl.when(section != 0)
    def _():
        def body(i, part, carry):
            down_rows.wait(i)
            a_ref[:, part] = dot_nt(rows_ref[...], down_ref[part, :]).astype(BF16)
            return carry

        tiles(down_ref.shape[0], body)


def middle_kernel(x_refs, back_refs, router_ref, place_ref, pick_ref, info_ref, raw_ref,
                  gate_in, up_in, down_in,
                  active_ref, prob_ref, rg_ref, gate_out, up_out,
                  x_ref, x_sems, gate_ref, up_ref, down_ref, gate_sems, up_sems, rows_sems, cols_sems,
                  rows_ref, hidden_ref, d_gate_ref, d_up_ref, dprob_ref, store_sems):
    section = lax.axis_index("section")

    @pl.when(section == 0)
    def _():
        gate_loads = Loads(gate_in, gate_ref, gate_sems, 1)
        up_loads = Loads(up_in, up_ref, up_sems, 1)
        start_all(gate_loads, up_loads)
        gate_stores = Loads(down_ref, gate_out, store_sems, 0)
        up_stores = Loads(down_ref, up_out, store_sems, 0)
        turn_around(gate_loads, gate_ref, down_ref, gate_stores, None)
        turn_around(up_loads, up_ref, down_ref, up_stores, gate_stores)
        lax.fori_loop(0, up_stores.count, lambda i, carry: (up_stores.wait(i), carry)[1], 0)

    @pl.when(section == 1)
    def _():
        gate_loads = Loads(gate_in, gate_ref, gate_sems, 1)
        up_loads = Loads(up_in, up_ref, up_sems, 1)
        fetches = piece_copies(x_refs, x_ref, x_sems)
        for copy in fetches:
            copy.start()
        start_all(gate_loads, up_loads)
        for copy in fetches:
            copy.wait()
        squares = select(pick_ref, x_ref, rows_ref)
        signs = info_ref[0]
        gap = norm_and_gap(rows_ref, squares, router_ref, signs, hidden_ref)
        prob = jax.nn.sigmoid(gap)
        prob_ref[...] = jnp.broadcast_to(prob, prob_ref.shape)
        dprob_ref[...] = jnp.zeros_like(dprob_ref)

        def body(i, part, carry):
            gate_loads.wait(i)
            up_loads.wait(i)
            gate_pre = dot_nn(hidden_ref[...], gate_ref[:, part])
            up_pre = dot_nn(hidden_ref[...], up_ref[:, part])
            grads_of(gate_pre, up_pre, raw_ref[:, part].astype(F32), prob, part, dprob_ref,
                     active_ref, d_gate_ref, d_up_ref)
            turn_part(gate_ref, down_ref, part)
            return carry

        tiles(gate_ref.shape[1], body, most=512)
        send_back(down_ref, up_ref, None, None, d_gate_ref, d_up_ref, dprob_ref, gap, signs,
                  hidden_ref, router_ref, place_ref, back_refs, rg_ref)


def last_kernel(u_refs, out_refs, router_ref, place_ref, pick_ref, info_ref, hidden_ref, prob_ref,
                rg_in_ref, a_ref, b_ref, active_ref, gate_in, up_in, down_in,
                rg_ref,
                x_ref, x_sems, gate_ref, up_ref, down_ref, gate_sems, up_sems, rows_sems, cols_sems,
                rows_ref, d_gate_ref, d_up_ref, dprob_ref):
    section = lax.axis_index("section")

    @pl.when(section == 0)
    def _():
        down_rows = Loads(down_in, down_ref, rows_sems, 0)
        gate_loads = Loads(gate_in, gate_ref, gate_sems, 1)
        up_loads = Loads(up_in, up_ref, up_sems, 1)
        fetches = piece_copies(u_refs, x_ref, x_sems)
        for copy in fetches:
            copy.start()
        start_all(down_rows)
        start_all(gate_loads, up_loads)
        for copy in fetches:
            copy.wait()
        select(pick_ref, x_ref, rows_ref)
        gap = pick_lane(info_ref[1], 0)
        prob = jax.nn.sigmoid(gap)
        dprob_ref[...] = jnp.zeros_like(dprob_ref)

        def body(i, part, carry):
            down_rows.wait(i)
            d_raw = dot_nt(rows_ref[...], down_ref[part, :])
            grads_of(a_ref[:, part].astype(F32), b_ref[:, part].astype(F32), d_raw, prob, part,
                     dprob_ref, None, d_gate_ref, d_up_ref)
            return carry

        tiles(down_ref.shape[0], body)
        send_back(gate_ref, up_ref, gate_loads, up_loads, d_gate_ref, d_up_ref, dprob_ref, gap,
                  info_ref[0], hidden_ref, router_ref, place_ref, out_refs, rg_ref)

    @pl.when(section != 0)
    def _():
        down_cols = Loads(down_in, down_ref, cols_sems, 1)
        start_all(down_cols)
        send_down(active_ref, down_ref, down_cols, pick_lane(prob_ref[...], 0), place_ref, out_refs)
        rg_ref[...] = rg_in_ref[...]


def with_pieces(body, count, inputs, groups, *refs):
    ins, rest = refs[:inputs], refs[inputs:]
    body(ins[:count], rest[:groups], *ins[count:], *rest[groups:])


def expert_call(body, pieces, small, weights, outs, scratch, flops, far=(), by_rows=False):
    hidden_units, width = weights[2].shape
    shape = jax.ShapeDtypeStruct
    groups = lax.axis_size("dp")
    tokens = sum(p.shape[0] for p in pieces)
    outs = [shape((tokens // groups, width), BF16)] * groups + outs
    sems = lambda total, most: pltpu.SemaphoreType.DMA((total // tile_of(total, most),))
    pair = sems(width, 1024) if by_rows else sems(hidden_units, 512)
    scratch = [
        pltpu.VMEM((tokens, pieces[0].shape[1]), BF16), pltpu.SemaphoreType.DMA((len(pieces),)),
        *[pltpu.VMEM(w.shape, BF16) for w in weights],
        pair, pair, sems(hidden_units, 1024), sems(width, 1024),
    ] + scratch
    held = sum(w.size * w.dtype.itemsize for w in weights)
    block, outside = pl.BlockSpec(memory_space=pltpu.VMEM), pl.BlockSpec(memory_space=pl.ANY)
    in_specs = [outside] * len(pieces) + [block] * len(small) + [outside] * len(weights)
    results = pl.pallas_call(
        functools.partial(with_pieces, body, len(pieces), len(in_specs), groups),
        in_specs=in_specs,
        out_specs=[block] * len(outs) + [outside] * len(far),
        out_shape=outs + list(far),
        scratch_shapes=scratch,
        cost_estimate=pl.CostEstimate(flops=flops, bytes_accessed=held, transcendentals=0),
        compiler_params=pltpu.CompilerParams(
            vmem_limit_bytes=held + 6 * 2**20 + 4 * tokens * width * 2
        ),
    )(*pieces, *small, *weights)
    return results[:groups], *results[groups:]


def moved(block, axes, target):
    sizes = [lax.axis_size(a) for a in axes]
    spots = [()]
    for n in sizes:
        spots = [spot + (i,) for spot in spots for i in range(n)]
    number = {spot: i for i, spot in enumerate(spots)}
    pairs = [(number[spot], number[target(*spot)]) for spot in spots if target(*spot) in number]
    return lax.ppermute(block, axes, pairs)


def flips():
    bits = lax.axis_size("dp").bit_length() - 1
    return [1 << b for b in reversed(range(bits))]


def flipped(block, bit):
    return moved(block, ("dp",), lambda d: (d ^ bit,))


def gathered(block):
    count = lax.axis_size("expert")
    parts = [block] + [
        moved(block, ("expert",), lambda e, k=k: ((e + k) % count,)) for k in range(1, count)
    ]
    groups = [parts]
    for bit in flips():
        ahead = groups
        if bit == flips()[-1] and len(groups) > 1:
            ahead = [lax.optimization_barrier((parts, groups[1][-1]))[0]] + groups[1:]
        groups = groups + [[flipped(part, bit) for part in group] for group in ahead]
    return [part for group in groups for part in group]


def combined(pieces, hop=0, late=None):
    count = lax.axis_size("expert")
    own = pieces[0].shape[0] // count
    add = lambda kept, came: (kept.astype(F32) + came.astype(F32)).astype(BF16)
    cut = lambda group: [group[k * own:(k + 1) * own] for k in range(count)]
    order = list(reversed(flips()))
    half = len(pieces) // 2
    came = [flipped(group, order[0]) for group in pieces[half:]]
    groups = [
        [add(*pair) for pair in zip(cut(kept), cut(got))] for kept, got in zip(pieces[:half], came)
    ]
    for bit in order[1:]:
        groups, late = lax.optimization_barrier((groups, late))
        half = len(groups) // 2
        groups = [
            [add(kept, flipped(sent, bit)) for kept, sent in zip(*pair)]
            for pair in zip(groups[:half], groups[half:])
        ]
    if late is not None:
        for bit in flips()[:-1]:
            late = late + flipped(late, bit)
    total = 0.0
    for k, part in enumerate(groups[0]):
        if hop:
            part = moved(part, ("section", "expert"), lambda s, e, k=k: (s + hop, (e - k) % count))
        elif k:
            part = moved(part, ("expert",), lambda e, k=k: ((e - k) % count,))
        if late is not None and k == count - 2:
            late = lax.optimization_barrier((part, late))[1]
        total = total + part.astype(F32)
    return total, late


def summed(block):
    count = lax.axis_size("expert")
    total = block
    for k in range(1, count):
        total = total + moved(block, ("expert",), lambda e, k=k: ((e + k) % count,))
    return total


def across(block, distance):
    return moved(block, ("section",), lambda s: (s + distance,))


def swapped(block):
    return moved(block, ("section",), lambda s: (lax.axis_size("section") - 1 - s,))


def input_grad(layer_in, upstream, d_hidden, gain_row):
    values = layer_in.astype(F32)
    inv_rms = lax.rsqrt(jnp.mean(values * values, axis=-1, keepdims=True) + EPSILON)
    weighted = gain_row * d_hidden
    mean = jnp.mean(values * weighted, axis=-1, keepdims=True)
    cubed = inv_rms * inv_rms * inv_rms
    d_in = upstream.astype(F32) + inv_rms * weighted - values * cubed * mean
    return d_in.astype(BF16)


def per_device(inputs, cotangent, norm_gain, router, w_gate, w_up, w_down, routes):
    section = lax.axis_index("section")
    at_start = section == 0
    micro, toks, width = inputs.shape
    experts, top_k = router.shape[2], routes.shape[3]
    capacity = 3 * top_k * toks // (2 * experts)
    peers = lax.axis_size("expert") * lax.axis_size("dp")
    own = micro * toks
    tokens, rows = peers * own, peers * micro * capacity
    weights = (w_gate[0, 0], w_up[0, 0], w_down[0, 0])
    hidden_units = weights[0].shape[1]
    gain_row = norm_gain[0].astype(F32)
    blank = jnp.zeros((LANES - 1 - experts, width), BF16)
    router_w = jnp.concatenate([router[0].T, blank, norm_gain], axis=0)
    shape = jax.ShapeDtypeStruct
    dot_flops = 2 * rows * width * hidden_units
    row_block, lane_block = pltpu.VMEM((rows, width), BF16), pltpu.VMEM((rows, LANES), F32)
    d_block = pltpu.VMEM((rows, hidden_units), BF16)

    mine = jnp.where(at_start, inputs, cotangent).reshape(own, width)
    tail = jnp.pad(routes[0].reshape(own, top_k).astype(BF16), ((0, 0), (0, LANES - top_k)))
    payload = jnp.concatenate([mine, tail], axis=1)
    with_gain = jnp.concatenate([mine, jnp.pad(norm_gain, ((0, 7), (0, 0)))], axis=0)
    pieces, swap = lax.optimization_barrier((gathered(payload), swapped(with_gain)))
    theirs, their_gain = swap[:own], swap[own].astype(F32)
    out, place, pick, hidden, info, stash_a, stash_b = expert_call(
        first_kernel, pieces, [router_w], weights,
        [shape((tokens, rows), BF16), shape((rows, tokens), BF16),
         shape((rows, width), BF16), shape((2, rows, LANES), F32),
         shape((rows, hidden_units), BF16), shape((rows, hidden_units), BF16)],
        [row_block, d_block],
        3 * dot_flops,
    )
    acts_mid = (theirs.astype(F32) + combined(out, 1)[0]).astype(BF16)

    pieces, acts_start = lax.optimization_barrier((gathered(acts_mid), across(acts_mid, -1)))
    back, active, prob, rg, gate_t, up_t = expert_call(
        middle_kernel, pieces,
        [router_w, place, pick, info, stash_a], weights,
        [shape((rows, hidden_units), BF16), shape((rows, LANES), F32), shape((experts, width), F32)],
        [row_block, row_block, d_block, d_block, lane_block,
         pltpu.SemaphoreType.DMA((hidden_units // tile_of(hidden_units, 512),))],
        4 * dot_flops, far=[shape((hidden_units, width), BF16)] * 2,
    )
    grads_mid = input_grad(acts_start, theirs, combined(back, -1)[0], their_gain)

    out, rg = expert_call(
        last_kernel, gathered(grads_mid),
        [router_w, place, pick, info, hidden, prob, rg, stash_a, stash_b, active],
        (gate_t, up_t, weights[2]),
        [shape((experts, width), F32)],
        [row_block, d_block, d_block, lane_block],
        3 * dot_flops, by_rows=True,
    )
    grads_end = across(grads_mid, 1)
    total, rg = combined(out, late=rg + flipped(rg, flips()[-1]))
    router_total = summed(rg).T
    grads_start = input_grad(mine, grads_mid, total, gain_row)
    acts_end = (acts_mid.astype(F32) + total).astype(BF16)
    acts = jnp.where(at_start, acts_start, acts_end).reshape(1, micro, toks, width)
    grads = jnp.where(at_start, grads_start, grads_end).reshape(1, micro, toks, width)
    return acts, grads, router_total[None]


def solution(mesh):
    placed = (
        P(None, GROUP, None),
        P(None, GROUP, None),
        P("section", None),
        P("section", None, None),
        P("section", "expert", None, "dp"),
        P("section", "expert", None, "dp"),
        P("section", "expert", "dp", None),
        P("section", None, GROUP, None),
    )
    return jax.shard_map(
        per_device,
        mesh=mesh,
        in_specs=placed,
        out_specs=(
            P("section", None, GROUP, None),
            P("section", None, GROUP, None),
            P("section", None, None),
        ),
        check_vma=False,
    )
```

```python
import functools

import jax
import jax.numpy as jnp
from jax import lax
from jax.experimental import pallas as pl
from jax.experimental.pallas import tpu as pltpu
from jax.sharding import PartitionSpec as P

EPSILON = 1e-05
LANES = 128
GROUP = ("expert", "dp")
F32 = jnp.float32
BF16 = jnp.bfloat16


def dot_nn(a, b):
    return jnp.dot(a, b, preferred_element_type=F32)


def dot_nt(a, b):
    return lax.dot_general(a, b, (((1,), (1,)), ((), ())), preferred_element_type=F32)


def lanes_like(rows):
    return lax.broadcasted_iota(jnp.int32, (rows, LANES), 1)


def pick_lane(block, lane):
    return jnp.sum(jnp.where(lanes_like(block.shape[0]) == lane, block, 0.0), axis=1, keepdims=True)


def hi_lo(block):
    high = block.astype(BF16)
    return high, (block - high.astype(F32)).astype(BF16)


def place_rows(tail, me, place_ref, pick_ref):
    tokens, rows = place_ref.shape
    wide = -(-rows // LANES) * LANES
    first, second = pick_lane(tail, 0), pick_lane(tail, 1)
    mine = jnp.broadcast_to(((first == me) | (second == me)).astype(F32), (tokens, wide))
    row = lax.broadcasted_iota(jnp.int32, (tokens, tokens), 0)
    col = lax.broadcasted_iota(jnp.int32, (tokens, tokens), 1)
    earlier = dot_nn((col < row).astype(F32).astype(BF16), mine.astype(BF16))
    slot = lax.broadcasted_iota(jnp.int32, (tokens, wide), 1).astype(F32)
    place = jnp.where((earlier == slot) & (mine > 0.5), 1.0, 0.0)
    place_ref[...] = place[:, :rows].astype(BF16)
    pick_ref[...] = jnp.transpose(place)[:rows].astype(BF16)


def signs_of(tail, me):
    first, second = pick_lane(tail, 0), pick_lane(tail, 1)
    other = first + second - me
    lane = lanes_like(tail.shape[0]).astype(F32)
    both = (lane == me).astype(F32) - (lane == other).astype(F32)
    return jnp.where(first != second, both, 0.0)


def norm_and_gap(rows_ref, squares, router_ref, signs, hidden_ref):
    rows, width = rows_ref.shape
    used = router_ref.shape[0]
    inv_rms = lax.rsqrt(squares / width + EPSILON)

    def scale(i, part, total):
        hidden = (rows_ref[:, part].astype(F32) * inv_rms * router_ref[used - 1:, part].astype(F32)).astype(BF16)
        hidden_ref[:, part] = hidden
        return total + dot_nt(hidden, router_ref[:, part])

    logits = tiles(width, scale, jnp.zeros((rows, used), F32))
    return jnp.sum(logits * signs[:, :used], axis=1, keepdims=True)


def tile_of(total, most=1024):
    return next(c for c in (1024, 512, 256, 128) if c <= most and total % c == 0)


def tiles(total, body, carry=0, most=1024):
    step = tile_of(total, most)

    def one(i, carry):
        return body(i, pl.ds(pl.multiple_of(i * step, step), step), carry)

    return lax.fori_loop(0, total // step, one, carry)


class Loads:
    def __init__(self, source, target, sems, axis):
        self.source, self.target, self.sems, self.axis = source, target, sems, axis
        self.count, self.total = sems.shape[0], target.shape[axis]

    def copy(self, i):
        step = self.total // self.count
        part = pl.ds(pl.multiple_of(i * step, step), step)
        spot = (slice(None), part) if self.axis else (part,)
        return pltpu.make_async_copy(self.source.at[spot], self.target.at[spot], self.sems.at[i])

    def wait(self, i):
        self.copy(i).wait()


def start_all(*loads):
    def one(i, carry):
        for load in loads:
            load.copy(i).start()
        return carry

    lax.fori_loop(0, loads[0].count, one, 0)


def select(pick_ref, x_ref, rows_ref):
    def body(i, part, total):
        rows = dot_nn(pick_ref[...], x_ref[:, part])
        rows_ref[:, part] = rows.astype(BF16)
        return total + jnp.sum(rows * rows, axis=1, keepdims=True)

    return tiles(rows_ref.shape[1], body, jnp.zeros((rows_ref.shape[0], 1), F32))


def piece_copies(x_refs, x_ref, sems):
    start, copies = 0, []
    for i, ref in enumerate(x_refs):
        copies.append(pltpu.make_async_copy(ref, x_ref.at[pl.ds(start, ref.shape[0])], sems.at[i]))
        start += ref.shape[0]
    return copies


def fetch(x_refs, x_ref, sems):
    copies = piece_copies(x_refs, x_ref, sems)
    for copy in copies:
        copy.start()
    for copy in copies:
        copy.wait()


def spread(place_ref, rows, out_refs, part):
    piece = out_refs[0].shape[0]
    block = dot_nn(place_ref[...], rows).astype(BF16)
    for i, out_ref in enumerate(out_refs):
        out_ref[:, part] = block[i * piece:(i + 1) * piece]


def send_down(active_ref, down_ref, down_loads, prob, place_ref, out_refs):
    def body(i, part, carry):
        down_loads.wait(i)
        rows = dot_nn(active_ref[...], down_ref[:, part]) * prob
        spread(place_ref, rows.astype(BF16), out_refs, part)
        return carry

    tiles(down_ref.shape[1], body)


def grads_of(gate_pre, up_pre, d_raw, prob, part, dprob_ref, active_ref, d_gate_ref, d_up_ref):
    gate_sig = jax.nn.sigmoid(gate_pre)
    act = gate_pre * gate_sig
    active = (act * up_pre).astype(BF16)
    if active_ref is not None:
        active_ref[:, part] = active
    gain = jnp.sum(active.astype(F32) * d_raw, axis=1, keepdims=True)
    dprob_ref[...] += jnp.broadcast_to(gain, dprob_ref.shape)
    d_active = d_raw * prob
    d_gate = d_active * up_pre * gate_sig * (1.0 + gate_pre * (1.0 - gate_sig))
    d_gate_ref[:, part] = d_gate.astype(BF16)
    d_up_ref[:, part] = (d_active * act).astype(BF16)


def turn_part(source, target, part):
    width = source.shape[0]
    step = tile_of(width)
    for start in range(0, width, step):
        cols = pl.ds(start, step)
        target[part, cols] = jnp.transpose(source[cols, part])


def turn_around(loads, source, target, stores, earlier):
    def body(i, part, carry):
        loads.wait(i)
        if earlier is not None:
            earlier.wait(i)
        turn_part(source, target, part)
        stores.copy(i).start()
        return carry

    tiles(source.shape[1], body)


def send_back(gate_ref, up_ref, gate_loads, up_loads, d_gate_ref, d_up_ref, dprob_ref, gap, signs,
              hidden_ref, router_ref, place_ref, out_refs, rg_ref):
    c = jax.nn.sigmoid(gap) * jax.nn.sigmoid(-gap) * dprob_ref[...] * signs
    c_high, c_low = hi_lo(c[:, :router_ref.shape[0]])
    t_high, t_low = hi_lo(jnp.transpose(c)[:rg_ref.shape[0]])

    def body(i, part, carry):
        if gate_loads is not None:
            gate_loads.wait(i)
            up_loads.wait(i)
        back = dot_nn(d_gate_ref[...], gate_ref[:, part])
        if up_loads is not None:
            back = back + dot_nn(d_up_ref[...], up_ref[:, part])
        else:
            back = back + dot_nt(d_up_ref[...], up_ref[part, :])
        extra = dot_nn(c_high, router_ref[:, part]) + dot_nn(c_low, router_ref[:, part])
        spread(place_ref, (back + extra).astype(BF16), out_refs, part)
        hidden = hidden_ref[:, part]
        rg_ref[:, part] = dot_nn(t_high, hidden) + dot_nn(t_low, hidden)
        return carry

    tiles(router_ref.shape[1], body)


def first_kernel(x_refs, out_refs, router_ref, gate_in, up_in, down_in,
                 place_ref, pick_ref, hidden_ref, info_ref, a_ref, b_ref,
                 x_ref, x_sems, gate_ref, up_ref, down_ref, gate_sems, up_sems, rows_sems, cols_sems,
                 rows_ref, active_ref):
    section = lax.axis_index("section")
    width = router_ref.shape[1]
    gate_loads = Loads(gate_in, gate_ref, gate_sems, 1)
    up_loads = Loads(up_in, up_ref, up_sems, 1)
    down_cols = Loads(down_in, down_ref, cols_sems, 1)
    down_rows = Loads(down_in, down_ref, rows_sems, 0)
    fetches = piece_copies(x_refs, x_ref, x_sems)
    for copy in fetches:
        copy.start()

    @pl.when(section == 0)
    def _():
        start_all(gate_loads, up_loads)
        start_all(down_cols)

    @pl.when(section != 0)
    def _():
        start_all(down_rows)

    for copy in fetches:
        copy.wait()
    me = lax.axis_index("expert").astype(F32)
    tail = x_ref[:, width:]
    place_rows(tail.astype(F32), me, place_ref, pick_ref)
    squares = select(pick_ref, x_ref, rows_ref)
    info_ref[0] = signs_of(dot_nn(pick_ref[...], tail), me)

    @pl.when(section == 0)
    def _():
        gap = norm_and_gap(rows_ref, squares, router_ref, info_ref[0], hidden_ref)
        info_ref[1] = jnp.broadcast_to(gap, info_ref.shape[1:])

        def body(i, part, carry):
            gate_loads.wait(i)
            up_loads.wait(i)
            gate_pre = dot_nn(hidden_ref[...], gate_ref[:, part])
            up_pre = dot_nn(hidden_ref[...], up_ref[:, part])
            a_ref[:, part] = gate_pre.astype(BF16)
            b_ref[:, part] = up_pre.astype(BF16)
            active_ref[:, part] = (gate_pre * jax.nn.sigmoid(gate_pre) * up_pre).astype(BF16)
            return carry

        tiles(gate_ref.shape[1], body)
        send_down(active_ref, down_ref, down_cols, jax.nn.sigmoid(gap), place_ref, out_refs)

    @pl.when(section != 0)
    def _():
        def body(i, part, carry):
            down_rows.wait(i)
            a_ref[:, part] = dot_nt(rows_ref[...], down_ref[part, :]).astype(BF16)
            return carry

        tiles(down_ref.shape[0], body)


def middle_kernel(x_refs, back_refs, router_ref, place_ref, pick_ref, info_ref, raw_ref,
                  gate_in, up_in, down_in,
                  active_ref, prob_ref, rg_ref, gate_out, up_out,
                  x_ref, x_sems, gate_ref, up_ref, down_ref, gate_sems, up_sems, rows_sems, cols_sems,
                  rows_ref, hidden_ref, d_gate_ref, d_up_ref, dprob_ref, store_sems):
    section = lax.axis_index("section")

    @pl.when(section == 0)
    def _():
        gate_loads = Loads(gate_in, gate_ref, gate_sems, 1)
        up_loads = Loads(up_in, up_ref, up_sems, 1)
        start_all(gate_loads, up_loads)
        gate_stores = Loads(down_ref, gate_out, store_sems, 0)
        up_stores = Loads(down_ref, up_out, store_sems, 0)
        turn_around(gate_loads, gate_ref, down_ref, gate_stores, None)
        turn_around(up_loads, up_ref, down_ref, up_stores, gate_stores)
        lax.fori_loop(0, up_stores.count, lambda i, carry: (up_stores.wait(i), carry)[1], 0)

    @pl.when(section == 1)
    def _():
        gate_loads = Loads(gate_in, gate_ref, gate_sems, 1)
        up_loads = Loads(up_in, up_ref, up_sems, 1)
        fetches = piece_copies(x_refs, x_ref, x_sems)
        for copy in fetches:
            copy.start()
        start_all(gate_loads, up_loads)
        for copy in fetches:
            copy.wait()
        squares = select(pick_ref, x_ref, rows_ref)
        signs = info_ref[0]
        gap = norm_and_gap(rows_ref, squares, router_ref, signs, hidden_ref)
        prob = jax.nn.sigmoid(gap)
        prob_ref[...] = jnp.broadcast_to(prob, prob_ref.shape)
        dprob_ref[...] = jnp.zeros_like(dprob_ref)

        def body(i, part, carry):
            gate_loads.wait(i)
            up_loads.wait(i)
            gate_pre = dot_nn(hidden_ref[...], gate_ref[:, part])
            up_pre = dot_nn(hidden_ref[...], up_ref[:, part])
            grads_of(gate_pre, up_pre, raw_ref[:, part].astype(F32), prob, part, dprob_ref,
                     active_ref, d_gate_ref, d_up_ref)
            turn_part(gate_ref, down_ref, part)
            return carry

        tiles(gate_ref.shape[1], body)
        send_back(down_ref, up_ref, None, None, d_gate_ref, d_up_ref, dprob_ref, gap, signs,
                  hidden_ref, router_ref, place_ref, back_refs, rg_ref)


def last_kernel(u_refs, out_refs, router_ref, place_ref, pick_ref, info_ref, hidden_ref, prob_ref,
                rg_in_ref, a_ref, b_ref, active_ref, gate_in, up_in, down_in,
                rg_ref,
                x_ref, x_sems, gate_ref, up_ref, down_ref, gate_sems, up_sems, rows_sems, cols_sems,
                rows_ref, d_gate_ref, d_up_ref, dprob_ref):
    section = lax.axis_index("section")

    @pl.when(section == 0)
    def _():
        down_rows = Loads(down_in, down_ref, rows_sems, 0)
        gate_loads = Loads(gate_in, gate_ref, gate_sems, 1)
        up_loads = Loads(up_in, up_ref, up_sems, 1)
        fetches = piece_copies(u_refs, x_ref, x_sems)
        for copy in fetches:
            copy.start()
        start_all(down_rows)
        start_all(gate_loads, up_loads)
        for copy in fetches:
            copy.wait()
        select(pick_ref, x_ref, rows_ref)
        gap = pick_lane(info_ref[1], 0)
        prob = jax.nn.sigmoid(gap)
        dprob_ref[...] = jnp.zeros_like(dprob_ref)

        def body(i, part, carry):
            down_rows.wait(i)
            d_raw = dot_nt(rows_ref[...], down_ref[part, :])
            grads_of(a_ref[:, part].astype(F32), b_ref[:, part].astype(F32), d_raw, prob, part,
                     dprob_ref, None, d_gate_ref, d_up_ref)
            return carry

        tiles(down_ref.shape[0], body)
        send_back(gate_ref, up_ref, gate_loads, up_loads, d_gate_ref, d_up_ref, dprob_ref, gap,
                  info_ref[0], hidden_ref, router_ref, place_ref, out_refs, rg_ref)

    @pl.when(section != 0)
    def _():
        down_cols = Loads(down_in, down_ref, cols_sems, 1)
        start_all(down_cols)
        send_down(active_ref, down_ref, down_cols, pick_lane(prob_ref[...], 0), place_ref, out_refs)
        rg_ref[...] = rg_in_ref[...]


def with_pieces(body, count, inputs, groups, *refs):
    ins, rest = refs[:inputs], refs[inputs:]
    body(ins[:count], rest[:groups], *ins[count:], *rest[groups:])


def expert_call(body, pieces, small, weights, outs, scratch, flops, far=(), by_rows=False):
    hidden_units, width = weights[2].shape
    shape = jax.ShapeDtypeStruct
    groups = lax.axis_size("dp")
    tokens = sum(p.shape[0] for p in pieces)
    outs = [shape((tokens // groups, width), BF16)] * groups + outs
    sems = lambda total, most: pltpu.SemaphoreType.DMA((total // tile_of(total, most),))
    pair = sems(width, 1024) if by_rows else sems(hidden_units, 1024)
    scratch = [
        pltpu.VMEM((tokens, pieces[0].shape[1]), BF16), pltpu.SemaphoreType.DMA((len(pieces),)),
        *[pltpu.VMEM(w.shape, BF16) for w in weights],
        pair, pair, sems(hidden_units, 1024), sems(width, 1024),
    ] + scratch
    held = sum(w.size * w.dtype.itemsize for w in weights)
    block, outside = pl.BlockSpec(memory_space=pltpu.VMEM), pl.BlockSpec(memory_space=pl.ANY)
    in_specs = [outside] * len(pieces) + [block] * len(small) + [outside] * len(weights)
    results = pl.pallas_call(
        functools.partial(with_pieces, body, len(pieces), len(in_specs), groups),
        in_specs=in_specs,
        out_specs=[block] * len(outs) + [outside] * len(far),
        out_shape=outs + list(far),
        scratch_shapes=scratch,
        cost_estimate=pl.CostEstimate(flops=flops, bytes_accessed=held, transcendentals=0),
        compiler_params=pltpu.CompilerParams(
            vmem_limit_bytes=held + 6 * 2**20 + 4 * tokens * width * 2
        ),
    )(*pieces, *small, *weights)
    return results[:groups], *results[groups:]


def moved(block, axes, target):
    sizes = [lax.axis_size(a) for a in axes]
    spots = [()]
    for n in sizes:
        spots = [spot + (i,) for spot in spots for i in range(n)]
    number = {spot: i for i, spot in enumerate(spots)}
    pairs = [(number[spot], number[target(*spot)]) for spot in spots if target(*spot) in number]
    return lax.ppermute(block, axes, pairs)


def flips():
    bits = lax.axis_size("dp").bit_length() - 1
    return [1 << b for b in reversed(range(bits))]


def flipped(block, bit):
    return moved(block, ("dp",), lambda d: (d ^ bit,))


def gathered(block):
    count = lax.axis_size("expert")
    parts = [block] + [
        moved(block, ("expert",), lambda e, k=k: ((e + k) % count,)) for k in range(1, count)
    ]
    groups = [parts]
    for bit in flips():
        ahead = groups
        if bit == flips()[-1] and len(groups) > 1:
            ahead = [lax.optimization_barrier((parts, groups[1][-1]))[0]] + groups[1:]
        groups = groups + [[flipped(part, bit) for part in group] for group in ahead]
    return [part for group in groups for part in group]


def combined(pieces, hop=0, late=None):
    count = lax.axis_size("expert")
    own = pieces[0].shape[0] // count
    add = lambda kept, came: (kept.astype(F32) + came.astype(F32)).astype(BF16)
    cut = lambda group: [group[k * own:(k + 1) * own] for k in range(count)]
    order = list(reversed(flips()))
    half = len(pieces) // 2
    came = [flipped(group, order[0]) for group in pieces[half:]]
    groups = [
        [add(*pair) for pair in zip(cut(kept), cut(got))] for kept, got in zip(pieces[:half], came)
    ]
    for bit in order[1:]:
        groups, late = lax.optimization_barrier((groups, late))
        half = len(groups) // 2
        groups = [
            [add(kept, flipped(sent, bit)) for kept, sent in zip(*pair)]
            for pair in zip(groups[:half], groups[half:])
        ]
    if late is not None:
        for bit in flips()[:-1]:
            late = late + flipped(late, bit)
    total = 0.0
    for k, part in enumerate(groups[0]):
        if hop:
            part = moved(part, ("section", "expert"), lambda s, e, k=k: (s + hop, (e - k) % count))
        elif k:
            part = moved(part, ("expert",), lambda e, k=k: ((e - k) % count,))
        if late is not None and k == count - 2:
            late = lax.optimization_barrier((part, late))[1]
        total = total + part.astype(F32)
    return total, late


def summed(block):
    count = lax.axis_size("expert")
    total = block
    for k in range(1, count):
        total = total + moved(block, ("expert",), lambda e, k=k: ((e + k) % count,))
    return total


def across(block, distance):
    return moved(block, ("section",), lambda s: (s + distance,))


def swapped(block):
    return moved(block, ("section",), lambda s: (lax.axis_size("section") - 1 - s,))


def input_grad(layer_in, upstream, d_hidden, gain_row):
    values = layer_in.astype(F32)
    inv_rms = lax.rsqrt(jnp.mean(values * values, axis=-1, keepdims=True) + EPSILON)
    weighted = gain_row * d_hidden
    mean = jnp.mean(values * weighted, axis=-1, keepdims=True)
    cubed = inv_rms * inv_rms * inv_rms
    d_in = upstream.astype(F32) + inv_rms * weighted - values * cubed * mean
    return d_in.astype(BF16)


def per_device(inputs, cotangent, norm_gain, router, w_gate, w_up, w_down, routes):
    section = lax.axis_index("section")
    at_start = section == 0
    micro, toks, width = inputs.shape
    experts, top_k = router.shape[2], routes.shape[3]
    capacity = 3 * top_k * toks // (2 * experts)
    peers = lax.axis_size("expert") * lax.axis_size("dp")
    own = micro * toks
    tokens, rows = peers * own, peers * micro * capacity
    weights = (w_gate[0, 0], w_up[0, 0], w_down[0, 0])
    hidden_units = weights[0].shape[1]
    gain_row = norm_gain[0].astype(F32)
    blank = jnp.zeros((15 - experts % 16, width), BF16)
    router_w = jnp.concatenate([router[0].T, blank, norm_gain], axis=0)
    shape = jax.ShapeDtypeStruct
    dot_flops = 2 * rows * width * hidden_units
    row_block, lane_block = pltpu.VMEM((rows, width), BF16), pltpu.VMEM((rows, LANES), F32)
    d_block = pltpu.VMEM((rows, hidden_units), BF16)

    mine = jnp.where(at_start, inputs, cotangent).reshape(own, width)
    tail = jnp.pad(routes[0].reshape(own, top_k).astype(BF16), ((0, 0), (0, LANES - top_k)))
    payload = jnp.concatenate([mine, tail], axis=1)
    with_gain = jnp.concatenate([mine, jnp.pad(norm_gain, ((0, 7), (0, 0)))], axis=0)
    pieces, swap = lax.optimization_barrier((gathered(payload), swapped(with_gain)))
    theirs, their_gain = swap[:own], swap[own].astype(F32)
    out, place, pick, hidden, info, stash_a, stash_b = expert_call(
        first_kernel, pieces, [router_w], weights,
        [shape((tokens, rows), BF16), shape((rows, tokens), BF16),
         shape((rows, width), BF16), shape((2, rows, LANES), F32),
         shape((rows, hidden_units), BF16), shape((rows, hidden_units), BF16)],
        [row_block, d_block],
        3 * dot_flops,
    )
    acts_mid = (theirs.astype(F32) + combined(out, 1)[0]).astype(BF16)

    pieces, acts_start = lax.optimization_barrier((gathered(acts_mid), across(acts_mid, -1)))
    back, active, prob, rg, gate_t, up_t = expert_call(
        middle_kernel, pieces,
        [router_w, place, pick, info, stash_a], weights,
        [shape((rows, hidden_units), BF16), shape((rows, LANES), F32), shape((experts, width), F32)],
        [row_block, row_block, d_block, d_block, lane_block,
         pltpu.SemaphoreType.DMA((hidden_units // tile_of(hidden_units),))],
        4 * dot_flops, far=[shape((hidden_units, width), BF16)] * 2,
    )
    grads_mid = input_grad(acts_start, theirs, combined(back, -1)[0], their_gain)

    out, rg = expert_call(
        last_kernel, gathered(grads_mid),
        [router_w, place, pick, info, hidden, prob, rg, stash_a, stash_b, active],
        (gate_t, up_t, weights[2]),
        [shape((experts, width), F32)],
        [row_block, d_block, d_block, lane_block],
        3 * dot_flops, by_rows=True,
    )
    grads_end = across(grads_mid, 1)
    total, rg = combined(out, late=rg + flipped(rg, flips()[-1]))
    router_total = summed(rg).T
    grads_start = input_grad(mine, grads_mid, total, gain_row)
    acts_end = (acts_mid.astype(F32) + total).astype(BF16)
    acts = jnp.where(at_start, acts_start, acts_end).reshape(1, micro, toks, width)
    grads = jnp.where(at_start, grads_start, grads_end).reshape(1, micro, toks, width)
    return acts, grads, router_total[None]


def solution(mesh):
    placed = (
        P(None, GROUP, None),
        P(None, GROUP, None),
        P("section", None),
        P("section", None, None),
        P("section", "expert", None, "dp"),
        P("section", "expert", None, "dp"),
        P("section", "expert", "dp", None),
        P("section", None, GROUP, None),
    )
    return jax.shard_map(
        per_device,
        mesh=mesh,
        in_specs=placed,
        out_specs=(
            P("section", None, GROUP, None),
            P("section", None, GROUP, None),
            P("section", None, None),
        ),
        check_vma=False,
    )
```
